32 devices in a mesh: space: 16 (over z, x, core), ch: 2 (over y).
Axes of the slice: x: 2, y: 2, z: 4, core: 2. Of those that a mesh axis runs over, the one named last changes fastest.
Arguments:
- inputs: bfloat16 [256, 1, 128, 128], P('ch', None, 'space'), may hold values from -6 to 6
- w_up: bfloat16 [64, 128, 256], P(None, 'ch'), may hold values from -0.125 to 0.125
- b_up: float32 [128], replicated, may hold values from -4 to 4
- w_conv: bfloat16 [27, 128, 128], replicated, may hold values from -0.109375 to 0.109375
- b_conv: float32 [128], replicated, may hold values from -4 to 4
Outputs:
- result: bfloat16 [128, 2, 256, 256], P(None, None, ('space', 'ch'))
The draws below stay inside these ranges and needn't reach their ends.
All inputs are finite; a program needn't handle non-finite values.
Results may differ from the reference program's by a relative error of at most 0.0036.
Values may be sent and summed in bfloat16 or wider, within the bound.
No kernel may reach another device: no remote copies, remote signals or barrier semaphores. Data moves between devices by JAX's collectives and lax.ppermute only.
A program may use at most 128 MiB of HBM per device.

```python
import jax
import jax.numpy as jnp
import numpy as np

CIN = 256
COUT = 128
DEPTH = 1
COLS = 128
ROWS = 128


def block_scale(own_key, extent, split, least, top_value):
    def one(dim, parts):
        steps = jax.random.uniform(jax.random.fold_in(jax.random.fold_in(own_key, 6), dim), (parts,), jnp.float32, least / len(split), top_value / len(split))
        return jnp.repeat(jnp.exp(steps), extent[dim] // parts).reshape((-1,) + (1,) * (len(extent) - dim - 1))

    factor_of = one(*split[0])
    for cut in split[1:]:
        factor_of = factor_of * one(*cut)
    return factor_of


def scatter_about(rng, dims, spread, reach, shards=(), kind=jnp.bfloat16):
    drawn = jax.random.normal(rng, dims, jnp.float32) * spread
    if len(shards) > 0:
        drawn = block_scale(rng, dims, shards, -0.22, 0.18) * drawn
    return jnp.clip(drawn, min=-reach, max=reach).astype(kind)


def setup_inputs(seed: int = 0) -> dict:
    splits = jax.random.split(jax.random.key(seed), 6)
    inputs = scatter_about(splits[0], (CIN, DEPTH, ROWS, COLS), 1.0, 6.0, ((0, 2), (2, 16)))
    w_up = scatter_about(splits[1], (64, COUT, CIN), (8 * CIN) ** -0.5, 0.125, ((1, 2),))
    b_up = scatter_about(splits[2], (COUT,), 1.0, 4.0, (), jnp.float32)
    w_conv = scatter_about(splits[3], (27, COUT, COUT), (27 * COUT) ** -0.5, 0.109375)
    b_conv = scatter_about(splits[4], (COUT,), 1.0, 4.0, (), jnp.float32)
    return dict(inputs=inputs, w_up=w_up, b_up=b_up, w_conv=w_conv, b_conv=b_conv)


PHASES = (((1, 0), (3, -1)), ((2, 0), (0, 1)))


def upsample(padded, weights, tables):
    chans = padded.shape[0]
    lengths = [padded.shape[1] - 2, padded.shape[2] - 2, padded.shape[3] - 2]
    counts = [len(tables[0]), len(tables[1]), len(tables[2])]
    groups = {}
    for depth_phase, depth_taps in enumerate(tables[0]):
        for depth_tap, depth_shift in depth_taps:
            for row_phase, row_taps in enumerate(tables[1]):
                for row_tap, row_shift in row_taps:
                    for col_phase, col_taps in enumerate(tables[2]):
                        for col_tap, col_shift in col_taps:
                            phase = (depth_phase * counts[1] + row_phase) * counts[2] + col_phase
                            kernel = depth_tap * 16 + row_tap * 4 + col_tap
                            offsets = (depth_shift, row_shift, col_shift)
                            if offsets not in groups:
                                groups[offsets] = []
                            groups[offsets].append((phase, kernel))
    outer = weights.shape[1]
    volume = lengths[0] * lengths[1] * lengths[2]
    totals = [jnp.zeros((outer, volume), jnp.float32) for phase in range(counts[0] * counts[1] * counts[2])]
    for shifts in sorted(groups.keys()):
        members = groups[shifts]
        piece = padded[:, 1 + shifts[0]:1 + shifts[0] + lengths[0], 1 + shifts[1]:1 + shifts[1] + lengths[1], 1 + shifts[2]:1 + shifts[2] + lengths[2]]
        piece = piece.reshape(chans, volume)
        kernels = np.array([member[1] for member in members], dtype=np.int32)
        stacked = weights[kernels].reshape(len(members) * outer, chans)
        product = jnp.dot(stacked, piece, preferred_element_type=jnp.float32).reshape(len(members), outer, volume)
        for place, member in enumerate(members):
            totals[member[0]] = totals[member[0]] + product[place]
    grid = jnp.stack(totals).reshape(counts[0], counts[1], counts[2], outer, lengths[0], lengths[1], lengths[2])
    grid = grid.transpose(3, 4, 0, 5, 1, 6, 2)
    return grid.reshape(outer, lengths[0] * counts[0], lengths[1] * counts[1], lengths[2] * counts[2])


def convolve(padded, weights):
    chans = padded.shape[0]
    lengths = [padded.shape[1] - 2, padded.shape[2] - 2, padded.shape[3] - 2]
    volume = lengths[0] * lengths[1] * lengths[2]
    total = jnp.zeros((weights.shape[1], volume), jnp.float32)
    for depth_shift in (-1, 0, 1):
        for row_shift in (-1, 0, 1):
            for col_shift in (-1, 0, 1):
                kernel = (depth_shift + 1) * 9 + (row_shift + 1) * 3 + (col_shift + 1)
                piece = padded[:, 1 + depth_shift:1 + depth_shift + lengths[0], 1 + row_shift:1 + row_shift + lengths[1], 1 + col_shift:1 + col_shift + lengths[2]]
                total = total + jnp.dot(weights[kernel], piece.reshape(chans, volume), preferred_element_type=jnp.float32)
    return total.reshape(weights.shape[1], lengths[0], lengths[1], lengths[2])


def reference(inputs, w_up, b_up, w_conv, b_conv):
    padded = jnp.pad(inputs, ((0, 0), (1, 1), (1, 1), (1, 1)))
    summed = upsample(padded, w_up, (PHASES, PHASES, PHASES))
    activated = summed + b_up[:, None, None, None]
    upsampled = jnp.where(activated > 0, activated, 0.2 * activated).astype(jnp.bfloat16)
    padded_up = jnp.pad(upsampled, ((0, 0), (1, 1), (1, 1), (1, 1)))
    result = convolve(padded_up, w_conv) + b_conv[:, None, None, None]
    return result.astype(jnp.bfloat16)
```

```python
import jax
import jax.numpy as jnp
from jax import lax
from jax.experimental import pallas as pl
from jax.experimental.pallas import tpu as pltpu
from jax.sharding import PartitionSpec as P

AXES = ("space", "ch")
PHASES = (((1, 0), (3, -1)), ((2, 0), (0, 1)))
COLUMNS = ((3, 0, 1), (0, 1, 2))


def column_of(bias):
    lanes = bias.shape[-1]
    return jnp.transpose(jnp.broadcast_to(bias, (lanes, lanes)))


def shifted(value, step):
    cols = value.shape[1]
    place = lax.broadcasted_iota(jnp.int32, value.shape, 1)
    edge = 0 if step == 1 else cols - 1
    return jnp.where(place == edge, 0.0, pltpu.roll(value, step % cols, 1))


def compute(x_ref, w_ref, b_up_ref, w_conv_ref, b_conv_ref, out_ref, u_ref, total_ref, first, last):
    rows = out_ref.shape[2]
    cout = out_ref.shape[0]
    cols = x_ref.shape[3]
    held = rows + 2
    bias = column_of(b_up_ref[...])
    bias = jnp.concatenate([bias, bias], axis=0)
    for row_phase in (0, 1):
        for col_phase in (0, 1):
            taps = []
            for row_tap, row_shift in PHASES[row_phase]:
                for col_tap, col_shift in PHASES[col_phase]:
                    slot = row_shift + 1 - row_phase
                    taps.append((row_tap * 4 + col_tap, slot, col_shift % 3))
            kernel = jnp.concatenate([w_ref[tap] for tap, _, _ in taps], axis=1)
            for start in range(0, held // 2, 2):
                places = range(start, min(start + 2, held // 2))
                cells = jnp.concatenate(
                    [
                        jnp.concatenate([x_ref[copy, slot + place] for place in places], axis=1)
                        for _, slot, copy in taps
                    ],
                    axis=0,
                )
                summed = jnp.dot(kernel, cells, preferred_element_type=jnp.float32)
                for number, place in enumerate(places):
                    row = 2 * place + 1 - row_phase
                    value = summed[:, number * cols : (number + 1) * cols] + bias
                    value = jnp.where(value > 0, value, 0.2 * value)
                    if row == 0:
                        value = jnp.where(first, 0.0, value)
                    if row == held - 1:
                        value = jnp.where(last, 0.0, value)
                    u_ref[col_phase, row] = value.astype(jnp.bfloat16)
                    moved = shifted(value, -1 if col_phase == 0 else 1)
                    u_ref[2 + col_phase, row] = moved.astype(jnp.bfloat16)

    bias = column_of(b_conv_ref[...])
    bias = jnp.concatenate([bias, bias], axis=0)
    source = lax.broadcasted_iota(jnp.int32, (2 * cols, 2 * cols), 0)
    target = lax.broadcasted_iota(jnp.int32, (2 * cols, 2 * cols), 1)
    wanted = jnp.where(source < cols, 2 * source, 2 * (source - cols) + 1)
    interleave = jnp.where(wanted == target, 1.0, 0.0).astype(jnp.bfloat16)
    kernels = []
    for row_tap in range(3):
        for col_tap in range(3):
            below, here, above = [w_conv_ref[a * 9 + row_tap * 3 + col_tap] for a in range(3)]
            kernels.append(
                jnp.concatenate(
                    [jnp.concatenate([here, above], 1), jnp.concatenate([below, here], 1)], 0
                )
            )
    kernel = jnp.concatenate(kernels, axis=1)
    for start in range(0, rows, 2):
        halves = []
        for col_phase in (0, 1):
            cells = jnp.concatenate(
                [
                    jnp.concatenate([u_ref[copy, start + row_tap], u_ref[copy, start + row_tap + 1]], 1)
                    for row_tap in range(3)
                    for copy in COLUMNS[col_phase]
                ],
                axis=0,
            )
            halves.append(jnp.dot(kernel, cells, preferred_element_type=jnp.float32))
        for number in (0, 1):
            pair = [
                (half[:, number * cols : (number + 1) * cols] + bias).astype(jnp.bfloat16)
                for half in halves
            ]
            pair = jnp.concatenate(pair, axis=1)
            mixed = jnp.dot(pair, interleave, preferred_element_type=jnp.float32)
            for side in (0, 1):
                total_ref[side, pl.ds(start + number, 2 * cout, stride=rows), :] = mixed[
                    :, side * cols : (side + 1) * cols
                ]
    for plane in (0, 1):
        for side in (0, 1):
            block = total_ref[side, pl.ds(plane * cout * rows, cout * rows), :]
            out_ref[:, plane, :, side * cols : (side + 1) * cols] = block.reshape(
                cout, rows, cols
            ).astype(jnp.bfloat16)


def store_row(x_ref, slot, offset, value):
    chans = value.shape[0]
    where = pl.ds(pl.multiple_of(offset, 16), chans)
    wide = value.astype(jnp.float32)
    x_ref[0, slot, where] = value
    x_ref[1, slot, where] = shifted(wide, -1).astype(jnp.bfloat16)
    x_ref[2, slot, where] = shifted(wide, 1).astype(jnp.bfloat16)


def position():
    s, c = lax.axis_index("space"), lax.axis_index("ch")
    return s, c


def paired_kernel(
    own_ref, peer_ref, near_ref, far_ref, w_own_ref, w_peer_ref, w_core_ref,
    b_up_ref, w_conv_ref, b_conv_ref, out_ref, x_ref, w_ref, u_ref, total_ref, sems,
):
    s, c = position()
    core = lax.rem(s, 2)
    part, cout = w_own_ref.shape[1], out_ref.shape[0]

    def rows_of(plane, half):
        return pl.ds(pl.multiple_of(plane * cout + half * part, part), part)

    copies = [
        pltpu.make_async_copy(w_own_ref.at[pl.ds(16, 16)], w_ref.at[:, rows_of(0, c)], sems.at[0]),
        pltpu.make_async_copy(w_own_ref.at[pl.ds(32, 16)], w_ref.at[:, rows_of(1, c)], sems.at[1]),
        pltpu.make_async_copy(w_peer_ref, w_ref.at[:, rows_of(core, 1 - c)], sems.at[2]),
        pltpu.make_async_copy(w_core_ref, w_ref.at[:, rows_of(1 - core, 1 - c)], sems.at[3]),
    ]
    for copy in copies:
        copy.start()
    chans = own_ref.shape[1]
    share = peer_ref.shape[0]
    own, other = c * chans, (1 - c) * chans
    for place in range(share):
        store_row(x_ref, place + 1 - c, own, own_ref[place + c * (own_ref.shape[0] - share)])
        store_row(x_ref, place + 1 - c, other, peer_ref[place])
    store_row(x_ref, c * share, own, near_ref[0])
    store_row(x_ref, c * share, other, far_ref[0])
    for copy in copies:
        copy.wait()
    first = (s == 0) & (c == 0)
    last = (s == lax.axis_size("space") - 1) & (c == 1)
    compute(x_ref, w_ref, b_up_ref, w_conv_ref, b_conv_ref, out_ref, u_ref, total_ref, first, last)


def gathered_kernel(
    rows_ref, w_all_ref, b_up_ref, w_conv_ref, b_conv_ref, out_ref, x_ref, w_ref, u_ref, total_ref, sems
):
    s, c = position()
    cout = out_ref.shape[0]
    copies = [
        pltpu.make_async_copy(
            w_all_ref.at[pl.ds(16 * plane, 16)], w_ref.at[:, pl.ds(plane * cout, cout)], sems.at[plane]
        )
        for plane in (0, 1)
    ]
    for copy in copies:
        copy.start()
    for slot in range(rows_ref.shape[0]):
        store_row(x_ref, slot, 0, rows_ref[slot])
    for copy in copies:
        copy.wait()
    first = (s == 0) & (c == 0)
    last = (s == lax.axis_size("space") - 1) & (c == lax.axis_size("ch") - 1)
    compute(x_ref, w_ref, b_up_ref, w_conv_ref, b_conv_ref, out_ref, u_ref, total_ref, first, last)


def run(kernel, spaces, operands, sizes):
    cin, cout, rows, cols = sizes
    spec = {"vmem": pl.BlockSpec(memory_space=pltpu.VMEM), "any": pl.BlockSpec(memory_space=pl.ANY)}
    return pl.pallas_call(
        kernel,
        out_shape=jax.ShapeDtypeStruct((cout, 2, rows, 2 * cols), jnp.bfloat16),
        in_specs=[spec[space] for space in spaces],
        out_specs=spec["vmem"],
        scratch_shapes=[
            pltpu.VMEM((3, rows // 2 + 2, cin, cols), jnp.bfloat16),
            pltpu.VMEM((16, 2 * cout, cin), jnp.bfloat16),
            pltpu.VMEM((4, rows + 2, 2 * cout, cols), jnp.bfloat16),
            pltpu.VMEM((2, 2 * cout * rows, cols), jnp.float32),
            pltpu.SemaphoreType.DMA((4,)),
        ],
        compiler_params=pltpu.CompilerParams(vmem_limit_bytes=48 * 2**20),
    )(*operands)


def paired(inputs, w_up, b_up, w_conv, b_conv, sizes):
    spaces = lax.axis_size("space")
    s, c = position()
    core = lax.rem(s, 2)
    held = inputs.shape[2]
    share = held // 2 + 1

    def at(space, ch):
        return space * 2 + ch

    across = [(at(i, j), at(i, 1 - j)) for i in range(spaces) for j in (0, 1)]
    cores = [(at(i, j), at(i ^ 1, j)) for i in range(spaces) for j in (0, 1)]
    down = [(at(i - 1, 0), at(i, 0)) for i in range(1, spaces)]
    up = [(at(i + 1, 1), at(i, 1)) for i in range(spaces - 1)]
    down_far = [(at(i - 1, 1), at(i, 0)) for i in range(1, spaces)]
    up_far = [(at(i + 1, 0), at(i, 1)) for i in range(spaces - 1)]

    w_mine = lax.dynamic_slice_in_dim(w_up, 16 + 16 * core, 16, 0)
    w_peer = lax.ppermute(w_mine, AXES, across)
    w_core = lax.ppermute(w_peer, AXES, cores)

    rows = inputs[:, 0].transpose(1, 0, 2)
    wanted = lax.dynamic_slice_in_dim(rows, (1 - c) * (held - share), share, 0)
    peer = lax.ppermute(wanted, AXES, across)
    edge_near = lax.dynamic_slice_in_dim(rows, (1 - c) * (held - 1), 1, 0)
    edge_far = lax.dynamic_slice_in_dim(rows, c * (held - 1), 1, 0)
    near = lax.ppermute(edge_near, AXES, down + up)
    far = lax.ppermute(edge_far, AXES, down_far + up_far)
    operands = (rows, peer, near, far, w_up, w_peer, w_core, b_up[None], w_conv, b_conv[None])
    places = ("vmem",) * 4 + ("any",) * 3 + ("vmem",) * 3
    return run(paired_kernel, places, operands, sizes)


def gathered(inputs, w_up, b_up, w_conv, b_conv, sizes):
    spaces, chs = lax.axis_size("space"), lax.axis_size("ch")
    c = lax.axis_index("ch")
    w_all = lax.all_gather(w_up[16:48], "ch", axis=1, tiled=True)
    rows = lax.all_gather(inputs[:, 0], "ch", axis=0, tiled=True).transpose(1, 0, 2)
    forward = [(i, i + 1) for i in range(spaces - 1)]
    backward = [(j, i) for i, j in forward]
    low = lax.ppermute(rows[-1:], "space", forward)
    high = lax.ppermute(rows[:1], "space", backward)
    rows = jnp.concatenate([low, rows, high], axis=0)
    share = inputs.shape[2] // chs
    rows = lax.dynamic_slice_in_dim(rows, c * share, share + 2, 0)
    operands = (rows, w_all, b_up[None], w_conv, b_conv[None])
    return run(gathered_kernel, ("vmem", "any", "vmem", "vmem", "vmem"), operands, sizes)


def local(inputs, w_up, b_up, w_conv, b_conv):
    chs = lax.axis_size("ch")
    sizes = (w_up.shape[2], w_conv.shape[1], 2 * inputs.shape[2] // chs, inputs.shape[3])
    plan = paired if chs == 2 and lax.axis_size("space") % 2 == 0 else gathered
    return plan(inputs, w_up, b_up, w_conv, b_conv, sizes)


def solution(mesh):
    return jax.shard_map(
        local,
        mesh=mesh,
        in_specs=(P("ch", None, "space", None), P(None, "ch", None), P(), P(), P()),
        out_specs=P(None, None, ("space", "ch"), None),
        check_vma=False,
    )
```

```python
import jax
import jax.numpy as jnp
from jax import lax
from jax.experimental import pallas as pl
from jax.experimental.pallas import tpu as pltpu
from jax.sharding import PartitionSpec as P

AXES = ("space", "ch")
PHASES = (((1, 0), (3, -1)), ((2, 0), (0, 1)))
COLUMNS = ((3, 0, 1), (0, 1, 2))


def column_of(bias):
    lanes = bias.shape[-1]
    return jnp.transpose(jnp.broadcast_to(bias, (lanes, lanes)))


def shifted(value, step):
    cols = value.shape[1]
    place = lax.broadcasted_iota(jnp.int32, value.shape, 1)
    edge = 0 if step == 1 else cols - 1
    return jnp.where(place == edge, 0.0, pltpu.roll(value, step % cols, 1))


def compute(x_ref, w_ref, b_up_ref, w_conv_ref, b_conv_ref, out_ref, u_ref, total_ref, first, last):
    rows = out_ref.shape[2]
    cout = out_ref.shape[0]
    cols = x_ref.shape[3]
    held = rows + 2
    bias = column_of(b_up_ref[...])
    bias = jnp.concatenate([bias, bias], axis=0)
    for row_phase in (0, 1):
        for col_phase in (0, 1):
            taps = []
            for row_tap, row_shift in PHASES[row_phase]:
                for col_tap, col_shift in PHASES[col_phase]:
                    slot = row_shift + 1 - row_phase
                    taps.append((row_tap * 4 + col_tap, slot, col_shift % 3))
            kernel = jnp.concatenate([w_ref[tap] for tap, _, _ in taps], axis=1)
            for start in range(0, held // 2, 2):
                places = range(start, min(start + 2, held // 2))
                cells = jnp.concatenate(
                    [
                        jnp.concatenate([x_ref[copy, slot + place] for place in places], axis=1)
                        for _, slot, copy in taps
                    ],
                    axis=0,
                )
                summed = jnp.dot(kernel, cells, preferred_element_type=jnp.float32)
                for number, place in enumerate(places):
                    row = 2 * place + 1 - row_phase
                    value = summed[:, number * cols : (number + 1) * cols] + bias
                    value = jnp.where(value > 0, value, 0.2 * value)
                    if row == 0:
                        value = jnp.where(first, 0.0, value)
                    if row == held - 1:
                        value = jnp.where(last, 0.0, value)
                    u_ref[col_phase, row] = value.astype(jnp.bfloat16)
                    moved = shifted(value, -1 if col_phase == 0 else 1)
                    u_ref[2 + col_phase, row] = moved.astype(jnp.bfloat16)

    bias = column_of(b_conv_ref[...])
    bias = jnp.concatenate([bias, bias], axis=0)
    source = lax.broadcasted_iota(jnp.int32, (2 * cols, 2 * cols), 0)
    target = lax.broadcasted_iota(jnp.int32, (2 * cols, 2 * cols), 1)
    wanted = jnp.where(source < cols, 2 * source, 2 * (source - cols) + 1)
    interleave = jnp.where(wanted == target, 1.0, 0.0).astype(jnp.bfloat16)
    kernels = []
    for row_tap in range(3):
        for col_tap in range(3):
            below, here, above = [w_conv_ref[a * 9 + row_tap * 3 + col_tap] for a in range(3)]
            kernels.append(
                jnp.concatenate(
                    [jnp.concatenate([here, above], 1), jnp.concatenate([below, here], 1)], 0
                )
            )
    kernel = jnp.concatenate(kernels, axis=1)
    for start in range(0, rows, 2):
        halves = []
        for col_phase in (0, 1):
            cells = jnp.concatenate(
                [
                    jnp.concatenate([u_ref[copy, start + row_tap], u_ref[copy, start + row_tap + 1]], 1)
                    for row_tap in range(3)
                    for copy in COLUMNS[col_phase]
                ],
                axis=0,
            )
            halves.append(jnp.dot(kernel, cells, preferred_element_type=jnp.float32))
        for number in (0, 1):
            pair = [
                (half[:, number * cols : (number + 1) * cols] + bias).astype(jnp.bfloat16)
                for half in halves
            ]
            pair = jnp.concatenate(pair, axis=1)
            mixed = jnp.dot(pair, interleave, preferred_element_type=jnp.float32)
            for side in (0, 1):
                total_ref[side, pl.ds(start + number, 2 * cout, stride=rows), :] = mixed[
                    :, side * cols : (side + 1) * cols
                ]
    for plane in (0, 1):
        for side in (0, 1):
            block = total_ref[side, pl.ds(plane * cout * rows, cout * rows), :]
            out_ref[:, plane, :, side * cols : (side + 1) * cols] = block.reshape(
                cout, rows, cols
            ).astype(jnp.bfloat16)


def store_row(x_ref, slot, offset, value):
    chans = value.shape[0]
    where = pl.ds(pl.multiple_of(offset, 16), chans)
    wide = value.astype(jnp.float32)
    x_ref[0, slot, where] = value
    x_ref[1, slot, where] = shifted(wide, -1).astype(jnp.bfloat16)
    x_ref[2, slot, where] = shifted(wide, 1).astype(jnp.bfloat16)


def position():
    s, c = lax.axis_index("space"), lax.axis_index("ch")
    return s, c


def paired_kernel(
    own_ref, peer_ref, near_ref, far_ref, w_own_ref, w_y_ref, w_y_core_ref, w_x_ref, w_x_core_ref,
    b_up_ref, w_conv_ref, b_conv_ref, out_ref, x_ref, w_ref, u_ref, total_ref, sems,
):
    s, c = position()
    part, cout = w_own_ref.shape[1], out_ref.shape[0]

    def taps_of(plane, half, first, count):
        place = pl.multiple_of(plane * cout + half * part, part)
        return w_ref.at[pl.ds(first, count), pl.ds(place, part)]

    copies = [
        pltpu.make_async_copy(
            w_own_ref.at[pl.ds(16 + 16 * plane, 16)], taps_of(plane, c, 0, 16), sems.at[plane]
        )
        for plane in (0, 1)
    ]
    me = lax.rem(s, 4)
    x, core = me // 2, lax.rem(me, 2)
    parts = ((w_y_ref, x, core), (w_y_core_ref, x, 1 - core), (w_x_ref, 1 - x, core), (w_x_core_ref, 1 - x, 1 - core))
    for number, (part_ref, plane, side) in enumerate(parts):
        copies.append(
            pltpu.make_async_copy(part_ref, taps_of(plane, 1 - c, 8 * side, 8), sems.at[2 + number])
        )
    for copy in copies:
        copy.start()
    chans = own_ref.shape[1]
    share = peer_ref.shape[0]
    own, other = c * chans, (1 - c) * chans
    for place in range(share):
        store_row(x_ref, place + 1 - c, own, own_ref[place + c * (own_ref.shape[0] - share)])
        store_row(x_ref, place + 1 - c, other, peer_ref[place])
    store_row(x_ref, c * share, own, near_ref[0])
    store_row(x_ref, c * share, other, far_ref[0])
    for copy in copies:
        copy.wait()
    first = (s == 0) & (c == 0)
    last = (s == lax.axis_size("space") - 1) & (c == 1)
    compute(x_ref, w_ref, b_up_ref, w_conv_ref, b_conv_ref, out_ref, u_ref, total_ref, first, last)


def gathered_kernel(
    rows_ref, w_all_ref, b_up_ref, w_conv_ref, b_conv_ref, out_ref, x_ref, w_ref, u_ref, total_ref, sems
):
    s, c = position()
    cout = out_ref.shape[0]
    copies = [
        pltpu.make_async_copy(
            w_all_ref.at[pl.ds(16 * plane, 16)], w_ref.at[:, pl.ds(plane * cout, cout)], sems.at[plane]
        )
        for plane in (0, 1)
    ]
    for copy in copies:
        copy.start()
    for slot in range(rows_ref.shape[0]):
        store_row(x_ref, slot, 0, rows_ref[slot])
    for copy in copies:
        copy.wait()
    first = (s == 0) & (c == 0)
    last = (s == lax.axis_size("space") - 1) & (c == lax.axis_size("ch") - 1)
    compute(x_ref, w_ref, b_up_ref, w_conv_ref, b_conv_ref, out_ref, u_ref, total_ref, first, last)


def run(kernel, spaces, operands, sizes):
    cin, cout, rows, cols = sizes
    spec = {"vmem": pl.BlockSpec(memory_space=pltpu.VMEM), "any": pl.BlockSpec(memory_space=pl.ANY)}
    return pl.pallas_call(
        kernel,
        out_shape=jax.ShapeDtypeStruct((cout, 2, rows, 2 * cols), jnp.bfloat16),
        in_specs=[spec[space] for space in spaces],
        out_specs=spec["vmem"],
        scratch_shapes=[
            pltpu.VMEM((3, rows // 2 + 2, cin, cols), jnp.bfloat16),
            pltpu.VMEM((16, 2 * cout, cin), jnp.bfloat16),
            pltpu.VMEM((4, rows + 2, 2 * cout, cols), jnp.bfloat16),
            pltpu.VMEM((2, 2 * cout * rows, cols), jnp.float32),
            pltpu.SemaphoreType.DMA((6,)),
        ],
        compiler_params=pltpu.CompilerParams(vmem_limit_bytes=48 * 2**20),
    )(*operands)


def paired(inputs, w_up, b_up, w_conv, b_conv, sizes):
    spaces = lax.axis_size("space")
    s, c = position()
    held = inputs.shape[2]
    share = held // 2 + 1

    def at(space, ch):
        return space * 2 + ch

    across = [(at(i, j), at(i, 1 - j)) for i in range(spaces) for j in (0, 1)]
    cores = [(at(i, j), at(i ^ 1, j)) for i in range(spaces) for j in (0, 1)]
    pairs = [(at(i, j), at(i ^ 2, j)) for i in range(spaces) for j in (0, 1)]
    down = [(at(i - 1, 0), at(i, 0)) for i in range(1, spaces)]
    up = [(at(i + 1, 1), at(i, 1)) for i in range(spaces - 1)]
    down_far = [(at(i - 1, 1), at(i, 0)) for i in range(1, spaces)]
    up_far = [(at(i + 1, 0), at(i, 1)) for i in range(spaces - 1)]

    quarter = 8 * lax.rem(s, 4)
    w_y = lax.ppermute(lax.dynamic_slice_in_dim(w_up, 16 + quarter, 8, 0), AXES, across)

    rows = inputs[:, 0].transpose(1, 0, 2)
    wanted = lax.dynamic_slice_in_dim(rows, (1 - c) * (held - share), share, 0)
    edge_near = lax.dynamic_slice_in_dim(rows, (1 - c) * (held - 1), 1, 0)
    edge_far = lax.dynamic_slice_in_dim(rows, c * (held - 1), 1, 0)
    w_y, wanted, edge_near, edge_far = lax.optimization_barrier((w_y, wanted, edge_near, edge_far))
    w_x = lax.ppermute(w_y, AXES, pairs)
    peer = lax.ppermute(wanted, AXES, across)
    near = lax.ppermute(edge_near, AXES, down + up)
    far = lax.ppermute(edge_far, AXES, down_far + up_far)
    w_y_core = lax.ppermute(w_y, AXES, cores)
    w_x, w_y_core, peer, near, far = lax.optimization_barrier((w_x, w_y_core, peer, near, far))
    w_x_core = lax.ppermute(w_x, AXES, cores)
    w_parts = (w_y, w_y_core, w_x, w_x_core)
    operands = (rows, peer, near, far, w_up, *w_parts, b_up[None], w_conv, b_conv[None])
    places = ("vmem",) * 4 + ("any",) * 5 + ("vmem",) * 3
    return run(paired_kernel, places, operands, sizes)


def gathered(inputs, w_up, b_up, w_conv, b_conv, sizes):
    spaces, chs = lax.axis_size("space"), lax.axis_size("ch")
    c = lax.axis_index("ch")
    w_all = lax.all_gather(w_up[16:48], "ch", axis=1, tiled=True)
    rows = lax.all_gather(inputs[:, 0], "ch", axis=0, tiled=True).transpose(1, 0, 2)
    forward = [(i, i + 1) for i in range(spaces - 1)]
    backward = [(j, i) for i, j in forward]
    low = lax.ppermute(rows[-1:], "space", forward)
    high = lax.ppermute(rows[:1], "space", backward)
    rows = jnp.concatenate([low, rows, high], axis=0)
    share = inputs.shape[2] // chs
    rows = lax.dynamic_slice_in_dim(rows, c * share, share + 2, 0)
    operands = (rows, w_all, b_up[None], w_conv, b_conv[None])
    return run(gathered_kernel, ("vmem", "any", "vmem", "vmem", "vmem"), operands, sizes)


def local(inputs, w_up, b_up, w_conv, b_conv):
    chs = lax.axis_size("ch")
    sizes = (w_up.shape[2], w_conv.shape[1], 2 * inputs.shape[2] // chs, inputs.shape[3])
    plan = paired if chs == 2 and lax.axis_size("space") % 4 == 0 else gathered
    return plan(inputs, w_up, b_up, w_conv, b_conv, sizes)


def solution(mesh):
    return jax.shard_map(
        local,
        mesh=mesh,
        in_specs=(P("ch", None, "space", None), P(None, "ch", None), P(), P(), P()),
        out_specs=P(None, None, ("space", "ch"), None),
        check_vma=False,
    )
```

```python
import jax
import jax.numpy as jnp
from jax import lax
from jax.experimental import pallas as pl
from jax.experimental.pallas import tpu as pltpu
from jax.sharding import PartitionSpec as P

AXES = ("space", "ch")
PHASES = (((1, 0), (3, -1)), ((2, 0), (0, 1)))
COLUMNS = ((3, 0, 1), (0, 1, 2))


def column_of(bias):
    lanes = bias.shape[-1]
    return jnp.transpose(jnp.broadcast_to(bias, (lanes, lanes)))


def shifted(value, step):
    cols = value.shape[1]
    place = lax.broadcasted_iota(jnp.int32, value.shape, 1)
    edge = 0 if step == 1 else cols - 1
    return jnp.where(place == edge, 0.0, pltpu.roll(value, step % cols, 1))


def compute(x_ref, w_ref, b_up_ref, late, w_conv_ref, b_conv_ref, out_ref, u_ref, total_ref, first, last):
    rows = out_ref.shape[2]
    cout = out_ref.shape[0]
    cols = x_ref.shape[3]
    held = rows + 2
    bias = column_of(b_up_ref[...])
    bias = jnp.concatenate([bias, bias], axis=0)
    for row_phase in (0, 1):
        for col_phase in (0, 1):
            taps = []
            for row_tap, row_shift in PHASES[row_phase]:
                for col_tap, col_shift in PHASES[col_phase]:
                    slot = row_shift + 1 - row_phase
                    taps.append((row_tap * 4 + col_tap, slot, col_shift % 3))
            kernel = jnp.concatenate([w_ref[tap] for tap, _, _ in taps], axis=1)
            for start in range(0, held // 2, 2):
                places = range(start, min(start + 2, held // 2))
                cells = jnp.concatenate(
                    [
                        jnp.concatenate([x_ref[copy, slot + place] for place in places], axis=1)
                        for _, slot, copy in taps
                    ],
                    axis=0,
                )
                summed = jnp.dot(kernel, cells, preferred_element_type=jnp.float32)
                for number, place in enumerate(places):
                    row = 2 * place + 1 - row_phase
                    value = summed[:, number * cols : (number + 1) * cols] + bias
                    value = jnp.where(value > 0, value, 0.2 * value)
                    if row == 0:
                        value = jnp.where(first, 0.0, value)
                    if row == held - 1:
                        value = jnp.where(last, 0.0, value)
                    u_ref[col_phase, row] = value.astype(jnp.bfloat16)
                    moved = shifted(value, -1 if col_phase == 0 else 1)
                    u_ref[2 + col_phase, row] = moved.astype(jnp.bfloat16)

    late.wait()
    bias = column_of(b_conv_ref[...])
    bias = jnp.concatenate([bias, bias], axis=0)
    source = lax.broadcasted_iota(jnp.int32, (2 * cols, 2 * cols), 0)
    target = lax.broadcasted_iota(jnp.int32, (2 * cols, 2 * cols), 1)
    wanted = jnp.where(source < cols, 2 * source, 2 * (source - cols) + 1)
    interleave = jnp.where(wanted == target, 1.0, 0.0).astype(jnp.bfloat16)
    kernels = []
    for row_tap in range(3):
        for col_tap in range(3):
            below, here, above = [w_conv_ref[a * 9 + row_tap * 3 + col_tap] for a in range(3)]
            kernels.append(
                jnp.concatenate(
                    [jnp.concatenate([here, above], 1), jnp.concatenate([below, here], 1)], 0
                )
            )
    kernel = jnp.concatenate(kernels, axis=1)
    for start in range(0, rows, 2):
        halves = []
        for col_phase in (0, 1):
            cells = jnp.concatenate(
                [
                    jnp.concatenate([u_ref[copy, start + row_tap], u_ref[copy, start + row_tap + 1]], 1)
                    for row_tap in range(3)
                    for copy in COLUMNS[col_phase]
                ],
                axis=0,
            )
            halves.append(jnp.dot(kernel, cells, preferred_element_type=jnp.float32))
        for number in (0, 1):
            pair = [
                (half[:, number * cols : (number + 1) * cols] + bias).astype(jnp.bfloat16)
                for half in halves
            ]
            pair = jnp.concatenate(pair, axis=1)
            mixed = jnp.dot(pair, interleave, preferred_element_type=jnp.float32)
            for side in (0, 1):
                total_ref[side, pl.ds(start + number, 2 * cout, stride=rows), :] = mixed[
                    :, side * cols : (side + 1) * cols
                ]
    for plane in (0, 1):
        for side in (0, 1):
            block = total_ref[side, pl.ds(plane * cout * rows, cout * rows), :]
            out_ref[:, plane, :, side * cols : (side + 1) * cols] = block.reshape(
                cout, rows, cols
            ).astype(jnp.bfloat16)


def store_row(x_ref, slot, offset, value):
    chans = value.shape[0]
    where = pl.ds(pl.multiple_of(offset, 16), chans)
    wide = value.astype(jnp.float32)
    x_ref[0, slot, where] = value
    x_ref[1, slot, where] = shifted(wide, -1).astype(jnp.bfloat16)
    x_ref[2, slot, where] = shifted(wide, 1).astype(jnp.bfloat16)


def position():
    s, c = lax.axis_index("space"), lax.axis_index("ch")
    return s, c


def paired_kernel(
    own_ref, peer_ref, near_ref, far_ref, w_own_ref, *refs,
):
    *part_refs, b_up_ref, w_conv_ref, b_conv_ref, out_ref, x_ref, w_ref, v_ref, u_ref, total_ref, sems = refs
    s, c = position()
    part, cout = w_own_ref.shape[1], out_ref.shape[0]

    def taps_of(plane, half, first, count):
        place = pl.multiple_of(plane * cout + half * part, part)
        return w_ref.at[pl.ds(first, count), pl.ds(place, part)]

    copies = [
        pltpu.make_async_copy(
            w_own_ref.at[pl.ds(16 + 16 * plane, 16)], taps_of(plane, c, 0, 16), sems.at[plane]
        )
        for plane in (0, 1)
    ]
    me = lax.rem(s, 4)
    x, core = me // 2, lax.rem(me, 2)
    sources = ((x, core), (x, 1 - core), (1 - x, core), (1 - x, 1 - core))
    for number, part_ref in enumerate(part_refs):
        plane, side = sources[number // 2]
        place = taps_of(plane, 1 - c, 8 * side + 4 * (number % 2), 4)
        copies.append(pltpu.make_async_copy(part_ref, place, sems.at[2 + number]))
    late = pltpu.make_async_copy(w_conv_ref, v_ref, sems.at[10])
    for copy in copies + [late]:
        copy.start()
    chans = own_ref.shape[1]
    share = peer_ref.shape[0]
    own, other = c * chans, (1 - c) * chans
    for place in range(share):
        store_row(x_ref, place + 1 - c, own, own_ref[place + c * (own_ref.shape[0] - share)])
        store_row(x_ref, place + 1 - c, other, peer_ref[place])
    store_row(x_ref, c * share, own, near_ref[0])
    store_row(x_ref, c * share, other, far_ref[0])
    for copy in copies:
        copy.wait()
    first = (s == 0) & (c == 0)
    last = (s == lax.axis_size("space") - 1) & (c == 1)
    compute(x_ref, w_ref, b_up_ref, late, v_ref, b_conv_ref, out_ref, u_ref, total_ref, first, last)


def gathered_kernel(
    rows_ref, w_all_ref, b_up_ref, w_conv_ref, b_conv_ref, out_ref, x_ref, w_ref, v_ref, u_ref, total_ref, sems
):
    s, c = position()
    cout = out_ref.shape[0]
    copies = [
        pltpu.make_async_copy(
            w_all_ref.at[pl.ds(16 * plane, 16)], w_ref.at[:, pl.ds(plane * cout, cout)], sems.at[plane]
        )
        for plane in (0, 1)
    ]
    late = pltpu.make_async_copy(w_conv_ref, v_ref, sems.at[10])
    for copy in copies + [late]:
        copy.start()
    for slot in range(rows_ref.shape[0]):
        store_row(x_ref, slot, 0, rows_ref[slot])
    for copy in copies:
        copy.wait()
    first = (s == 0) & (c == 0)
    last = (s == lax.axis_size("space") - 1) & (c == lax.axis_size("ch") - 1)
    compute(x_ref, w_ref, b_up_ref, late, v_ref, b_conv_ref, out_ref, u_ref, total_ref, first, last)


def run(kernel, spaces, operands, sizes):
    cin, cout, rows, cols = sizes
    spec = {"vmem": pl.BlockSpec(memory_space=pltpu.VMEM), "any": pl.BlockSpec(memory_space=pl.ANY), "hbm": pl.BlockSpec(memory_space=pltpu.HBM)}
    return pl.pallas_call(
        kernel,
        out_shape=jax.ShapeDtypeStruct((cout, 2, rows, 2 * cols), jnp.bfloat16),
        in_specs=[spec[space] for space in spaces],
        out_specs=spec["vmem"],
        scratch_shapes=[
            pltpu.VMEM((3, rows // 2 + 2, cin, cols), jnp.bfloat16),
            pltpu.VMEM((16, 2 * cout, cin), jnp.bfloat16),
            pltpu.VMEM((27, cout, cout), jnp.bfloat16),
            pltpu.VMEM((4, rows + 2, 2 * cout, cols), jnp.bfloat16),
            pltpu.VMEM((2, 2 * cout * rows, cols), jnp.float32),
            pltpu.SemaphoreType.DMA((11,)),
        ],
        compiler_params=pltpu.CompilerParams(vmem_limit_bytes=48 * 2**20),
    )(*operands)


def paired(inputs, w_up, b_up, w_conv, b_conv, sizes):
    spaces = lax.axis_size("space")
    s, c = position()
    held = inputs.shape[2]
    share = held // 2 + 1

    def at(space, ch):
        return space * 2 + ch

    across = [(at(i, j), at(i, 1 - j)) for i in range(spaces) for j in (0, 1)]
    cores = [(at(i, j), at(i ^ 1, j)) for i in range(spaces) for j in (0, 1)]
    pairs = [(at(i, j), at(i ^ 2, j)) for i in range(spaces) for j in (0, 1)]
    steps = [(at(i - 1, 0), at(i, 0)) for i in range(1, spaces)]
    steps += [(at(i + 1, 1), at(i, 1)) for i in range(spaces - 1)]

    quarter = 16 + 8 * lax.rem(s, 4)
    mine = [lax.dynamic_slice_in_dim(w_up, quarter + 4 * piece, 4, 0) for piece in (0, 1)]
    mine = lax.optimization_barrier(mine)
    w_y = [lax.ppermute(piece, AXES, across) for piece in mine]

    rows = inputs[:, 0].transpose(1, 0, 2)
    wanted = lax.dynamic_slice_in_dim(rows, (1 - c) * (held - share), share, 0)
    edge = lax.dynamic_slice_in_dim(rows, (1 - c) * (held - 1), 1, 0)
    edge_other = lax.dynamic_slice_in_dim(rows, c * (held - 1), 1, 0)
    w_y[0], wanted, edge, edge_other = lax.optimization_barrier((w_y[0], wanted, edge, edge_other))
    w_x, w_y_core = [None, None], [None, None]
    w_x[0] = lax.ppermute(w_y[0], AXES, pairs)
    far = lax.ppermute(edge_other, AXES, across)
    peer = lax.ppermute(wanted, AXES, across)
    w_y_core[0] = lax.ppermute(w_y[0], AXES, cores)
    near = lax.ppermute(edge, AXES, steps)
    w_y[1], w_y_core[0] = lax.optimization_barrier((w_y[1], w_y_core[0]))
    w_x[1] = lax.ppermute(w_y[1], AXES, pairs)
    w_y_core[1] = lax.ppermute(w_y[1], AXES, cores)
    far, near, w_x[0], w_y_core[1] = lax.optimization_barrier((far, near, w_x[0], w_y_core[1]))
    far = lax.ppermute(far, AXES, steps)
    w_x_core = [lax.ppermute(w_x[0], AXES, cores), None]
    far, peer, w_x[1] = lax.optimization_barrier((far, peer, w_x[1]))
    w_x_core[1] = lax.ppermute(w_x[1], AXES, cores)
    w_parts = (*w_y, *w_y_core, *w_x, *w_x_core)
    operands = (rows, peer, near, far, w_up, *w_parts, b_up[None], w_conv, b_conv[None])
    places = ("vmem",) * 4 + ("any",) * 9 + ("vmem", "hbm", "vmem")
    return run(paired_kernel, places, operands, sizes)


def gathered(inputs, w_up, b_up, w_conv, b_conv, sizes):
    spaces, chs = lax.axis_size("space"), lax.axis_size("ch")
    c = lax.axis_index("ch")
    w_all = lax.all_gather(w_up[16:48], "ch", axis=1, tiled=True)
    rows = lax.all_gather(inputs[:, 0], "ch", axis=0, tiled=True).transpose(1, 0, 2)
    forward = [(i, i + 1) for i in range(spaces - 1)]
    backward = [(j, i) for i, j in forward]
    low = lax.ppermute(rows[-1:], "space", forward)
    high = lax.ppermute(rows[:1], "space", backward)
    rows = jnp.concatenate([low, rows, high], axis=0)
    share = inputs.shape[2] // chs
    rows = lax.dynamic_slice_in_dim(rows, c * share, share + 2, 0)
    operands = (rows, w_all, b_up[None], w_conv, b_conv[None])
    return run(gathered_kernel, ("vmem", "any", "vmem", "hbm", "vmem"), operands, sizes)


def local(inputs, w_up, b_up, w_conv, b_conv):
    chs = lax.axis_size("ch")
    sizes = (w_up.shape[2], w_conv.shape[1], 2 * inputs.shape[2] // chs, inputs.shape[3])
    plan = paired if chs == 2 and lax.axis_size("space") % 4 == 0 else gathered
    return plan(inputs, w_up, b_up, w_conv, b_conv, sizes)


def solution(mesh):
    return jax.shard_map(
        local,
        mesh=mesh,
        in_specs=(P("ch", None, "space", None), P(None, "ch", None), P(), P(), P()),
        out_specs=P(None, None, ("space", "ch"), None),
        check_vma=False,
    )
```

```python
import jax
import jax.numpy as jnp
from jax import lax
from jax.experimental import pallas as pl
from jax.experimental.pallas import tpu as pltpu
from jax.sharding import PartitionSpec as P

AXES = ("space", "ch")
PHASES = (((1, 0), (3, -1)), ((2, 0), (0, 1)))
COLUMNS = ((3, 0, 1), (0, 1, 2))


def column_of(bias):
    lanes = bias.shape[-1]
    return jnp.transpose(jnp.broadcast_to(bias, (lanes, lanes)))


def shifted(value, step):
    cols = value.shape[1]
    place = lax.broadcasted_iota(jnp.int32, value.shape, 1)
    edge = 0 if step == 1 else cols - 1
    return jnp.where(place == edge, 0.0, pltpu.roll(value, step % cols, 1))


def compute(x_ref, w_ref, b_up_ref, w_conv_ref, b_conv_ref, out_ref, u_ref, total_ref, first, last):
    rows = out_ref.shape[2]
    cout = out_ref.shape[0]
    cols = x_ref.shape[3]
    held = rows + 2
    bias = column_of(b_up_ref[...])
    bias = jnp.concatenate([bias, bias], axis=0)
    for row_phase in (0, 1):
        for col_phase in (0, 1):
            taps = []
            for row_tap, row_shift in PHASES[row_phase]:
                for col_tap, col_shift in PHASES[col_phase]:
                    slot = row_shift + 1 - row_phase
                    taps.append((row_tap * 4 + col_tap, slot, col_shift % 3))
            kernel = jnp.concatenate([w_ref[tap] for tap, _, _ in taps], axis=1)
            for start in range(0, held // 2, 2):
                places = range(start, min(start + 2, held // 2))
                cells = jnp.concatenate(
                    [
                        jnp.concatenate([x_ref[copy, slot + place] for place in places], axis=1)
                        for _, slot, copy in taps
                    ],
                    axis=0,
                )
                summed = jnp.dot(kernel, cells, preferred_element_type=jnp.float32)
                for number, place in enumerate(places):
                    row = 2 * place + 1 - row_phase
                    value = summed[:, number * cols : (number + 1) * cols] + bias
                    value = jnp.where(value > 0, value, 0.2 * value)
                    if row == 0:
                        value = jnp.where(first, 0.0, value)
                    if row == held - 1:
                        value = jnp.where(last, 0.0, value)
                    u_ref[col_phase, row] = value.astype(jnp.bfloat16)
                    moved = shifted(value, -1 if col_phase == 0 else 1)
                    u_ref[2 + col_phase, row] = moved.astype(jnp.bfloat16)

    bias = column_of(b_conv_ref[...])
    bias = jnp.concatenate([bias, bias], axis=0)
    source = lax.broadcasted_iota(jnp.int32, (2 * cols, 2 * cols), 0)
    target = lax.broadcasted_iota(jnp.int32, (2 * cols, 2 * cols), 1)
    wanted = jnp.where(source < cols, 2 * source, 2 * (source - cols) + 1)
    interleave = jnp.where(wanted == target, 1.0, 0.0).astype(jnp.bfloat16)
    kernels = []
    for row_tap in range(3):
        for col_tap in range(3):
            below, here, above = [w_conv_ref[a * 9 + row_tap * 3 + col_tap] for a in range(3)]
            kernels.append(
                jnp.concatenate(
                    [jnp.concatenate([here, above], 1), jnp.concatenate([below, here], 1)], 0
                )
            )
    kernel = jnp.concatenate(kernels, axis=1)
    for start in range(0, rows, 2):
        halves = []
        for col_phase in (0, 1):
            cells = jnp.concatenate(
                [
                    jnp.concatenate([u_ref[copy, start + row_tap], u_ref[copy, start + row_tap + 1]], 1)
                    for row_tap in range(3)
                    for copy in COLUMNS[col_phase]
                ],
                axis=0,
            )
            halves.append(jnp.dot(kernel, cells, preferred_element_type=jnp.float32))
        for number in (0, 1):
            pair = [
                (half[:, number * cols : (number + 1) * cols] + bias).astype(jnp.bfloat16)
                for half in halves
            ]
            pair = jnp.concatenate(pair, axis=1)
            mixed = jnp.dot(pair, interleave, preferred_element_type=jnp.float32)
            for side in (0, 1):
                total_ref[side, pl.ds(start + number, 2 * cout, stride=rows), :] = mixed[
                    :, side * cols : (side + 1) * cols
                ]
    for plane in (0, 1):
        for side in (0, 1):
            block = total_ref[side, pl.ds(plane * cout * rows, cout * rows), :]
            out_ref[:, plane, :, side * cols : (side + 1) * cols] = block.reshape(
                cout, rows, cols
            ).astype(jnp.bfloat16)


def store_row(x_ref, slot, offset, value):
    chans = value.shape[0]
    where = pl.ds(pl.multiple_of(offset, 16), chans)
    wide = value.astype(jnp.float32)
    x_ref[0, slot, where] = value
    x_ref[1, slot, where] = shifted(wide, -1).astype(jnp.bfloat16)
    x_ref[2, slot, where] = shifted(wide, 1).astype(jnp.bfloat16)


def position():
    s, c = lax.axis_index("space"), lax.axis_index("ch")
    return s, c


def paired_kernel(
    own_ref, edge_ref, peer_ref, near_ref, far_ref, w_own_ref, w_y_ref, w_y_core_ref, w_x_ref, w_x_core_ref,
    b_up_ref, w_conv_ref, b_conv_ref, out_ref, x_ref, w_ref, u_ref, total_ref, sems,
):
    s, c = position()
    part, cout = w_own_ref.shape[1], out_ref.shape[0]

    def taps_of(plane, half, first, count):
        place = pl.multiple_of(plane * cout + half * part, part)
        return w_ref.at[pl.ds(first, count), pl.ds(place, part)]

    copies = [
        pltpu.make_async_copy(
            w_own_ref.at[pl.ds(16 + 16 * plane, 16)], taps_of(plane, c, 0, 16), sems.at[plane]
        )
        for plane in (0, 1)
    ]
    me = lax.rem(s, 4)
    x, core = me // 2, lax.rem(me, 2)
    parts = ((w_y_ref, x, core), (w_y_core_ref, x, 1 - core), (w_x_ref, 1 - x, core), (w_x_core_ref, 1 - x, 1 - core))
    for number, (part_ref, plane, side) in enumerate(parts):
        copies.append(
            pltpu.make_async_copy(part_ref, taps_of(plane, 1 - c, 8 * side, 8), sems.at[2 + number])
        )
    for copy in copies:
        copy.start()
    chans = own_ref.shape[1]
    share = peer_ref.shape[0]
    own, other = c * chans, (1 - c) * chans
    for place in range(share + 1):
        store_row(x_ref, place + 1 - c, own, own_ref[place + c * (own_ref.shape[0] - share - 1)])
    for place in range(share):
        store_row(x_ref, place + 2 - 2 * c, other, peer_ref[place])
    store_row(x_ref, 1 + c * (share - 1), other, edge_ref[0])
    store_row(x_ref, c * (share + 1), own, far_ref[0])
    store_row(x_ref, c * (share + 1), other, near_ref[0])
    for copy in copies:
        copy.wait()
    first = (s == 0) & (c == 0)
    last = (s == lax.axis_size("space") - 1) & (c == 1)
    compute(x_ref, w_ref, b_up_ref, w_conv_ref, b_conv_ref, out_ref, u_ref, total_ref, first, last)


def gathered_kernel(
    rows_ref, w_all_ref, b_up_ref, w_conv_ref, b_conv_ref, out_ref, x_ref, w_ref, u_ref, total_ref, sems
):
    s, c = position()
    cout = out_ref.shape[0]
    copies = [
        pltpu.make_async_copy(
            w_all_ref.at[pl.ds(16 * plane, 16)], w_ref.at[:, pl.ds(plane * cout, cout)], sems.at[plane]
        )
        for plane in (0, 1)
    ]
    for copy in copies:
        copy.start()
    for slot in range(rows_ref.shape[0]):
        store_row(x_ref, slot, 0, rows_ref[slot])
    for copy in copies:
        copy.wait()
    first = (s == 0) & (c == 0)
    last = (s == lax.axis_size("space") - 1) & (c == lax.axis_size("ch") - 1)
    compute(x_ref, w_ref, b_up_ref, w_conv_ref, b_conv_ref, out_ref, u_ref, total_ref, first, last)


def run(kernel, spaces, operands, sizes):
    cin, cout, rows, cols = sizes
    spec = {"vmem": pl.BlockSpec(memory_space=pltpu.VMEM), "any": pl.BlockSpec(memory_space=pl.ANY)}
    return pl.pallas_call(
        kernel,
        out_shape=jax.ShapeDtypeStruct((cout, 2, rows, 2 * cols), jnp.bfloat16),
        in_specs=[spec[space] for space in spaces],
        out_specs=spec["vmem"],
        scratch_shapes=[
            pltpu.VMEM((3, rows // 2 + 2, cin, cols), jnp.bfloat16),
            pltpu.VMEM((16, 2 * cout, cin), jnp.bfloat16),
            pltpu.VMEM((4, rows + 2, 2 * cout, cols), jnp.bfloat16),
            pltpu.VMEM((2, 2 * cout * rows, cols), jnp.float32),
            pltpu.SemaphoreType.DMA((6,)),
        ],
        compiler_params=pltpu.CompilerParams(vmem_limit_bytes=48 * 2**20),
    )(*operands)


def paired(inputs, w_up, b_up, w_conv, b_conv, sizes):
    spaces = lax.axis_size("space")
    s, c = position()
    held = inputs.shape[2]
    share = held // 2 + 1

    def at(space, ch):
        return space * 2 + ch

    across = [(at(i, j), at(i, 1 - j)) for i in range(spaces) for j in (0, 1)]
    cores = [(at(i, j), at(i ^ 1, j)) for i in range(spaces) for j in (0, 1)]
    pairs = [(at(i, j), at(i ^ 2, j)) for i in range(spaces) for j in (0, 1)]
    outer = [(t, t + 1) for t in range(1, 2 * spaces - 1, 2)]
    outer += [(j, i) for i, j in outer]

    quarter = 8 * lax.rem(s, 4)
    w_y = lax.ppermute(lax.dynamic_slice_in_dim(w_up, 16 + quarter, 8, 0), AXES, across)

    rows = inputs[:, 0].transpose(1, 0, 2)
    last = held - 1
    edge_own = lax.dynamic_slice_in_dim(rows, c * last, 1, 0)
    edge_other = lax.dynamic_slice_in_dim(rows, (1 - c) * last, 1, 0)
    wanted = lax.dynamic_slice_in_dim(rows, 1 + (1 - c) * (held - share - 1), share - 1, 0)
    edge_own, edge_other, wanted = lax.optimization_barrier((edge_own, edge_other, wanted))
    edge = lax.ppermute(edge_other, AXES, across)
    peer = lax.ppermute(wanted, AXES, across)
    w_y, edge = lax.optimization_barrier((w_y, edge))
    w_x = lax.ppermute(w_y, AXES, pairs)
    w_y_core = lax.ppermute(w_y, AXES, cores)
    near = lax.ppermute(edge_own, AXES, outer)
    far = lax.ppermute(edge, AXES, outer)
    w_x, w_y_core, peer, near, far = lax.optimization_barrier((w_x, w_y_core, peer, near, far))
    w_x_core = lax.ppermute(w_x, AXES, cores)
    w_parts = (w_y, w_y_core, w_x, w_x_core)
    operands = (rows, edge, peer, near, far, w_up, *w_parts, b_up[None], w_conv, b_conv[None])
    places = ("vmem",) * 5 + ("any",) * 5 + ("vmem",) * 3
    return run(paired_kernel, places, operands, sizes)


def gathered(inputs, w_up, b_up, w_conv, b_conv, sizes):
    spaces, chs = lax.axis_size("space"), lax.axis_size("ch")
    c = lax.axis_index("ch")
    w_all = lax.all_gather(w_up[16:48], "ch", axis=1, tiled=True)
    rows = lax.all_gather(inputs[:, 0], "ch", axis=0, tiled=True).transpose(1, 0, 2)
    forward = [(i, i + 1) for i in range(spaces - 1)]
    backward = [(j, i) for i, j in forward]
    low = lax.ppermute(rows[-1:], "space", forward)
    high = lax.ppermute(rows[:1], "space", backward)
    rows = jnp.concatenate([low, rows, high], axis=0)
    share = inputs.shape[2] // chs
    rows = lax.dynamic_slice_in_dim(rows, c * share, share + 2, 0)
    operands = (rows, w_all, b_up[None], w_conv, b_conv[None])
    return run(gathered_kernel, ("vmem", "any", "vmem", "vmem", "vmem"), operands, sizes)


def local(inputs, w_up, b_up, w_conv, b_conv):
    chs = lax.axis_size("ch")
    sizes = (w_up.shape[2], w_conv.shape[1], 2 * inputs.shape[2] // chs, inputs.shape[3])
    plan = paired if chs == 2 and lax.axis_size("space") % 4 == 0 else gathered
    return plan(inputs, w_up, b_up, w_conv, b_conv, sizes)


def solution(mesh):
    return jax.shard_map(
        local,
        mesh=mesh,
        in_specs=(P("ch", None, "space", None), P(None, "ch", None), P(), P(), P()),
        out_specs=P(None, None, ("space", "ch"), None),
        check_vma=False,
    )
```

```python
import jax
import jax.numpy as jnp
from jax import lax
from jax.experimental import pallas as pl
from jax.experimental.pallas import tpu as pltpu
from jax.sharding import PartitionSpec as P

AXES = ("space", "ch")
PHASES = (((1, 0), (3, -1)), ((2, 0), (0, 1)))
COLUMNS = ((3, 0, 1), (0, 1, 2))


def column_of(bias):
    lanes = bias.shape[-1]
    return jnp.transpose(jnp.broadcast_to(bias, (lanes, lanes)))


def shifted(value, step):
    cols = value.shape[1]
    place = lax.broadcasted_iota(jnp.int32, value.shape, 1)
    edge = 0 if step == 1 else cols - 1
    return jnp.where(place == edge, 0.0, pltpu.roll(value, step % cols, 1))


def compute(x_ref, w_ref, w_conv_ref, b_ref, kept, out_ref, u_ref, total_ref, first, last):
    rows = out_ref.shape[2]
    cout = out_ref.shape[0]
    cols = x_ref.shape[3]
    held = rows + 2
    kept[0].wait()
    bias = column_of(b_ref[0])
    bias = jnp.concatenate([bias, bias], axis=0)
    for row_phase in (0, 1):
        for col_phase in (0, 1):
            taps = []
            for row_tap, row_shift in PHASES[row_phase]:
                for col_tap, col_shift in PHASES[col_phase]:
                    slot = row_shift + 1 - row_phase
                    taps.append((row_tap * 4 + col_tap, slot, col_shift % 3))
            kernel = jnp.concatenate([w_ref[tap] for tap, _, _ in taps], axis=1)
            for start in range(0, held // 2, 2):
                places = range(start, min(start + 2, held // 2))
                cells = jnp.concatenate(
                    [
                        jnp.concatenate([x_ref[copy, slot + place] for place in places], axis=1)
                        for _, slot, copy in taps
                    ],
                    axis=0,
                )
                summed = jnp.dot(kernel, cells, preferred_element_type=jnp.float32)
                for number, place in enumerate(places):
                    row = 2 * place + 1 - row_phase
                    value = summed[:, number * cols : (number + 1) * cols] + bias
                    value = jnp.where(value > 0, value, 0.2 * value)
                    if row == 0:
                        value = jnp.where(first, 0.0, value)
                    if row == held - 1:
                        value = jnp.where(last, 0.0, value)
                    u_ref[col_phase, row] = value.astype(jnp.bfloat16)
                    moved = shifted(value, -1 if col_phase == 0 else 1)
                    u_ref[2 + col_phase, row] = moved.astype(jnp.bfloat16)

    kept[1].wait()
    kept[2].wait()
    bias = column_of(b_ref[1])
    bias = jnp.concatenate([bias, bias], axis=0)
    source = lax.broadcasted_iota(jnp.int32, (2 * cols, 2 * cols), 0)
    target = lax.broadcasted_iota(jnp.int32, (2 * cols, 2 * cols), 1)
    wanted = jnp.where(source < cols, 2 * source, 2 * (source - cols) + 1)
    interleave = jnp.where(wanted == target, 1.0, 0.0).astype(jnp.bfloat16)
    kernels = []
    for row_tap in range(3):
        for col_tap in range(3):
            below, here, above = [w_conv_ref[a * 9 + row_tap * 3 + col_tap] for a in range(3)]
            kernels.append(
                jnp.concatenate(
                    [jnp.concatenate([here, above], 1), jnp.concatenate([below, here], 1)], 0
                )
            )
    kernel = jnp.concatenate(kernels, axis=1)
    for start in range(0, rows, 2):
        halves = []
        for col_phase in (0, 1):
            cells = jnp.concatenate(
                [
                    jnp.concatenate([u_ref[copy, start + row_tap], u_ref[copy, start + row_tap + 1]], 1)
                    for row_tap in range(3)
                    for copy in COLUMNS[col_phase]
                ],
                axis=0,
            )
            halves.append(jnp.dot(kernel, cells, preferred_element_type=jnp.float32))
        for number in (0, 1):
            pair = [
                (half[:, number * cols : (number + 1) * cols] + bias).astype(jnp.bfloat16)
                for half in halves
            ]
            pair = jnp.concatenate(pair, axis=1)
            mixed = jnp.dot(pair, interleave, preferred_element_type=jnp.float32)
            for side in (0, 1):
                total_ref[side, pl.ds(start + number, 2 * cout, stride=rows), :] = mixed[
                    :, side * cols : (side + 1) * cols
                ]
    for plane in (0, 1):
        for side in (0, 1):
            block = total_ref[side, pl.ds(plane * cout * rows, cout * rows), :]
            out_ref[:, plane, :, side * cols : (side + 1) * cols] = block.reshape(
                cout, rows, cols
            ).astype(jnp.bfloat16)


def store_row(x_ref, slot, offset, value):
    chans = value.shape[0]
    where = pl.ds(pl.multiple_of(offset, 16), chans)
    wide = value.astype(jnp.float32)
    x_ref[0, slot, where] = value
    x_ref[1, slot, where] = shifted(wide, -1).astype(jnp.bfloat16)
    x_ref[2, slot, where] = shifted(wide, 1).astype(jnp.bfloat16)


def position():
    s, c = lax.axis_index("space"), lax.axis_index("ch")
    return s, c


def paired_kernel(own_ref, peer_ref, near_ref, far_ref, w_own_ref, *refs):
    *part_refs, b_up_ref, w_conv_ref, b_conv_ref, out_ref, x_ref, w_ref, v_ref, b_ref, u_ref, total_ref, sems = refs
    s, c = position()
    part, cout = w_own_ref.shape[1], out_ref.shape[0]
    kept = keep(b_up_ref, w_conv_ref, b_conv_ref, b_ref, v_ref, sems)

    def taps_of(plane, half, first, count):
        place = pl.multiple_of(plane * cout + half * part, part)
        return w_ref.at[pl.ds(first, count), pl.ds(place, part)]

    copies = [
        pltpu.make_async_copy(
            w_own_ref.at[pl.ds(16 + 16 * plane, 16)], taps_of(plane, c, 0, 16), sems.at[3 + plane]
        )
        for plane in (0, 1)
    ]
    me = lax.rem(s, 4)
    x, core = me // 2, lax.rem(me, 2)
    firsts = [4 * (2 * i + j) for i in (x, 1 - x) for j in (core, 1 - core)] + [8 * core, 8 - 8 * core]
    for number, part_ref in enumerate(part_refs):
        place = taps_of(number // 4, 1 - c, firsts[number], part_ref.shape[0])
        copies.append(pltpu.make_async_copy(part_ref, place, sems.at[5 + number]))
    for copy in copies:
        copy.start()
    chans = own_ref.shape[1]
    share = peer_ref.shape[0]
    own, other = c * chans, (1 - c) * chans
    for place in range(share):
        store_row(x_ref, place + 1 - c, own, own_ref[place + c * (own_ref.shape[0] - share)])
        store_row(x_ref, place + 1 - c, other, peer_ref[place])
    store_row(x_ref, c * share, own, near_ref[0])
    store_row(x_ref, c * share, other, far_ref[0])
    for copy in copies:
        copy.wait()
    first = (s == 0) & (c == 0)
    last = (s == lax.axis_size("space") - 1) & (c == 1)
    compute(x_ref, w_ref, v_ref, b_ref, kept, out_ref, u_ref, total_ref, first, last)


def gathered_kernel(rows_ref, w_all_ref, *refs):
    b_up_ref, w_conv_ref, b_conv_ref, out_ref, x_ref, w_ref, v_ref, b_ref, u_ref, total_ref, sems = refs
    s, c = position()
    cout = out_ref.shape[0]
    kept = keep(b_up_ref, w_conv_ref, b_conv_ref, b_ref, v_ref, sems)
    copies = [
        pltpu.make_async_copy(
            w_all_ref.at[pl.ds(16 * plane, 16)], w_ref.at[:, pl.ds(plane * cout, cout)], sems.at[3 + plane]
        )
        for plane in (0, 1)
    ]
    for copy in copies:
        copy.start()
    for slot in range(rows_ref.shape[0]):
        store_row(x_ref, slot, 0, rows_ref[slot])
    for copy in copies:
        copy.wait()
    first = (s == 0) & (c == 0)
    last = (s == lax.axis_size("space") - 1) & (c == lax.axis_size("ch") - 1)
    compute(x_ref, w_ref, v_ref, b_ref, kept, out_ref, u_ref, total_ref, first, last)


def keep(b_up_ref, w_conv_ref, b_conv_ref, b_ref, v_ref, sems):
    kept = [
        pltpu.make_async_copy(b_up_ref, b_ref.at[0], sems.at[0]),
        pltpu.make_async_copy(w_conv_ref, v_ref, sems.at[1]),
        pltpu.make_async_copy(b_conv_ref, b_ref.at[1], sems.at[2]),
    ]
    for copy in kept:
        copy.start()
    return kept


def run(kernel, spaces, operands, sizes):
    cin, cout, rows, cols = sizes
    spec = {"vmem": pl.BlockSpec(memory_space=pltpu.VMEM), "any": pl.BlockSpec(memory_space=pl.ANY)}
    spec["hbm"] = spec["any"]
    operands = [
        pltpu.with_memory_space_constraint(operand, pltpu.HBM) if space == "hbm" else operand
        for operand, space in zip(operands, spaces)
    ]
    return pl.pallas_call(
        kernel,
        out_shape=jax.ShapeDtypeStruct((cout, 2, rows, 2 * cols), jnp.bfloat16),
        in_specs=[spec[space] for space in spaces],
        out_specs=spec["vmem"],
        scratch_shapes=[
            pltpu.VMEM((3, rows // 2 + 2, cin, cols), jnp.bfloat16),
            pltpu.VMEM((16, 2 * cout, cin), jnp.bfloat16),
            pltpu.VMEM((27, cout, cout), jnp.bfloat16),
            pltpu.VMEM((2, 1, cout), jnp.float32),
            pltpu.VMEM((4, rows + 2, 2 * cout, cols), jnp.bfloat16),
            pltpu.VMEM((2, 2 * cout * rows, cols), jnp.float32),
            pltpu.SemaphoreType.DMA((11,)),
        ],
        compiler_params=pltpu.CompilerParams(vmem_limit_bytes=48 * 2**20),
    )(*operands)


def paired(inputs, w_up, b_up, w_conv, b_conv, sizes):
    spaces = lax.axis_size("space")
    s, c = position()
    held = inputs.shape[2]
    share = held // 2 + 1

    def at(space, ch):
        return space * 2 + ch

    across = [(at(i, j), at(i, 1 - j)) for i in range(spaces) for j in (0, 1)]
    cores = [(at(i, j), at(i ^ 1, j)) for i in range(spaces) for j in (0, 1)]
    pairs = [(at(i, j), at(i ^ 2, j)) for i in range(spaces) for j in (0, 1)]
    down = [(at(i - 1, 0), at(i, 0)) for i in range(1, spaces)]
    up = [(at(i + 1, 1), at(i, 1)) for i in range(spaces - 1)]
    outer = [(t, t + 1) for t in range(1, 2 * spaces - 1, 2)]
    outer += [(j, i) for i, j in outer]

    w_a = lax.dynamic_slice_in_dim(w_up, 16 + 4 * lax.rem(s, 4), 4, 0)
    w_b = lax.dynamic_slice_in_dim(w_up, 32 + 8 * lax.rem(s, 2), 8, 0)
    w_a, w_b = lax.optimization_barrier((w_a, w_b))
    w_a = lax.ppermute(w_a, AXES, across)
    w_b = lax.ppermute(w_b, AXES, across)

    rows = inputs[:, 0].transpose(1, 0, 2)
    last = held - 1
    edge_outer = lax.dynamic_slice_in_dim(rows, c * last, 1, 0)
    edge_inner = lax.dynamic_slice_in_dim(rows, (1 - c) * last, 1, 0)
    wanted = lax.dynamic_slice_in_dim(rows, (1 - c) * (held - share), share, 0)
    w_a, edge_outer, edge_inner, wanted = lax.optimization_barrier((w_a, edge_outer, edge_inner, wanted))
    w_ax = lax.ppermute(w_a, AXES, pairs)
    peer = lax.ppermute(wanted, AXES, across)
    w_ac = lax.ppermute(w_a, AXES, cores)
    near = lax.ppermute(edge_inner, AXES, down + up)
    far = lax.ppermute(edge_outer, AXES, outer)
    w_b, w_ax, w_ac = lax.optimization_barrier((w_b, w_ax, w_ac))
    w_bc = lax.ppermute(w_b, AXES, cores)
    w_axc = lax.ppermute(w_ax, AXES, cores)
    w_parts = (w_a, w_ac, w_ax, w_axc, w_b, w_bc)
    operands = (rows, peer, near, far, w_up, *w_parts, b_up[None], w_conv, b_conv[None])
    places = ("vmem",) * 4 + ("any",) * 7 + ("hbm",) * 3
    return run(paired_kernel, places, operands, sizes)


def gathered(inputs, w_up, b_up, w_conv, b_conv, sizes):
    spaces, chs = lax.axis_size("space"), lax.axis_size("ch")
    c = lax.axis_index("ch")
    w_all = lax.all_gather(w_up[16:48], "ch", axis=1, tiled=True)
    rows = lax.all_gather(inputs[:, 0], "ch", axis=0, tiled=True).transpose(1, 0, 2)
    forward = [(i, i + 1) for i in range(spaces - 1)]
    backward = [(j, i) for i, j in forward]
    low = lax.ppermute(rows[-1:], "space", forward)
    high = lax.ppermute(rows[:1], "space", backward)
    rows = jnp.concatenate([low, rows, high], axis=0)
    share = inputs.shape[2] // chs
    rows = lax.dynamic_slice_in_dim(rows, c * share, share + 2, 0)
    operands = (rows, w_all, b_up[None], w_conv, b_conv[None])
    return run(gathered_kernel, ("vmem", "any", "hbm", "hbm", "hbm"), operands, sizes)


def local(inputs, w_up, b_up, w_conv, b_conv):
    chs = lax.axis_size("ch")
    sizes = (w_up.shape[2], w_conv.shape[1], 2 * inputs.shape[2] // chs, inputs.shape[3])
    plan = paired if chs == 2 and lax.axis_size("space") % 4 == 0 else gathered
    return plan(inputs, w_up, b_up, w_conv, b_conv, sizes)


def solution(mesh):
    return jax.shard_map(
        local,
        mesh=mesh,
        in_specs=(P("ch", None, "space", None), P(None, "ch", None), P(), P(), P()),
        out_specs=P(None, None, ("space", "ch"), None),
        check_vma=False,
    )
```

```python
import functools

import jax
import jax.numpy as jnp
from jax import lax
from jax.experimental import pallas as pl
from jax.experimental.pallas import tpu as pltpu
from jax.sharding import PartitionSpec as P

AXES = ("space", "ch")
PHASES = (((1, 0), (3, -1)), ((2, 0), (0, 1)))
COLUMNS = ((3, 0, 1), (0, 1, 2))
VMEM = pl.BlockSpec(memory_space=pltpu.VMEM)
ANY = pl.BlockSpec(memory_space=pl.ANY)
LIMIT = 40 * 2**20


def column_of(bias):
    lanes = bias.shape[-1]
    return jnp.transpose(jnp.broadcast_to(bias, (lanes, lanes)))


def shifted(value, step):
    cols = value.shape[1]
    place = lax.broadcasted_iota(jnp.int32, value.shape, 1)
    edge = 0 if step == 1 else cols - 1
    return jnp.where(place == edge, 0.0, pltpu.roll(value, step % cols, 1))


def upsample(x_ref, tap_of, bias, u_ref, first, last):
    held, cols = u_ref.shape[1], u_ref.shape[3]
    for row_phase in (0, 1):
        for col_phase in (0, 1):
            taps = []
            for row_tap, row_shift in PHASES[row_phase]:
                for col_tap, col_shift in PHASES[col_phase]:
                    slot = row_shift + 1 - row_phase
                    taps.append((row_tap * 4 + col_tap, slot, col_shift % 3))
            kernel = jnp.concatenate([tap_of(tap) for tap, _, _ in taps], axis=1)
            for start in range(0, held // 2, 2):
                places = range(start, min(start + 2, held // 2))
                cells = jnp.concatenate(
                    [
                        jnp.concatenate([x_ref[copy, slot + place] for place in places], axis=1)
                        for _, slot, copy in taps
                    ],
                    axis=0,
                )
                summed = jnp.dot(kernel, cells, preferred_element_type=jnp.float32)
                for number, place in enumerate(places):
                    row = 2 * place + 1 - row_phase
                    value = summed[:, number * cols : (number + 1) * cols] + bias
                    value = jnp.where(value > 0, value, 0.2 * value)
                    if row == 0:
                        value = jnp.where(first, 0.0, value)
                    if row == held - 1:
                        value = jnp.where(last, 0.0, value)
                    u_ref[col_phase, row] = value.astype(jnp.bfloat16)
                    moved = shifted(value, -1 if col_phase == 0 else 1)
                    u_ref[2 + col_phase, row] = moved.astype(jnp.bfloat16)


def convolve(kernel, u_ref, start, col_phase):
    cells = jnp.concatenate(
        [
            jnp.concatenate([u_ref[copy, start + row_tap], u_ref[copy, start + row_tap + 1]], 1)
            for row_tap in range(3)
            for copy in COLUMNS[col_phase]
        ],
        axis=0,
    )
    return jnp.dot(kernel, cells, preferred_element_type=jnp.float32)


def split_kernels(w_conv_ref, halves_ref):
    cout = w_conv_ref.shape[1]
    part = cout // 2
    low = lax.broadcasted_iota(jnp.int32, (cout, cout), 1) < part
    for row_tap in range(3):
        for col_tap in range(3):
            taps = [w_conv_ref[a * 9 + row_tap * 3 + col_tap].astype(jnp.float32) for a in range(3)]
            turned = [pltpu.roll(tap, part, 1) for tap in taps]
            columns = pl.ds((row_tap * 3 + col_tap) * cout, cout)
            for plane in (0, 1):
                near, far = 1 - plane, 2 - plane
                rows = pl.ds(plane * cout, cout)
                halves_ref[0, rows, columns] = jnp.where(low, taps[near], turned[far]).astype(jnp.bfloat16)
                halves_ref[1, rows, columns] = jnp.where(low, turned[near], taps[far]).astype(jnp.bfloat16)


def bias_of(bias_ref, column_ref, half):
    column_ref[...] = column_of(bias_ref[...])
    part = column_ref.shape[0] // 2
    bias = column_ref[pl.ds(pl.multiple_of(half * part, part), part)]
    return jnp.concatenate([bias, bias], axis=0)


def ends(s, c):
    first = (s == 0) & (c == 0)
    last = (s == lax.axis_size("space") - 1) & (c == lax.axis_size("ch") - 1)
    return first, last


def store_row(x_ref, slot, offset, value):
    where = pl.ds(pl.multiple_of(offset, 16), value.shape[0])
    x_ref[0, slot, where] = value.astype(jnp.bfloat16)
    x_ref[1, slot, where] = shifted(value, -1).astype(jnp.bfloat16)
    x_ref[2, slot, where] = shifted(value, 1).astype(jnp.bfloat16)


def own_part(half, first, last, w_half_ref, b_up_ref, w_conv_ref, x_ref, sum_ref, other_ref, halves_ref, column_ref, u_ref):
    planes = (w_half_ref.shape[0] - 32) // 2
    split_kernels(w_conv_ref, halves_ref)
    other_ref[...] = halves_ref[1 - half]

    def tap_of(tap):
        return jnp.concatenate([w_half_ref[planes + tap], w_half_ref[planes + 16 + tap]], axis=0)

    upsample(x_ref, tap_of, bias_of(b_up_ref, column_ref, half), u_ref, first, last)
    kernel = halves_ref[half]
    cols = u_ref.shape[3]
    for start in range(0, u_ref.shape[1] - 2, 2):
        for col_phase in (0, 1):
            sum_ref[col_phase, :, start * cols : (start + 2) * cols] = convolve(kernel, u_ref, start, col_phase)


def paired_first(own_ref, peer_ref, halo_ref, w_half_ref, b_up_ref, w_conv_ref, x_ref, sum_ref, other_ref, *scratch):
    *rest, wide_ref = scratch
    s, c = lax.axis_index("space"), lax.axis_index("ch")
    chans, rows, cols = own_ref.shape
    share = rows // 2 + 1
    for number, source in enumerate((own_ref, peer_ref)):
        wide_ref[number] = source[...].astype(jnp.float32).reshape(chans * rows, cols)
    for number in (0, 1):
        offset = (c if number == 0 else 1 - c) * chans
        for place in range(share):
            value = wide_ref[number, pl.ds(place + c * (rows - share), chans, stride=rows), :]
            store_row(x_ref, place + 1 - c, offset, value)
        store_row(x_ref, c * share, offset, halo_ref[number].astype(jnp.float32))
    own_part(c, *ends(s, c), w_half_ref, b_up_ref, w_conv_ref, x_ref, sum_ref, other_ref, *rest)


def gathered_first(rows_ref, w_half_ref, b_up_ref, w_conv_ref, x_ref, sum_ref, other_ref, *scratch):
    s, c = lax.axis_index("space"), lax.axis_index("ch")
    for slot in range(rows_ref.shape[0]):
        store_row(x_ref, slot, 0, rows_ref[slot].astype(jnp.float32))
    own_part(0, *ends(s, c), w_half_ref, b_up_ref, w_conv_ref, x_ref, sum_ref, other_ref, *scratch)


def second(paired, count, *refs):
    parts, refs = refs[:count], refs[count:]
    x_ref, sum_ref, other_ref, b_up_ref, b_conv_ref, out_ref, w_ref, column_ref, u_ref, total_ref, sems = refs
    s, c = lax.axis_index("space"), lax.axis_index("ch")
    half = 1 - c if paired else 1
    copies = []
    if paired:
        me, core = lax.rem(s, 4), lax.rem(s, 2)
        x = me // 2
        taps = [4 * (2 * i + j) for i in (x, 1 - x) for j in (core, 1 - core)] + [8 * core, 8 - 8 * core]
        for number, part_ref in enumerate(parts):
            place = w_ref.at[number // 4, pl.ds(taps[number], part_ref.shape[0])]
            copies.append(pltpu.make_async_copy(part_ref, place, sems.at[number]))
    else:
        for plane in (0, 1):
            source = parts[0].at[pl.ds(16 * plane, 16)]
            copies.append(pltpu.make_async_copy(source, w_ref.at[plane], sems.at[plane]))
    for copy in copies:
        copy.start()
    cout, _, rows, _ = out_ref.shape
    cols = x_ref.shape[3]
    source = lax.broadcasted_iota(jnp.int32, (2 * cols, 2 * cols), 0)
    target = lax.broadcasted_iota(jnp.int32, (2 * cols, 2 * cols), 1)
    wanted = jnp.where(source < cols, 2 * source, 2 * (source - cols) + 1)
    interleave = jnp.where(wanted == target, 1.0, 0.0).astype(jnp.bfloat16)
    bias = bias_of(b_up_ref, column_ref, half)
    for copy in copies:
        copy.wait()

    def tap_of(tap):
        return jnp.concatenate([w_ref[0, tap], w_ref[1, tap]], axis=0)

    upsample(x_ref, tap_of, bias, u_ref, *ends(s, c))
    kernel = other_ref[...]
    bias = column_of(b_conv_ref[...])
    bias = jnp.concatenate([bias, bias], axis=0)
    for start in range(0, rows, 2):
        halves = [
            convolve(kernel, u_ref, start, col_phase) + sum_ref[col_phase, :, start * cols : (start + 2) * cols]
            for col_phase in (0, 1)
        ]
        for number in (0, 1):
            pair = [
                (half[:, number * cols : (number + 1) * cols] + bias).astype(jnp.bfloat16) for half in halves
            ]
            mixed = jnp.dot(jnp.concatenate(pair, axis=1), interleave, preferred_element_type=jnp.float32)
            for side in (0, 1):
                total_ref[side, pl.ds(start + number, 2 * cout, stride=rows), :] = mixed[
                    :, side * cols : (side + 1) * cols
                ]
    for plane in (0, 1):
        for side in (0, 1):
            block = total_ref[side, pl.ds(plane * cout * rows, cout * rows), :]
            out_ref[:, plane, :, side * cols : (side + 1) * cols] = block.reshape(cout, rows, cols).astype(
                jnp.bfloat16
            )


def cost(sizes, read):
    cin, cout, rows, cols = sizes
    flops = 2 * cout * 4 * cin * 2 * cols * (rows + 2) + 2 * 2 * cout * 9 * cout * 2 * cols * rows
    return pl.CostEstimate(flops=flops, bytes_accessed=read, transcendentals=0)


def call_first(body, operands, wide, sizes):
    cin, cout, rows, cols = sizes
    return pl.pallas_call(
        body,
        out_shape=(
            jax.ShapeDtypeStruct((3, rows // 2 + 2, cin, cols), jnp.bfloat16),
            jax.ShapeDtypeStruct((2, 2 * cout, rows * cols), jnp.float32),
            jax.ShapeDtypeStruct((2 * cout, 9 * cout), jnp.bfloat16),
        ),
        in_specs=[VMEM] * len(operands),
        out_specs=(VMEM,) * 3,
        scratch_shapes=[
            pltpu.VMEM((2, 2 * cout, 9 * cout), jnp.bfloat16),
            pltpu.VMEM((cout, cout), jnp.float32),
            pltpu.VMEM((4, rows + 2, cout, cols), jnp.bfloat16),
        ]
        + wide,
        cost_estimate=cost(sizes, 8 * 2**20),
        compiler_params=pltpu.CompilerParams(vmem_limit_bytes=LIMIT),
    )(*operands)


def call_second(paired, parts, results, biases, sizes):
    cin, cout, rows, cols = sizes
    return pl.pallas_call(
        functools.partial(second, paired, len(parts)),
        out_shape=jax.ShapeDtypeStruct((cout, 2, rows, 2 * cols), jnp.bfloat16),
        in_specs=[ANY] * len(parts) + [VMEM] * 5,
        out_specs=VMEM,
        scratch_shapes=[
            pltpu.VMEM((2, 16, cout // 2, cin), jnp.bfloat16),
            pltpu.VMEM((cout, cout), jnp.float32),
            pltpu.VMEM((4, rows + 2, cout, cols), jnp.bfloat16),
            pltpu.VMEM((2, 2 * cout * rows, cols), jnp.float32),
            pltpu.SemaphoreType.DMA((6,)),
        ],
        cost_estimate=cost(sizes, 8 * 2**20),
        compiler_params=pltpu.CompilerParams(vmem_limit_bytes=LIMIT),
    )(*parts, *results, *biases)


def paired(inputs, w_up, b_up, w_conv, b_conv, sizes):
    spaces = lax.axis_size("space")
    s, c = lax.axis_index("space"), lax.axis_index("ch")
    chans, _, held, cols = inputs.shape

    def at(space, ch):
        return space * 2 + ch

    across = [(at(i, j), at(i, 1 - j)) for i in range(spaces) for j in (0, 1)]
    cores = [(at(i, j), at(i ^ 1, j)) for i in range(spaces) for j in (0, 1)]
    pairs = [(at(i, j), at(i ^ 2, j)) for i in range(spaces) for j in (0, 1)]
    chain = [(at(i - 1, 0), at(i, 0)) for i in range(1, spaces)]
    chain += [(at(i + 1, 1), at(i, 1)) for i in range(spaces - 1)]

    peer = lax.ppermute(inputs, AXES, across)
    w_a = lax.dynamic_slice_in_dim(w_up, 16 + 4 * lax.rem(s, 4), 4, 0)
    w_b = lax.dynamic_slice_in_dim(w_up, 32 + 8 * lax.rem(s, 2), 8, 0)
    w_a, w_b = lax.optimization_barrier((w_a, w_b))
    w_a = lax.ppermute(w_a, AXES, across)
    w_b = lax.ppermute(w_b, AXES, across)

    own, peer = inputs.reshape(chans, held, cols), peer.reshape(chans, held, cols)
    edges = [lax.dynamic_slice_in_dim(rows, (1 - c) * (held - 1), 1, 1)[:, 0] for rows in (own, peer)]
    halo = lax.ppermute(jnp.stack(edges), AXES, chain)
    w_a, halo = lax.optimization_barrier((w_a, halo))
    w_ax = lax.ppermute(w_a, AXES, pairs)
    w_ac = lax.ppermute(w_a, AXES, cores)
    biases = (b_up[None], b_conv[None])
    wide = [pltpu.VMEM((2, chans * held, cols), jnp.float32)]
    results = call_first(paired_first, (own, peer, halo, w_up, biases[0], w_conv), wide, sizes)
    w_b, w_ax, w_ac, *results = lax.optimization_barrier((w_b, w_ax, w_ac, *results))
    w_bc = lax.ppermute(w_b, AXES, cores)
    w_axc = lax.ppermute(w_ax, AXES, cores)
    return call_second(True, (w_a, w_ac, w_ax, w_axc, w_b, w_bc), results, biases, sizes)


def gathered(inputs, w_up, b_up, w_conv, b_conv, sizes):
    spaces, chs = lax.axis_size("space"), lax.axis_size("ch")
    c = lax.axis_index("ch")
    w_all = lax.all_gather(w_up[16:48], "ch", axis=1, tiled=True)
    part = w_all.shape[1] // 2
    rows = lax.all_gather(inputs[:, 0], "ch", axis=0, tiled=True).transpose(1, 0, 2)
    forward = [(i, i + 1) for i in range(spaces - 1)]
    backward = [(j, i) for i, j in forward]
    low = lax.ppermute(rows[-1:], "space", forward)
    high = lax.ppermute(rows[:1], "space", backward)
    rows = jnp.concatenate([low, rows, high], axis=0)
    share = inputs.shape[2] // chs
    rows = lax.dynamic_slice_in_dim(rows, c * share, share + 2, 0)
    biases = (b_up[None], b_conv[None])
    results = call_first(gathered_first, (rows, w_all[:, :part], biases[0], w_conv), [], sizes)
    return call_second(False, (w_all[:, part:],), results, biases, sizes)


def local(inputs, w_up, b_up, w_conv, b_conv):
    chs = lax.axis_size("ch")
    sizes = (w_up.shape[2], w_conv.shape[1], 2 * inputs.shape[2] // chs, inputs.shape[3])
    plan = paired if chs == 2 and lax.axis_size("space") % 4 == 0 else gathered
    return plan(inputs, w_up, b_up, w_conv, b_conv, sizes)


def solution(mesh):
    return jax.shard_map(
        local,
        mesh=mesh,
        in_specs=(P("ch", None, "space", None), P(None, "ch", None), P(), P(), P()),
        out_specs=P(None, None, ("space", "ch"), None),
        check_vma=False,
    )
```

```python
import functools

import jax
import jax.numpy as jnp
from jax import lax
from jax.experimental import pallas as pl
from jax.experimental.pallas import tpu as pltpu
from jax.sharding import PartitionSpec as P

AXES = ("space", "ch")
PHASES = (((1, 0), (3, -1)), ((2, 0), (0, 1)))
COLUMNS = ((3, 0, 1), (0, 1, 2))
VMEM = pl.BlockSpec(memory_space=pltpu.VMEM)
ANY = pl.BlockSpec(memory_space=pl.ANY)
LIMIT = 40 * 2**20


def column_of(bias):
    lanes = bias.shape[-1]
    return jnp.transpose(jnp.broadcast_to(bias, (lanes, lanes)))


def shifted(value, step):
    cols = value.shape[1]
    place = lax.broadcasted_iota(jnp.int32, value.shape, 1)
    edge = 0 if step == 1 else cols - 1
    return jnp.where(place == edge, 0.0, pltpu.roll(value, step % cols, 1))


def upsample(x_ref, tap_of, bias, u_ref, first, last):
    held, cols = u_ref.shape[1], u_ref.shape[3]
    for row_phase in (0, 1):
        for col_phase in (0, 1):
            taps = []
            for row_tap, row_shift in PHASES[row_phase]:
                for col_tap, col_shift in PHASES[col_phase]:
                    slot = row_shift + 1 - row_phase
                    taps.append((row_tap * 4 + col_tap, slot, col_shift % 3))
            kernel = jnp.concatenate([tap_of(tap) for tap, _, _ in taps], axis=1)
            for start in range(0, held // 2, 2):
                places = range(start, min(start + 2, held // 2))
                cells = jnp.concatenate(
                    [
                        jnp.concatenate([x_ref[copy, slot + place] for place in places], axis=1)
                        for _, slot, copy in taps
                    ],
                    axis=0,
                )
                summed = jnp.dot(kernel, cells, preferred_element_type=jnp.float32)
                for number, place in enumerate(places):
                    row = 2 * place + 1 - row_phase
                    value = summed[:, number * cols : (number + 1) * cols] + bias
                    value = jnp.maximum(value, 0.2 * value)
                    if row == 0:
                        value = jnp.where(first, 0.0, value)
                    if row == held - 1:
                        value = jnp.where(last, 0.0, value)
                    u_ref[col_phase, row] = value.astype(jnp.bfloat16)
                    moved = shifted(value, -1 if col_phase == 0 else 1)
                    u_ref[2 + col_phase, row] = moved.astype(jnp.bfloat16)


def convolve(kernel, u_ref, start, col_phase):
    cells = jnp.concatenate(
        [
            jnp.concatenate([u_ref[copy, start + row_tap], u_ref[copy, start + row_tap + 1]], 1)
            for row_tap in range(3)
            for copy in COLUMNS[col_phase]
        ],
        axis=0,
    )
    return jnp.dot(kernel, cells, preferred_element_type=jnp.float32)


def split_kernels(w_conv_ref, halves_ref):
    cout = w_conv_ref.shape[1]
    part = cout // 2
    low = lax.broadcasted_iota(jnp.int32, (cout, cout), 1) < part
    for row_tap in range(3):
        for col_tap in range(3):
            taps = [w_conv_ref[a * 9 + row_tap * 3 + col_tap].astype(jnp.float32) for a in range(3)]
            turned = [pltpu.roll(tap, part, 1) for tap in taps]
            columns = pl.ds((row_tap * 3 + col_tap) * cout, cout)
            for plane in (0, 1):
                near, far = 1 - plane, 2 - plane
                rows = pl.ds(plane * cout, cout)
                halves_ref[0, rows, columns] = jnp.where(low, taps[near], turned[far]).astype(jnp.bfloat16)
                halves_ref[1, rows, columns] = jnp.where(low, turned[near], taps[far]).astype(jnp.bfloat16)


def bias_of(bias_ref, column_ref, blocks):
    column_ref[...] = column_of(bias_ref[...])
    return jnp.concatenate([column_ref[pl.ds(pl.multiple_of(at, 16), size)] for at, size in blocks], axis=0)


def ends(s, c):
    first = (s == 0) & (c == 0)
    last = (s == lax.axis_size("space") - 1) & (c == lax.axis_size("ch") - 1)
    return first, last


def store_row(x_ref, slot, offset, value):
    where = pl.ds(pl.multiple_of(offset, 16), value.shape[0])
    x_ref[0, slot, where] = value.astype(jnp.bfloat16)
    x_ref[1, slot, where] = shifted(value, -1).astype(jnp.bfloat16)
    x_ref[2, slot, where] = shifted(value, 1).astype(jnp.bfloat16)


def arrival(x_core, part):
    if x_core is None:
        return [[(0, part)], [(0, part)]]
    quarter, half = part // 4, part // 2
    return [
        [((x_core ^ number) * quarter, quarter) for number in range(4)],
        [((lax.rem(x_core, 2) ^ number) * half, half) for number in (0, 1)],
    ]


def arrange(x_core, part):
    source = lax.broadcasted_iota(jnp.int32, (2 * part, 2 * part), 0)
    target = lax.broadcasted_iota(jnp.int32, (2 * part, 2 * part), 1)
    wanted = jnp.zeros_like(target)
    for plane, blocks in enumerate(arrival(x_core, part)):
        place = plane * part
        for first, size in blocks:
            inside = (target >= place) & (target < place + size)
            wanted = jnp.where(inside, target - place + plane * part + first, wanted)
            place += size
    return jnp.where(source == wanted, 1.0, 0.0).astype(jnp.bfloat16)


def own_part(half, x_core, refs, results, scratch):
    w_half_ref, b_up_ref, w_conv_ref = refs
    x_ref, sum_ref, other_ref = results
    halves_ref, column_ref, u_ref, w_ref, v_ref, sems = scratch
    s, c = lax.axis_index("space"), lax.axis_index("ch")
    skipped = (w_half_ref.shape[0] - 32) // 2
    copies = [
        pltpu.make_async_copy(w_conv_ref, v_ref, sems.at[0]),
        pltpu.make_async_copy(w_half_ref.at[pl.ds(skipped, 32)], w_ref, sems.at[1]),
    ]
    for copy in copies:
        copy.start()
    yield
    cout, part, cols = w_conv_ref.shape[1], w_half_ref.shape[1], u_ref.shape[3]

    def tap_of(tap):
        return jnp.concatenate([w_ref[tap], w_ref[16 + tap]], axis=0)

    copies[1].wait()
    bias = bias_of(b_up_ref, column_ref, [(half * part, part)] * 2)
    upsample(x_ref, tap_of, bias, u_ref, *ends(s, c))
    copies[0].wait()
    split_kernels(v_ref, halves_ref)
    matrix = arrange(x_core, part)
    for number in range(9):
        columns = pl.ds(number * cout, cout)
        moved = jnp.dot(halves_ref[1 - half, :, columns], matrix, preferred_element_type=jnp.float32)
        other_ref[:, columns] = moved.astype(jnp.bfloat16)
    kernel = halves_ref[half]
    for start in range(0, u_ref.shape[1] - 2, 2):
        for col_phase in (0, 1):
            sum_ref[col_phase, :, start * cols : (start + 2) * cols] = convolve(kernel, u_ref, start, col_phase)


def paired_first(own_ref, peer_ref, near_ref, far_ref, *refs):
    refs, results, scratch = refs[:3], refs[3:6], refs[6:]
    *scratch, wide_ref, raw_ref, raw_sem = scratch
    x_ref = results[0]
    copy = pltpu.make_async_copy(own_ref, raw_ref, raw_sem)
    copy.start()
    s, c = lax.axis_index("space"), lax.axis_index("ch")
    steps = own_part(c, lax.rem(s, 4), refs, results, scratch)
    next(steps)
    chans, rows, cols = own_ref.shape
    share = rows // 2 + 1
    for number, (source, halo_ref) in enumerate(((peer_ref, far_ref), (raw_ref, near_ref))):
        if number == 1:
            copy.wait()
        wide_ref[number] = source[...].astype(jnp.float32).reshape(chans * rows, cols)
        offset = (1 - c if number == 0 else c) * chans
        for place in range(share):
            value = wide_ref[number, pl.ds(place + c * (rows - share), chans, stride=rows), :]
            store_row(x_ref, place + 1 - c, offset, value)
        store_row(x_ref, c * share, offset, halo_ref[...].astype(jnp.float32))
    for _ in steps:
        pass


def gathered_first(rows_ref, *refs):
    refs, results, scratch = refs[:3], refs[3:6], refs[6:]
    steps = own_part(0, None, refs, results, scratch)
    next(steps)
    for slot in range(rows_ref.shape[0]):
        store_row(results[0], slot, 0, rows_ref[slot].astype(jnp.float32))
    for _ in steps:
        pass


def second(paired, count, *refs):
    parts, refs = refs[:count], refs[count:]
    x_ref, sum_ref, other_ref, b_up_ref, b_conv_ref, out_ref, column_ref, u_ref, total_ref, made_ref, sems = refs
    s, c = lax.axis_index("space"), lax.axis_index("ch")
    cout, _, rows, _ = out_ref.shape
    part = cout // 2
    half, x_core = (1 - c, lax.rem(s, 4)) if paired else (1, None)
    cols = x_ref.shape[3]

    def tap_of(tap):
        return jnp.concatenate([part_ref[tap] for part_ref in parts], axis=0)

    blocks = [(half * part + at, size) for plane in arrival(x_core, part) for at, size in plane]
    bias = bias_of(b_up_ref, column_ref, blocks)
    upsample(x_ref, tap_of, bias, u_ref, *ends(s, c))
    source = lax.broadcasted_iota(jnp.int32, (2 * cols, 2 * cols), 0)
    target = lax.broadcasted_iota(jnp.int32, (2 * cols, 2 * cols), 1)
    wanted = jnp.where(source < cols, 2 * source, 2 * (source - cols) + 1)
    interleave = jnp.where(wanted == target, 1.0, 0.0).astype(jnp.bfloat16)
    kernel = other_ref[...]
    bias = column_of(b_conv_ref[...])
    bias = jnp.concatenate([bias, bias], axis=0)
    for start in range(0, rows, 2):
        halves = [
            convolve(kernel, u_ref, start, col_phase) + sum_ref[col_phase, :, start * cols : (start + 2) * cols]
            for col_phase in (0, 1)
        ]
        for number in (0, 1):
            pair = [
                (half[:, number * cols : (number + 1) * cols] + bias).astype(jnp.bfloat16) for half in halves
            ]
            mixed = jnp.dot(jnp.concatenate(pair, axis=1), interleave, preferred_element_type=jnp.float32)
            for side in (0, 1):
                total_ref[side, pl.ds(start + number, 2 * cout, stride=rows), :] = mixed[
                    :, side * cols : (side + 1) * cols
                ]
    copies = []
    for plane in (0, 1):
        for side in (0, 1):
            number = 2 * plane + side
            block = total_ref[side, pl.ds(plane * cout * rows, cout * rows), :]
            made_ref[number] = block.reshape(cout, rows, cols).astype(jnp.bfloat16)
            place = out_ref.at[:, plane, :, pl.ds(side * cols, cols)]
            copies.append(pltpu.make_async_copy(made_ref.at[number], place, sems.at[number]))
            copies[-1].start()
    for copy in copies:
        copy.wait()


def pieces(own_ref, w_up_ref, near_ref, far_ref, w_a_ref, w_b_ref, wide_ref, raw_ref, sems):
    s, c = lax.axis_index("space"), lax.axis_index("ch")
    raw = pltpu.make_async_copy(own_ref, raw_ref, sems.at[2])
    raw.start()
    firsts = [block[0] for plane in arrival(lax.rem(s, 4), w_up_ref.shape[1]) for block in plane[:1]]
    copies = []
    for plane, piece_ref in enumerate((w_a_ref, w_b_ref)):
        channels = pl.ds(pl.multiple_of(firsts[plane], 16), piece_ref.shape[1])
        source = w_up_ref.at[pl.ds(16 + 16 * plane, 16), channels]
        copies.append(pltpu.make_async_copy(source, piece_ref, sems.at[plane]))
        copies[-1].start()
    chans, rows, cols = own_ref.shape
    raw.wait()
    wide_ref[...] = raw_ref[...].astype(jnp.float32).reshape(chans * rows, cols)
    inner, outer = (1 - c) * (rows - 1), c * (rows - 1)
    near_ref[...] = wide_ref[pl.ds(inner, chans, stride=rows), :].astype(jnp.bfloat16)
    far_ref[...] = wide_ref[pl.ds(outer, chans, stride=rows), :].astype(jnp.bfloat16)
    for copy in copies:
        copy.wait()


def call_pieces(own, w_up):
    chans, rows, cols = own.shape
    part, cin = w_up.shape[1:]
    return pl.pallas_call(
        pieces,
        out_shape=(
            jax.ShapeDtypeStruct((chans, cols), jnp.bfloat16),
            jax.ShapeDtypeStruct((chans, cols), jnp.bfloat16),
            jax.ShapeDtypeStruct((16, part // 4, cin), jnp.bfloat16),
            jax.ShapeDtypeStruct((16, part // 2, cin), jnp.bfloat16),
        ),
        in_specs=[ANY, ANY],
        out_specs=(VMEM,) * 4,
        scratch_shapes=[
            pltpu.VMEM((chans * rows, cols), jnp.float32),
            pltpu.VMEM((chans, rows, cols), jnp.bfloat16),
            pltpu.SemaphoreType.DMA((3,)),
        ],
        compiler_params=pltpu.CompilerParams(vmem_limit_bytes=LIMIT),
    )(in_hbm(own), in_hbm(w_up))


def in_hbm(operand):
    return pltpu.with_memory_space_constraint(operand, pltpu.HBM)


def cost(sizes):
    cin, cout, rows, cols = sizes
    flops = 2 * cout * 4 * cin * 2 * cols * (rows + 2) + 2 * 2 * cout * 9 * cout * 2 * cols * rows
    return pl.CostEstimate(flops=flops, bytes_accessed=8 * 2**20, transcendentals=0)


def call_first(body, rows_in, spaces, weights, extra, sizes):
    cin, cout, rows, cols = sizes
    w_half, b_up, w_conv = weights
    return pl.pallas_call(
        body,
        out_shape=(
            jax.ShapeDtypeStruct((3, rows // 2 + 2, cin, cols), jnp.bfloat16),
            jax.ShapeDtypeStruct((2, 2 * cout, rows * cols), jnp.float32),
            jax.ShapeDtypeStruct((2 * cout, 9 * cout), jnp.bfloat16),
        ),
        in_specs=[*spaces, ANY, VMEM, ANY],
        out_specs=(VMEM,) * 3,
        scratch_shapes=[
            pltpu.VMEM((2, 2 * cout, 9 * cout), jnp.bfloat16),
            pltpu.VMEM((cout, cout), jnp.float32),
            pltpu.VMEM((4, rows + 2, cout, cols), jnp.bfloat16),
            pltpu.VMEM((32, cout // 2, cin), jnp.bfloat16),
            pltpu.VMEM((27, cout, cout), jnp.bfloat16),
            pltpu.SemaphoreType.DMA((2,)),
        ]
        + extra,
        cost_estimate=cost(sizes),
        compiler_params=pltpu.CompilerParams(vmem_limit_bytes=LIMIT),
    )(*rows_in, in_hbm(w_half), b_up, in_hbm(w_conv))


def call_second(paired, parts, results, biases, sizes):
    cin, cout, rows, cols = sizes
    return pl.pallas_call(
        functools.partial(second, paired, len(parts)),
        out_shape=jax.ShapeDtypeStruct((cout, 2, rows, 2 * cols), jnp.bfloat16),
        in_specs=[VMEM] * (len(parts) + 5),
        out_specs=ANY,
        scratch_shapes=[
            pltpu.VMEM((cout, cout), jnp.float32),
            pltpu.VMEM((4, rows + 2, cout, cols), jnp.bfloat16),
            pltpu.VMEM((2, 2 * cout * rows, cols), jnp.float32),
            pltpu.VMEM((4, cout, rows, cols), jnp.bfloat16),
            pltpu.SemaphoreType.DMA((4,)),
        ],
        cost_estimate=cost(sizes),
        compiler_params=pltpu.CompilerParams(vmem_limit_bytes=LIMIT),
    )(*parts, *results, *biases)


def paired(inputs, w_up, b_up, w_conv, b_conv, sizes):
    spaces = lax.axis_size("space")
    s, c = lax.axis_index("space"), lax.axis_index("ch")
    chans, _, held, cols = inputs.shape

    def at(space, ch):
        return space * 2 + ch

    across = [(at(i, j), at(i, 1 - j)) for i in range(spaces) for j in (0, 1)]
    cores = [(at(i, j), at(i ^ 1, j)) for i in range(spaces) for j in (0, 1)]
    pairs = [(at(i, j), at(i ^ 2, j)) for i in range(spaces) for j in (0, 1)]
    chain = [(at(i - 1, 0), at(i, 0)) for i in range(1, spaces)]
    chain += [(at(i + 1, 1), at(i, 1)) for i in range(spaces - 1)]

    outer = [(t, t + 1) for t in range(1, 2 * spaces - 1, 2)]
    outer += [(j, i) for i, j in outer]

    peer = lax.ppermute(inputs, AXES, across).reshape(chans, held, cols)
    own = inputs.reshape(chans, held, cols)
    near, far, w_a, w_b = call_pieces(own, w_up)
    w_a = lax.ppermute(w_a, AXES, across)
    w_b = lax.ppermute(w_b, AXES, across)
    near = lax.ppermute(near, AXES, chain)
    far = lax.ppermute(far, AXES, outer)
    w_ax = lax.ppermute(w_a, AXES, pairs)
    w_ac = lax.ppermute(w_a, AXES, cores)
    biases = (b_up[None], b_conv[None])
    extra = [
        pltpu.VMEM((2, chans * held, cols), jnp.float32),
        pltpu.VMEM((chans, held, cols), jnp.bfloat16),
        pltpu.SemaphoreType.DMA,
    ]
    rows_in = (in_hbm(own), peer, near, far)
    weights = (w_up, biases[0], w_conv)
    results = call_first(paired_first, rows_in, (ANY, VMEM, VMEM, VMEM), weights, extra, sizes)
    w_b, w_ax, w_ac, *results = lax.optimization_barrier((w_b, w_ax, w_ac, *results))
    w_bc = lax.ppermute(w_b, AXES, cores)
    w_axc = lax.ppermute(w_ax, AXES, cores)
    return call_second(True, (w_a, w_ac, w_ax, w_axc, w_b, w_bc), results, biases, sizes)


def gathered(inputs, w_up, b_up, w_conv, b_conv, sizes):
    spaces, chs = lax.axis_size("space"), lax.axis_size("ch")
    c = lax.axis_index("ch")
    w_all = lax.all_gather(w_up[16:48], "ch", axis=1, tiled=True)
    part = w_all.shape[1] // 2
    rows = lax.all_gather(inputs[:, 0], "ch", axis=0, tiled=True).transpose(1, 0, 2)
    forward = [(i, i + 1) for i in range(spaces - 1)]
    backward = [(j, i) for i, j in forward]
    low = lax.ppermute(rows[-1:], "space", forward)
    high = lax.ppermute(rows[:1], "space", backward)
    rows = jnp.concatenate([low, rows, high], axis=0)
    share = inputs.shape[2] // chs
    rows = lax.dynamic_slice_in_dim(rows, c * share, share + 2, 0)
    biases = (b_up[None], b_conv[None])
    weights = (w_all[:, :part], biases[0], w_conv)
    results = call_first(gathered_first, (rows,), (VMEM,), weights, [], sizes)
    return call_second(False, (w_all[:16, part:], w_all[16:, part:]), results, biases, sizes)


def local(inputs, w_up, b_up, w_conv, b_conv):
    chs = lax.axis_size("ch")
    sizes = (w_up.shape[2], w_conv.shape[1], 2 * inputs.shape[2] // chs, inputs.shape[3])
    plan = paired if chs == 2 and lax.axis_size("space") % 4 == 0 else gathered
    return plan(inputs, w_up, b_up, w_conv, b_conv, sizes)


def solution(mesh):
    return jax.shard_map(
        local,
        mesh=mesh,
        in_specs=(P("ch", None, "space", None), P(None, "ch", None), P(), P(), P()),
        out_specs=P(None, None, ("space", "ch"), None),
        check_vma=False,
    )
```

```python
import functools

import jax
import jax.numpy as jnp
from jax import lax
from jax.experimental import pallas as pl
from jax.experimental.pallas import tpu as pltpu
from jax.sharding import PartitionSpec as P

AXES = ("space", "ch")
PHASES = (((1, 0), (3, -1)), ((2, 0), (0, 1)))
COLUMNS = ((3, 0, 1), (0, 1, 2))
VMEM = pl.BlockSpec(memory_space=pltpu.VMEM)
ANY = pl.BlockSpec(memory_space=pl.ANY)
LIMIT = 40 * 2**20


def column_of(bias):
    lanes = bias.shape[-1]
    return jnp.transpose(jnp.broadcast_to(bias, (lanes, lanes)))


def shifted(value, step):
    cols = value.shape[1]
    place = lax.broadcasted_iota(jnp.int32, value.shape, 1)
    edge = 0 if step == 1 else cols - 1
    return jnp.where(place == edge, 0.0, pltpu.roll(value, step % cols, 1))


def upsample(x_ref, tap_of, bias, u_ref, first, last):
    held, cols = u_ref.shape[1], u_ref.shape[3]
    for row_phase in (0, 1):
        for col_phase in (0, 1):
            taps = []
            for row_tap, row_shift in PHASES[row_phase]:
                for col_tap, col_shift in PHASES[col_phase]:
                    slot = row_shift + 1 - row_phase
                    taps.append((row_tap * 4 + col_tap, slot, col_shift % 3))
            kernel = jnp.concatenate([tap_of(tap) for tap, _, _ in taps], axis=1)
            for start in range(0, held // 2, 2):
                places = range(start, min(start + 2, held // 2))
                cells = jnp.concatenate(
                    [
                        jnp.concatenate([x_ref[copy, slot + place] for place in places], axis=1)
                        for _, slot, copy in taps
                    ],
                    axis=0,
                )
                summed = jnp.dot(kernel, cells, preferred_element_type=jnp.float32)
                for number, place in enumerate(places):
                    row = 2 * place + 1 - row_phase
                    value = summed[:, number * cols : (number + 1) * cols] + bias
                    value = jnp.maximum(value, 0.2 * value)
                    if row == 0:
                        value = jnp.where(first, 0.0, value)
                    if row == held - 1:
                        value = jnp.where(last, 0.0, value)
                    u_ref[col_phase, row] = value.astype(jnp.bfloat16)
                    moved = shifted(value, -1 if col_phase == 0 else 1)
                    u_ref[2 + col_phase, row] = moved.astype(jnp.bfloat16)


def convolve(kernel, u_ref, start, col_phase):
    cells = jnp.concatenate(
        [
            jnp.concatenate([u_ref[copy, start + row_tap], u_ref[copy, start + row_tap + 1]], 1)
            for row_tap in range(3)
            for copy in COLUMNS[col_phase]
        ],
        axis=0,
    )
    return jnp.dot(kernel, cells, preferred_element_type=jnp.float32)


def split_kernels(w_conv_ref, halves_ref):
    cout = w_conv_ref.shape[1]
    part = cout // 2
    low = lax.broadcasted_iota(jnp.int32, (cout, cout), 1) < part
    for row_tap in range(3):
        for col_tap in range(3):
            taps = [w_conv_ref[a * 9 + row_tap * 3 + col_tap].astype(jnp.float32) for a in range(3)]
            turned = [pltpu.roll(tap, part, 1) for tap in taps]
            columns = pl.ds((row_tap * 3 + col_tap) * cout, cout)
            for plane in (0, 1):
                near, far = 1 - plane, 2 - plane
                rows = pl.ds(plane * cout, cout)
                halves_ref[0, rows, columns] = jnp.where(low, taps[near], turned[far]).astype(jnp.bfloat16)
                halves_ref[1, rows, columns] = jnp.where(low, turned[near], taps[far]).astype(jnp.bfloat16)


def bias_of(bias_ref, column_ref, blocks):
    column_ref[...] = column_of(bias_ref[...])
    return jnp.concatenate([column_ref[pl.ds(pl.multiple_of(at, 16), size)] for at, size in blocks], axis=0)


def ends(s, c):
    first = (s == 0) & (c == 0)
    last = (s == lax.axis_size("space") - 1) & (c == lax.axis_size("ch") - 1)
    return first, last


def store_row(x_ref, slot, offset, value):
    where = pl.ds(pl.multiple_of(offset, 16), value.shape[0])
    x_ref[0, slot, where] = value.astype(jnp.bfloat16)
    x_ref[1, slot, where] = shifted(value, -1).astype(jnp.bfloat16)
    x_ref[2, slot, where] = shifted(value, 1).astype(jnp.bfloat16)


def arrival(x_core, part):
    if x_core is None:
        return [[(0, part)], [(0, part)]]
    quarter, half = part // 4, part // 2
    return [
        [((x_core ^ number) * quarter, quarter) for number in range(4)],
        [((lax.rem(x_core, 2) ^ number) * half, half) for number in (0, 1)],
    ]


def arrange(x_core, part):
    source = lax.broadcasted_iota(jnp.int32, (2 * part, 2 * part), 0)
    target = lax.broadcasted_iota(jnp.int32, (2 * part, 2 * part), 1)
    wanted = jnp.zeros_like(target)
    for plane, blocks in enumerate(arrival(x_core, part)):
        place = plane * part
        for first, size in blocks:
            inside = (target >= place) & (target < place + size)
            wanted = jnp.where(inside, target - place + plane * part + first, wanted)
            place += size
    return jnp.where(source == wanted, 1.0, 0.0).astype(jnp.bfloat16)


def own_part(half, refs, results, scratch):
    w_half_ref, kernel_ref, b_up_ref = refs
    x_ref, sum_ref = results
    column_ref, u_ref = scratch
    s, c = lax.axis_index("space"), lax.axis_index("ch")
    part, cols = w_half_ref.shape[1], u_ref.shape[3]

    def tap_of(tap):
        return jnp.concatenate([w_half_ref[tap], w_half_ref[16 + tap]], axis=0)

    bias = bias_of(b_up_ref, column_ref, [(half * part, part)] * 2)
    upsample(x_ref, tap_of, bias, u_ref, *ends(s, c))
    kernel = kernel_ref[...]
    for start in range(0, u_ref.shape[1] - 2, 2):
        for col_phase in (0, 1):
            sum_ref[col_phase, :, start * cols : (start + 2) * cols] = convolve(kernel, u_ref, start, col_phase)


def store_rows(x_ref, wide_ref, offset):
    c = lax.axis_index("ch")
    share = x_ref.shape[1] - 1
    chans = x_ref.shape[2] // 2
    rows = wide_ref.shape[0] // chans
    for place in range(share):
        value = wide_ref[pl.ds(place + c * (rows - share), chans, stride=rows), :]
        store_row(x_ref, place + 1 - c, offset, value)


def prepare(paired, own_ref, w_half_ref, w_conv_ref, x_ref, w_ref, kernel_ref, other_ref, *scratch):
    halves_ref, v_ref, wide_ref, raw_ref, sems = scratch
    s, c = lax.axis_index("space"), lax.axis_index("ch")
    skipped = (w_half_ref.shape[0] - 32) // 2
    copies = [
        pltpu.make_async_copy(w_conv_ref, v_ref, sems.at[0]),
        pltpu.make_async_copy(own_ref, raw_ref, sems.at[1]),
        pltpu.make_async_copy(w_half_ref.at[pl.ds(skipped, 32)], w_ref, sems.at[2]),
    ]
    for copy in copies:
        copy.start()
    cout = w_conv_ref.shape[1]
    half, x_core = (c, lax.rem(s, 4)) if paired else (0, None)
    copies[0].wait()
    split_kernels(v_ref, halves_ref)
    kernel_ref[...] = halves_ref[half]
    matrix = arrange(x_core, cout // 2)
    for number in range(9):
        columns = pl.ds(number * cout, cout)
        moved = jnp.dot(halves_ref[1 - half, :, columns], matrix, preferred_element_type=jnp.float32)
        other_ref[:, columns] = moved.astype(jnp.bfloat16)
    copies[1].wait()
    if paired:
        chans, rows, cols = own_ref.shape
        wide_ref[...] = raw_ref[...].astype(jnp.float32).reshape(chans * rows, cols)
        store_rows(x_ref, wide_ref, c * chans)
    else:
        for slot in range(own_ref.shape[0]):
            store_row(x_ref, slot, 0, raw_ref[slot].astype(jnp.float32))
    copies[2].wait()


def paired_first(peer_ref, near_ref, far_ref, started_ref, *refs):
    refs, results, scratch = refs[:3], refs[3:5], refs[5:]
    *scratch, wide_ref = scratch
    x_ref = results[0]
    c = lax.axis_index("ch")
    chans, rows, cols = peer_ref.shape
    wide_ref[...] = peer_ref[...].astype(jnp.float32).reshape(chans * rows, cols)
    store_rows(x_ref, wide_ref, (1 - c) * chans)
    slot = c * (x_ref.shape[1] - 1)
    store_row(x_ref, slot, c * chans, near_ref[...].astype(jnp.float32))
    store_row(x_ref, slot, (1 - c) * chans, far_ref[...].astype(jnp.float32))
    own_part(c, refs, results, scratch)


def gathered_first(started_ref, *refs):
    own_part(0, refs[:3], refs[3:5], refs[5:])


def second(paired, count, *refs):
    parts, refs = refs[:count], refs[count:]
    x_ref, sum_ref, other_ref, b_up_ref, b_conv_ref, out_ref, column_ref, u_ref, total_ref, made_ref, sems = refs
    s, c = lax.axis_index("space"), lax.axis_index("ch")
    cout, _, rows, _ = out_ref.shape
    part = cout // 2
    half, x_core = (1 - c, lax.rem(s, 4)) if paired else (1, None)
    cols = x_ref.shape[3]

    def tap_of(tap):
        return jnp.concatenate([part_ref[tap] for part_ref in parts], axis=0)

    blocks = [(half * part + at, size) for plane in arrival(x_core, part) for at, size in plane]
    bias = bias_of(b_up_ref, column_ref, blocks)
    upsample(x_ref, tap_of, bias, u_ref, *ends(s, c))
    source = lax.broadcasted_iota(jnp.int32, (2 * cols, 2 * cols), 0)
    target = lax.broadcasted_iota(jnp.int32, (2 * cols, 2 * cols), 1)
    wanted = jnp.where(source < cols, 2 * source, 2 * (source - cols) + 1)
    interleave = jnp.where(wanted == target, 1.0, 0.0).astype(jnp.bfloat16)
    kernel = other_ref[...]
    bias = column_of(b_conv_ref[...])
    bias = jnp.concatenate([bias, bias], axis=0)
    for start in range(0, rows, 2):
        halves = [
            convolve(kernel, u_ref, start, col_phase) + sum_ref[col_phase, :, start * cols : (start + 2) * cols]
            for col_phase in (0, 1)
        ]
        for number in (0, 1):
            pair = [
                (half[:, number * cols : (number + 1) * cols] + bias).astype(jnp.bfloat16) for half in halves
            ]
            mixed = jnp.dot(jnp.concatenate(pair, axis=1), interleave, preferred_element_type=jnp.float32)
            for side in (0, 1):
                total_ref[side, pl.ds(start + number, 2 * cout, stride=rows), :] = mixed[
                    :, side * cols : (side + 1) * cols
                ]
    copies = []
    for plane in (0, 1):
        for side in (0, 1):
            number = 2 * plane + side
            block = total_ref[side, pl.ds(plane * cout * rows, cout * rows), :]
            made_ref[number] = block.reshape(cout, rows, cols).astype(jnp.bfloat16)
            place = out_ref.at[:, plane, :, pl.ds(side * cols, cols)]
            copies.append(pltpu.make_async_copy(made_ref.at[number], place, sems.at[number]))
            copies[-1].start()
    for copy in copies:
        copy.wait()


def pieces(own_ref, w_up_ref, near_ref, far_ref, w_a_ref, w_b_ref, wide_ref, raw_ref, sems):
    s, c = lax.axis_index("space"), lax.axis_index("ch")
    raw = pltpu.make_async_copy(own_ref, raw_ref, sems.at[2])
    raw.start()
    firsts = [block[0] for plane in arrival(lax.rem(s, 4), w_up_ref.shape[1]) for block in plane[:1]]
    copies = []
    for plane, piece_ref in enumerate((w_a_ref, w_b_ref)):
        channels = pl.ds(pl.multiple_of(firsts[plane], 16), piece_ref.shape[1])
        source = w_up_ref.at[pl.ds(16 + 16 * plane, 16), channels]
        copies.append(pltpu.make_async_copy(source, piece_ref, sems.at[plane]))
        copies[-1].start()
    chans, rows, cols = own_ref.shape
    raw.wait()
    wide_ref[...] = raw_ref[...].astype(jnp.float32).reshape(chans * rows, cols)
    inner, outer = (1 - c) * (rows - 1), c * (rows - 1)
    near_ref[...] = wide_ref[pl.ds(inner, chans, stride=rows), :].astype(jnp.bfloat16)
    far_ref[...] = wide_ref[pl.ds(outer, chans, stride=rows), :].astype(jnp.bfloat16)
    for copy in copies:
        copy.wait()


def call_pieces(own, w_up):
    chans, rows, cols = own.shape
    part, cin = w_up.shape[1:]
    return pl.pallas_call(
        pieces,
        out_shape=(
            jax.ShapeDtypeStruct((chans, cols), jnp.bfloat16),
            jax.ShapeDtypeStruct((chans, cols), jnp.bfloat16),
            jax.ShapeDtypeStruct((16, part // 4, cin), jnp.bfloat16),
            jax.ShapeDtypeStruct((16, part // 2, cin), jnp.bfloat16),
        ),
        in_specs=[ANY, ANY],
        out_specs=(VMEM,) * 4,
        scratch_shapes=[
            pltpu.VMEM((chans * rows, cols), jnp.float32),
            pltpu.VMEM((chans, rows, cols), jnp.bfloat16),
            pltpu.SemaphoreType.DMA((3,)),
        ],
        compiler_params=pltpu.CompilerParams(vmem_limit_bytes=LIMIT),
    )(in_hbm(own), in_hbm(w_up))


def in_hbm(operand):
    return pltpu.with_memory_space_constraint(operand, pltpu.HBM)


def cost(sizes):
    cin, cout, rows, cols = sizes
    flops = 2 * cout * 4 * cin * 2 * cols * (rows + 2) + 2 * 2 * cout * 9 * cout * 2 * cols * rows
    return pl.CostEstimate(flops=flops, bytes_accessed=8 * 2**20, transcendentals=0)


def call_prepare(paired, own, w_half, w_conv, sizes):
    cin, cout, rows, cols = sizes
    wide = own.shape[0] * own.shape[1] if paired else 8
    return pl.pallas_call(
        functools.partial(prepare, paired),
        out_shape=(
            jax.ShapeDtypeStruct((3, rows // 2 + 2, cin, cols), jnp.bfloat16),
            jax.ShapeDtypeStruct((32, cout // 2, cin), jnp.bfloat16),
            jax.ShapeDtypeStruct((2 * cout, 9 * cout), jnp.bfloat16),
            jax.ShapeDtypeStruct((2 * cout, 9 * cout), jnp.bfloat16),
        ),
        in_specs=[ANY] * 3,
        out_specs=(VMEM,) * 4,
        scratch_shapes=[
            pltpu.VMEM((2, 2 * cout, 9 * cout), jnp.bfloat16),
            pltpu.VMEM((27, cout, cout), jnp.bfloat16),
            pltpu.VMEM((wide, cols), jnp.float32),
            pltpu.VMEM(own.shape, jnp.bfloat16),
            pltpu.SemaphoreType.DMA((3,)),
        ],
        cost_estimate=pl.CostEstimate(flops=2 * 18 * 256 * cout * cout, bytes_accessed=8 * 2**20, transcendentals=0),
        compiler_params=pltpu.CompilerParams(vmem_limit_bytes=LIMIT),
    )(in_hbm(own), in_hbm(w_half), in_hbm(w_conv))


def call_first(body, rows_in, prepared, b_up, extra, sizes):
    cin, cout, rows, cols = sizes
    started, w_half, kernel = prepared
    return pl.pallas_call(
        body,
        out_shape=(
            jax.ShapeDtypeStruct(started.shape, jnp.bfloat16),
            jax.ShapeDtypeStruct((2, 2 * cout, rows * cols), jnp.float32),
        ),
        in_specs=[VMEM] * (len(rows_in) + 4),
        out_specs=(VMEM,) * 2,
        scratch_shapes=[
            pltpu.VMEM((cout, cout), jnp.float32),
            pltpu.VMEM((4, rows + 2, cout, cols), jnp.bfloat16),
        ]
        + extra,
        input_output_aliases={len(rows_in): 0},
        cost_estimate=cost(sizes),
        compiler_params=pltpu.CompilerParams(vmem_limit_bytes=LIMIT),
    )(*rows_in, started, w_half, kernel, b_up)


def call_second(paired, parts, results, biases, sizes):
    cin, cout, rows, cols = sizes
    return pl.pallas_call(
        functools.partial(second, paired, len(parts)),
        out_shape=jax.ShapeDtypeStruct((cout, 2, rows, 2 * cols), jnp.bfloat16),
        in_specs=[VMEM] * (len(parts) + 5),
        out_specs=ANY,
        scratch_shapes=[
            pltpu.VMEM((cout, cout), jnp.float32),
            pltpu.VMEM((4, rows + 2, cout, cols), jnp.bfloat16),
            pltpu.VMEM((2, 2 * cout * rows, cols), jnp.float32),
            pltpu.VMEM((4, cout, rows, cols), jnp.bfloat16),
            pltpu.SemaphoreType.DMA((4,)),
        ],
        cost_estimate=cost(sizes),
        compiler_params=pltpu.CompilerParams(vmem_limit_bytes=LIMIT),
    )(*parts, *results, *biases)


def paired(inputs, w_up, b_up, w_conv, b_conv, sizes):
    spaces = lax.axis_size("space")
    s, c = lax.axis_index("space"), lax.axis_index("ch")
    chans, _, held, cols = inputs.shape

    def at(space, ch):
        return space * 2 + ch

    across = [(at(i, j), at(i, 1 - j)) for i in range(spaces) for j in (0, 1)]
    cores = [(at(i, j), at(i ^ 1, j)) for i in range(spaces) for j in (0, 1)]
    pairs = [(at(i, j), at(i ^ 2, j)) for i in range(spaces) for j in (0, 1)]
    chain = [(at(i - 1, 0), at(i, 0)) for i in range(1, spaces)]
    chain += [(at(i + 1, 1), at(i, 1)) for i in range(spaces - 1)]

    outer = [(t, t + 1) for t in range(1, 2 * spaces - 1, 2)]
    outer += [(j, i) for i, j in outer]

    peer = lax.ppermute(inputs, AXES, across).reshape(chans, held, cols)
    own = inputs.reshape(chans, held, cols)
    near, far, w_a, w_b = call_pieces(own, w_up)
    near, far, w_conv = lax.optimization_barrier((near, far, w_conv))
    far = lax.ppermute(far, AXES, outer)
    near = lax.ppermute(near, AXES, chain)
    x, w_half, kernel, other = call_prepare(True, own, w_up, w_conv, sizes)
    near, far, w_a, w_b, kernel = lax.optimization_barrier((near, far, w_a, w_b, kernel))
    w_a = lax.ppermute(w_a, AXES, across)
    w_b = lax.ppermute(w_b, AXES, across)
    w_ax = lax.ppermute(w_a, AXES, pairs)
    w_ac = lax.ppermute(w_a, AXES, cores)
    biases = (b_up[None], b_conv[None])
    extra = [pltpu.VMEM((chans * held, cols), jnp.float32)]
    x, total = call_first(paired_first, (peer, near, far), (x, w_half, kernel), biases[0], extra, sizes)
    results = (x, total, other)
    w_b, w_ax, w_ac, *results = lax.optimization_barrier((w_b, w_ax, w_ac, *results))
    w_bc = lax.ppermute(w_b, AXES, cores)
    w_axc = lax.ppermute(w_ax, AXES, cores)
    return call_second(True, (w_a, w_ac, w_ax, w_axc, w_b, w_bc), results, biases, sizes)


def gathered(inputs, w_up, b_up, w_conv, b_conv, sizes):
    spaces, chs = lax.axis_size("space"), lax.axis_size("ch")
    c = lax.axis_index("ch")
    w_all = lax.all_gather(w_up[16:48], "ch", axis=1, tiled=True)
    part = w_all.shape[1] // 2
    rows = lax.all_gather(inputs[:, 0], "ch", axis=0, tiled=True).transpose(1, 0, 2)
    forward = [(i, i + 1) for i in range(spaces - 1)]
    backward = [(j, i) for i, j in forward]
    low = lax.ppermute(rows[-1:], "space", forward)
    high = lax.ppermute(rows[:1], "space", backward)
    rows = jnp.concatenate([low, rows, high], axis=0)
    share = inputs.shape[2] // chs
    rows = lax.dynamic_slice_in_dim(rows, c * share, share + 2, 0)
    biases = (b_up[None], b_conv[None])
    *prepared, other = call_prepare(False, rows, w_all[:, :part], w_conv, sizes)
    results = (*call_first(gathered_first, (), prepared, biases[0], [], sizes), other)
    return call_second(False, (w_all[:16, part:], w_all[16:, part:]), results, biases, sizes)


def local(inputs, w_up, b_up, w_conv, b_conv):
    chs = lax.axis_size("ch")
    sizes = (w_up.shape[2], w_conv.shape[1], 2 * inputs.shape[2] // chs, inputs.shape[3])
    plan = paired if chs == 2 and lax.axis_size("space") % 4 == 0 else gathered
    return plan(inputs, w_up, b_up, w_conv, b_conv, sizes)


def solution(mesh):
    return jax.shard_map(
        local,
        mesh=mesh,
        in_specs=(P("ch", None, "space", None), P(None, "ch", None), P(), P(), P()),
        out_specs=P(None, None, ("space", "ch"), None),
        check_vma=False,
    )
```

```python
import functools

import jax
import jax.numpy as jnp
from jax import lax
from jax.experimental import pallas as pl
from jax.experimental.pallas import tpu as pltpu
from jax.sharding import PartitionSpec as P

AXES = ("space", "ch")
PHASES = (((1, 0), (3, -1)), ((2, 0), (0, 1)))
COLUMNS = ((3, 0, 1), (0, 1, 2))
VMEM = pl.BlockSpec(memory_space=pltpu.VMEM)
ANY = pl.BlockSpec(memory_space=pl.ANY)
LIMIT = 40 * 2**20


def column_of(bias):
    lanes = bias.shape[-1]
    return jnp.transpose(jnp.broadcast_to(bias, (lanes, lanes)))


def shifted(value, step):
    cols = value.shape[1]
    place = lax.broadcasted_iota(jnp.int32, value.shape, 1)
    edge = 0 if step == 1 else cols - 1
    return jnp.where(place == edge, 0.0, pltpu.roll(value, step % cols, 1))


def upsample(x_ref, tap_of, bias, u_ref, first, last):
    held, cols = u_ref.shape[1], u_ref.shape[3]
    for row_phase in (0, 1):
        for col_phase in (0, 1):
            taps = []
            for row_tap, row_shift in PHASES[row_phase]:
                for col_tap, col_shift in PHASES[col_phase]:
                    slot = row_shift + 1 - row_phase
                    taps.append((row_tap * 4 + col_tap, slot, col_shift % 3))
            kernel = jnp.concatenate([tap_of(tap) for tap, _, _ in taps], axis=1)
            for start in range(0, held // 2, 2):
                places = range(start, min(start + 2, held // 2))
                cells = jnp.concatenate(
                    [
                        jnp.concatenate([x_ref[copy, slot + place] for place in places], axis=1)
                        for _, slot, copy in taps
                    ],
                    axis=0,
                )
                summed = jnp.dot(kernel, cells, preferred_element_type=jnp.float32)
                for number, place in enumerate(places):
                    row = 2 * place + 1 - row_phase
                    value = summed[:, number * cols : (number + 1) * cols] + bias
                    value = jnp.maximum(value, 0.2 * value)
                    if row == 0:
                        value = jnp.where(first, 0.0, value)
                    if row == held - 1:
                        value = jnp.where(last, 0.0, value)
                    u_ref[col_phase, row] = value.astype(jnp.bfloat16)
                    moved = shifted(value, -1 if col_phase == 0 else 1)
                    u_ref[2 + col_phase, row] = moved.astype(jnp.bfloat16)


def convolve(kernel, u_ref, start, col_phase):
    cells = jnp.concatenate(
        [
            jnp.concatenate([u_ref[copy, start + row_tap], u_ref[copy, start + row_tap + 1]], 1)
            for row_tap in range(3)
            for copy in COLUMNS[col_phase]
        ],
        axis=0,
    )
    return jnp.dot(kernel, cells, preferred_element_type=jnp.float32)


def split_kernels(w_conv_ref, halves_ref):
    cout = w_conv_ref.shape[1]
    part = cout // 2
    low = lax.broadcasted_iota(jnp.int32, (cout, cout), 1) < part
    for row_tap in range(3):
        for col_tap in range(3):
            taps = [w_conv_ref[a * 9 + row_tap * 3 + col_tap].astype(jnp.float32) for a in range(3)]
            turned = [pltpu.roll(tap, part, 1) for tap in taps]
            columns = pl.ds((row_tap * 3 + col_tap) * cout, cout)
            for plane in (0, 1):
                near, far = 1 - plane, 2 - plane
                rows = pl.ds(plane * cout, cout)
                halves_ref[0, rows, columns] = jnp.where(low, taps[near], turned[far]).astype(jnp.bfloat16)
                halves_ref[1, rows, columns] = jnp.where(low, turned[near], taps[far]).astype(jnp.bfloat16)


def bias_of(bias_ref, column_ref, blocks):
    column_ref[...] = column_of(bias_ref[...])
    return jnp.concatenate([column_ref[pl.ds(pl.multiple_of(at, 16), size)] for at, size in blocks], axis=0)


def ends(s, c):
    first = (s == 0) & (c == 0)
    last = (s == lax.axis_size("space") - 1) & (c == lax.axis_size("ch") - 1)
    return first, last


def store_row(x_ref, slot, offset, value):
    where = pl.ds(pl.multiple_of(offset, 16), value.shape[0])
    x_ref[0, slot, where] = value.astype(jnp.bfloat16)
    x_ref[1, slot, where] = shifted(value, -1).astype(jnp.bfloat16)
    x_ref[2, slot, where] = shifted(value, 1).astype(jnp.bfloat16)


def arrival(x_core, part):
    if x_core is None:
        return [[(0, part)], [(0, part)]]
    quarter, half = part // 4, part // 2
    return [
        [((x_core ^ number) * quarter, quarter) for number in range(4)],
        [((lax.rem(x_core, 2) ^ number) * half, half) for number in (0, 1)],
    ]


def arrange(x_core, part):
    source = lax.broadcasted_iota(jnp.int32, (2 * part, 2 * part), 0)
    target = lax.broadcasted_iota(jnp.int32, (2 * part, 2 * part), 1)
    wanted = jnp.zeros_like(target)
    for plane, blocks in enumerate(arrival(x_core, part)):
        place = plane * part
        for first, size in blocks:
            inside = (target >= place) & (target < place + size)
            wanted = jnp.where(inside, target - place + plane * part + first, wanted)
            place += size
    return jnp.where(source == wanted, 1.0, 0.0).astype(jnp.bfloat16)


def own_part(half, refs, results, scratch):
    w_half_ref, kernel_ref, b_up_ref = refs
    x_ref, sum_ref = results
    column_ref, u_ref = scratch
    s, c = lax.axis_index("space"), lax.axis_index("ch")
    part, cols = w_half_ref.shape[1], u_ref.shape[3]

    def tap_of(tap):
        return jnp.concatenate([w_half_ref[tap], w_half_ref[16 + tap]], axis=0)

    bias = bias_of(b_up_ref, column_ref, [(half * part, part)] * 2)
    upsample(x_ref, tap_of, bias, u_ref, *ends(s, c))
    kernel = kernel_ref[...]
    for start in range(0, u_ref.shape[1] - 2, 2):
        for col_phase in (0, 1):
            sum_ref[col_phase, :, start * cols : (start + 2) * cols] = convolve(kernel, u_ref, start, col_phase)


def prepare(paired, own_ref, w_half_ref, w_conv_ref, x_ref, w_ref, kernel_ref, other_ref, *scratch):
    halves_ref, v_ref, wide_ref, raw_ref, sems = scratch
    s, c = lax.axis_index("space"), lax.axis_index("ch")
    skipped = (w_half_ref.shape[0] - 32) // 2
    copies = [
        pltpu.make_async_copy(w_conv_ref, v_ref, sems.at[0]),
        pltpu.make_async_copy(own_ref, raw_ref, sems.at[1]),
        pltpu.make_async_copy(w_half_ref.at[pl.ds(skipped, 32)], w_ref, sems.at[2]),
    ]
    for copy in copies:
        copy.start()
    cout = w_conv_ref.shape[1]
    half, x_core = (c, lax.rem(s, 4)) if paired else (0, None)
    copies[0].wait()
    split_kernels(v_ref, halves_ref)
    kernel_ref[...] = halves_ref[half]
    matrix = arrange(x_core, cout // 2)
    for number in range(9):
        columns = pl.ds(number * cout, cout)
        moved = jnp.dot(halves_ref[1 - half, :, columns], matrix, preferred_element_type=jnp.float32)
        other_ref[:, columns] = moved.astype(jnp.bfloat16)
    copies[1].wait()
    if paired:
        chans, rows, cols = own_ref.shape
        wide_ref[...] = raw_ref[...].astype(jnp.float32).reshape(chans * rows, cols)
        share = x_ref.shape[1] - 1
        for place in range(share):
            value = wide_ref[pl.ds(place + c * (rows - share), chans, stride=rows), :]
            store_row(x_ref, place + 1 - c, c * chans, value)
    else:
        for slot in range(own_ref.shape[0]):
            store_row(x_ref, slot, 0, raw_ref[slot].astype(jnp.float32))
    copies[2].wait()


def paired_first(peer_ref, near_ref, far_ref, started_ref, *refs):
    refs, results, scratch = refs[:3], refs[3:5], refs[5:]
    x_ref = results[0]
    c = lax.axis_index("ch")
    share, chans, _ = peer_ref.shape
    for place in range(share):
        store_row(x_ref, place + 1 - c, (1 - c) * chans, peer_ref[place].astype(jnp.float32))
    slot = c * (x_ref.shape[1] - 1)
    store_row(x_ref, slot, c * chans, near_ref[...].astype(jnp.float32))
    store_row(x_ref, slot, (1 - c) * chans, far_ref[...].astype(jnp.float32))
    own_part(c, refs, results, scratch)


def gathered_first(started_ref, *refs):
    own_part(0, refs[:3], refs[3:5], refs[5:])


def second(paired, count, *refs):
    parts, refs = refs[:count], refs[count:]
    x_ref, sum_ref, other_ref, b_up_ref, b_conv_ref, out_ref, column_ref, u_ref, total_ref, made_ref, sems = refs
    s, c = lax.axis_index("space"), lax.axis_index("ch")
    cout, _, rows, _ = out_ref.shape
    part = cout // 2
    half, x_core = (1 - c, lax.rem(s, 4)) if paired else (1, None)
    cols = x_ref.shape[3]

    def tap_of(tap):
        return jnp.concatenate([part_ref[tap] for part_ref in parts], axis=0)

    blocks = [(half * part + at, size) for plane in arrival(x_core, part) for at, size in plane]
    bias = bias_of(b_up_ref, column_ref, blocks)
    upsample(x_ref, tap_of, bias, u_ref, *ends(s, c))
    source = lax.broadcasted_iota(jnp.int32, (2 * cols, 2 * cols), 0)
    target = lax.broadcasted_iota(jnp.int32, (2 * cols, 2 * cols), 1)
    wanted = jnp.where(source < cols, 2 * source, 2 * (source - cols) + 1)
    interleave = jnp.where(wanted == target, 1.0, 0.0).astype(jnp.bfloat16)
    kernel = other_ref[...]
    bias = column_of(b_conv_ref[...])
    bias = jnp.concatenate([bias, bias], axis=0)
    for start in range(0, rows, 2):
        halves = [
            convolve(kernel, u_ref, start, col_phase) + sum_ref[col_phase, :, start * cols : (start + 2) * cols]
            for col_phase in (0, 1)
        ]
        for number in (0, 1):
            pair = [
                (half[:, number * cols : (number + 1) * cols] + bias).astype(jnp.bfloat16) for half in halves
            ]
            mixed = jnp.dot(jnp.concatenate(pair, axis=1), interleave, preferred_element_type=jnp.float32)
            for side in (0, 1):
                total_ref[side, pl.ds(start + number, 2 * cout, stride=rows), :] = mixed[
                    :, side * cols : (side + 1) * cols
                ]
    copies = []
    for plane in (0, 1):
        for side in (0, 1):
            number = 2 * plane + side
            block = total_ref[side, pl.ds(plane * cout * rows, cout * rows), :]
            made_ref[number] = block.reshape(cout, rows, cols).astype(jnp.bfloat16)
            place = out_ref.at[:, plane, :, pl.ds(side * cols, cols)]
            copies.append(pltpu.make_async_copy(made_ref.at[number], place, sems.at[number]))
            copies[-1].start()
    for copy in copies:
        copy.wait()


def pieces(own_ref, w_up_ref, near_ref, far_ref, peer_ref, w_a_ref, w_b_ref, wide_ref, raw_ref, sems):
    s, c = lax.axis_index("space"), lax.axis_index("ch")
    raw = pltpu.make_async_copy(own_ref, raw_ref, sems.at[2])
    raw.start()
    firsts = [block[0] for plane in arrival(lax.rem(s, 4), w_up_ref.shape[1]) for block in plane[:1]]
    copies = []
    for plane, piece_ref in enumerate((w_a_ref, w_b_ref)):
        channels = pl.ds(pl.multiple_of(firsts[plane], 16), piece_ref.shape[1])
        source = w_up_ref.at[pl.ds(16 + 16 * plane, 16), channels]
        copies.append(pltpu.make_async_copy(source, piece_ref, sems.at[plane]))
        copies[-1].start()
    chans, rows, cols = own_ref.shape
    raw.wait()
    wide_ref[...] = raw_ref[...].astype(jnp.float32).reshape(chans * rows, cols)
    inner, outer = (1 - c) * (rows - 1), c * (rows - 1)
    near_ref[...] = wide_ref[pl.ds(inner, chans, stride=rows), :].astype(jnp.bfloat16)
    far_ref[...] = wide_ref[pl.ds(outer, chans, stride=rows), :].astype(jnp.bfloat16)
    share = peer_ref.shape[0]
    for place in range(share):
        row = wide_ref[pl.ds(place + (1 - c) * (rows - share), chans, stride=rows), :]
        peer_ref[place] = row.astype(jnp.bfloat16)
    for copy in copies:
        copy.wait()


def call_pieces(own, w_up):
    chans, rows, cols = own.shape
    part, cin = w_up.shape[1:]
    return pl.pallas_call(
        pieces,
        out_shape=(
            jax.ShapeDtypeStruct((chans, cols), jnp.bfloat16),
            jax.ShapeDtypeStruct((chans, cols), jnp.bfloat16),
            jax.ShapeDtypeStruct((rows // 2 + 1, chans, cols), jnp.bfloat16),
            jax.ShapeDtypeStruct((16, part // 4, cin), jnp.bfloat16),
            jax.ShapeDtypeStruct((16, part // 2, cin), jnp.bfloat16),
        ),
        in_specs=[ANY, ANY],
        out_specs=(VMEM,) * 5,
        scratch_shapes=[
            pltpu.VMEM((chans * rows, cols), jnp.float32),
            pltpu.VMEM((chans, rows, cols), jnp.bfloat16),
            pltpu.SemaphoreType.DMA((3,)),
        ],
        compiler_params=pltpu.CompilerParams(vmem_limit_bytes=LIMIT),
    )(in_hbm(own), in_hbm(w_up))


def in_hbm(operand):
    return pltpu.with_memory_space_constraint(operand, pltpu.HBM)


def cost(sizes):
    cin, cout, rows, cols = sizes
    flops = 2 * cout * 4 * cin * 2 * cols * (rows + 2) + 2 * 2 * cout * 9 * cout * 2 * cols * rows
    return pl.CostEstimate(flops=flops, bytes_accessed=8 * 2**20, transcendentals=0)


def call_prepare(paired, own, w_half, w_conv, sizes):
    cin, cout, rows, cols = sizes
    wide = own.shape[0] * own.shape[1] if paired else 8
    return pl.pallas_call(
        functools.partial(prepare, paired),
        out_shape=(
            jax.ShapeDtypeStruct((3, rows // 2 + 2, cin, cols), jnp.bfloat16),
            jax.ShapeDtypeStruct((32, cout // 2, cin), jnp.bfloat16),
            jax.ShapeDtypeStruct((2 * cout, 9 * cout), jnp.bfloat16),
            jax.ShapeDtypeStruct((2 * cout, 9 * cout), jnp.bfloat16),
        ),
        in_specs=[ANY] * 3,
        out_specs=(VMEM,) * 4,
        scratch_shapes=[
            pltpu.VMEM((2, 2 * cout, 9 * cout), jnp.bfloat16),
            pltpu.VMEM((27, cout, cout), jnp.bfloat16),
            pltpu.VMEM((wide, cols), jnp.float32),
            pltpu.VMEM(own.shape, jnp.bfloat16),
            pltpu.SemaphoreType.DMA((3,)),
        ],
        cost_estimate=pl.CostEstimate(flops=2 * 18 * 256 * cout * cout, bytes_accessed=8 * 2**20, transcendentals=0),
        compiler_params=pltpu.CompilerParams(vmem_limit_bytes=LIMIT),
    )(in_hbm(own), in_hbm(w_half), in_hbm(w_conv))


def call_first(body, rows_in, prepared, b_up, sizes):
    cin, cout, rows, cols = sizes
    started, w_half, kernel = prepared
    return pl.pallas_call(
        body,
        out_shape=(
            jax.ShapeDtypeStruct(started.shape, jnp.bfloat16),
            jax.ShapeDtypeStruct((2, 2 * cout, rows * cols), jnp.float32),
        ),
        in_specs=[VMEM] * (len(rows_in) + 4),
        out_specs=(VMEM,) * 2,
        scratch_shapes=[
            pltpu.VMEM((cout, cout), jnp.float32),
            pltpu.VMEM((4, rows + 2, cout, cols), jnp.bfloat16),
        ],
        input_output_aliases={len(rows_in): 0},
        cost_estimate=cost(sizes),
        compiler_params=pltpu.CompilerParams(vmem_limit_bytes=LIMIT),
    )(*rows_in, started, w_half, kernel, b_up)


def call_second(paired, parts, results, biases, sizes):
    cin, cout, rows, cols = sizes
    return pl.pallas_call(
        functools.partial(second, paired, len(parts)),
        out_shape=jax.ShapeDtypeStruct((cout, 2, rows, 2 * cols), jnp.bfloat16),
        in_specs=[VMEM] * (len(parts) + 5),
        out_specs=ANY,
        scratch_shapes=[
            pltpu.VMEM((cout, cout), jnp.float32),
            pltpu.VMEM((4, rows + 2, cout, cols), jnp.bfloat16),
            pltpu.VMEM((2, 2 * cout * rows, cols), jnp.float32),
            pltpu.VMEM((4, cout, rows, cols), jnp.bfloat16),
            pltpu.SemaphoreType.DMA((4,)),
        ],
        cost_estimate=cost(sizes),
        compiler_params=pltpu.CompilerParams(vmem_limit_bytes=LIMIT),
    )(*parts, *results, *biases)


def paired(inputs, w_up, b_up, w_conv, b_conv, sizes):
    spaces = lax.axis_size("space")
    s, c = lax.axis_index("space"), lax.axis_index("ch")
    chans, _, held, cols = inputs.shape

    def at(space, ch):
        return space * 2 + ch

    across = [(at(i, j), at(i, 1 - j)) for i in range(spaces) for j in (0, 1)]
    cores = [(at(i, j), at(i ^ 1, j)) for i in range(spaces) for j in (0, 1)]
    pairs = [(at(i, j), at(i ^ 2, j)) for i in range(spaces) for j in (0, 1)]
    chain = [(at(i - 1, 0), at(i, 0)) for i in range(1, spaces)]
    chain += [(at(i + 1, 1), at(i, 1)) for i in range(spaces - 1)]

    outer = [(t, t + 1) for t in range(1, 2 * spaces - 1, 2)]
    outer += [(j, i) for i, j in outer]

    own = inputs.reshape(chans, held, cols)
    near, far, peer, w_a, w_b = call_pieces(own, w_up)
    far = lax.ppermute(far, AXES, outer)
    far, peer, w_a, w_b, near, w_conv = lax.optimization_barrier((far, peer, w_a, w_b, near, w_conv))
    peer = lax.ppermute(peer, AXES, across)
    w_a = lax.ppermute(w_a, AXES, across)
    w_b = lax.ppermute(w_b, AXES, across)
    near = lax.ppermute(near, AXES, chain)
    x, w_half, kernel, other = call_prepare(True, own, w_up, w_conv, sizes)
    w_ax = lax.ppermute(w_a, AXES, pairs)
    w_ac = lax.ppermute(w_a, AXES, cores)
    biases = (b_up[None], b_conv[None])
    x, total = call_first(paired_first, (peer, near, far), (x, w_half, kernel), biases[0], sizes)
    results = (x, total, other)
    w_b, w_ax, w_ac, *results = lax.optimization_barrier((w_b, w_ax, w_ac, *results))
    w_bc = lax.ppermute(w_b, AXES, cores)
    w_axc = lax.ppermute(w_ax, AXES, cores)
    return call_second(True, (w_a, w_ac, w_ax, w_axc, w_b, w_bc), results, biases, sizes)


def gathered(inputs, w_up, b_up, w_conv, b_conv, sizes):
    spaces, chs = lax.axis_size("space"), lax.axis_size("ch")
    c = lax.axis_index("ch")
    w_all = lax.all_gather(w_up[16:48], "ch", axis=1, tiled=True)
    part = w_all.shape[1] // 2
    rows = lax.all_gather(inputs[:, 0], "ch", axis=0, tiled=True).transpose(1, 0, 2)
    forward = [(i, i + 1) for i in range(spaces - 1)]
    backward = [(j, i) for i, j in forward]
    low = lax.ppermute(rows[-1:], "space", forward)
    high = lax.ppermute(rows[:1], "space", backward)
    rows = jnp.concatenate([low, rows, high], axis=0)
    share = inputs.shape[2] // chs
    rows = lax.dynamic_slice_in_dim(rows, c * share, share + 2, 0)
    biases = (b_up[None], b_conv[None])
    *prepared, other = call_prepare(False, rows, w_all[:, :part], w_conv, sizes)
    results = (*call_first(gathered_first, (), prepared, biases[0], sizes), other)
    return call_second(False, (w_all[:16, part:], w_all[16:, part:]), results, biases, sizes)


def local(inputs, w_up, b_up, w_conv, b_conv):
    chs = lax.axis_size("ch")
    sizes = (w_up.shape[2], w_conv.shape[1], 2 * inputs.shape[2] // chs, inputs.shape[3])
    plan = paired if chs == 2 and lax.axis_size("space") % 4 == 0 else gathered
    return plan(inputs, w_up, b_up, w_conv, b_conv, sizes)


def solution(mesh):
    return jax.shard_map(
        local,
        mesh=mesh,
        in_specs=(P("ch", None, "space", None), P(None, "ch", None), P(), P(), P()),
        out_specs=P(None, None, ("space", "ch"), None),
        check_vma=False,
    )
```

```python
import functools

import jax
import jax.numpy as jnp
from jax import lax
from jax.experimental import pallas as pl
from jax.experimental.pallas import tpu as pltpu
from jax.sharding import PartitionSpec as P

AXES = ("space", "ch")
PHASES = (((1, 0), (3, -1)), ((2, 0), (0, 1)))
COLUMNS = ((3, 0, 1), (0, 1, 2))
VMEM = pl.BlockSpec(memory_space=pltpu.VMEM)
ANY = pl.BlockSpec(memory_space=pl.ANY)
LIMIT = 40 * 2**20


def column_of(bias):
    lanes = bias.shape[-1]
    return jnp.transpose(jnp.broadcast_to(bias, (lanes, lanes)))


def shifted(value, step):
    cols = value.shape[1]
    place = lax.broadcasted_iota(jnp.int32, value.shape, 1)
    edge = 0 if step == 1 else cols - 1
    return jnp.where(place == edge, 0.0, pltpu.roll(value, step % cols, 1))


def upsample(x_ref, tap_of, bias, u_ref, first, last):
    held, cols = u_ref.shape[1], u_ref.shape[3]
    for row_phase in (0, 1):
        for col_phase in (0, 1):
            taps = []
            for row_tap, row_shift in PHASES[row_phase]:
                for col_tap, col_shift in PHASES[col_phase]:
                    slot = row_shift + 1 - row_phase
                    taps.append((row_tap * 4 + col_tap, slot, col_shift % 3))
            kernel = jnp.concatenate([tap_of(tap) for tap, _, _ in taps], axis=1)
            for start in range(0, held // 2, 2):
                places = range(start, min(start + 2, held // 2))
                cells = jnp.concatenate(
                    [
                        jnp.concatenate([x_ref[copy, slot + place] for place in places], axis=1)
                        for _, slot, copy in taps
                    ],
                    axis=0,
                )
                summed = jnp.dot(kernel, cells, preferred_element_type=jnp.float32)
                for number, place in enumerate(places):
                    row = 2 * place + 1 - row_phase
                    value = summed[:, number * cols : (number + 1) * cols] + bias
                    value = jnp.maximum(value, 0.2 * value)
                    if row == 0:
                        value = jnp.where(first, 0.0, value)
                    if row == held - 1:
                        value = jnp.where(last, 0.0, value)
                    u_ref[col_phase, row] = value.astype(jnp.bfloat16)
                    moved = shifted(value, -1 if col_phase == 0 else 1)
                    u_ref[2 + col_phase, row] = moved.astype(jnp.bfloat16)


def convolve(kernel, u_ref, start, col_phase):
    cells = jnp.concatenate(
        [
            jnp.concatenate([u_ref[copy, start + row_tap], u_ref[copy, start + row_tap + 1]], 1)
            for row_tap in range(3)
            for copy in COLUMNS[col_phase]
        ],
        axis=0,
    )
    return jnp.dot(kernel, cells, preferred_element_type=jnp.float32)


def split_kernels(w_conv_ref, halves_ref):
    cout = w_conv_ref.shape[1]
    part = cout // 2
    low = lax.broadcasted_iota(jnp.int32, (cout, cout), 1) < part
    for row_tap in range(3):
        for col_tap in range(3):
            taps = [w_conv_ref[a * 9 + row_tap * 3 + col_tap].astype(jnp.float32) for a in range(3)]
            turned = [pltpu.roll(tap, part, 1) for tap in taps]
            columns = pl.ds((row_tap * 3 + col_tap) * cout, cout)
            for plane in (0, 1):
                near, far = 1 - plane, 2 - plane
                rows = pl.ds(plane * cout, cout)
                halves_ref[0, rows, columns] = jnp.where(low, taps[near], turned[far]).astype(jnp.bfloat16)
                halves_ref[1, rows, columns] = jnp.where(low, turned[near], taps[far]).astype(jnp.bfloat16)


def bias_of(bias_ref, column_ref, blocks):
    column_ref[...] = column_of(bias_ref[...])
    return jnp.concatenate([column_ref[pl.ds(pl.multiple_of(at, 16), size)] for at, size in blocks], axis=0)


def ends(s, c):
    first = (s == 0) & (c == 0)
    last = (s == lax.axis_size("space") - 1) & (c == lax.axis_size("ch") - 1)
    return first, last


def store_row(x_ref, slot, offset, value):
    where = pl.ds(pl.multiple_of(offset, 16), value.shape[0])
    x_ref[0, slot, where] = value.astype(jnp.bfloat16)
    x_ref[1, slot, where] = shifted(value, -1).astype(jnp.bfloat16)
    x_ref[2, slot, where] = shifted(value, 1).astype(jnp.bfloat16)


def arrival(x_core, part):
    if x_core is None:
        return [[(0, part)], [(0, part)]]
    quarter, half = part // 4, part // 2
    return [
        [((x_core ^ number) * quarter, quarter) for number in range(4)],
        [((lax.rem(x_core, 2) ^ number) * half, half) for number in (0, 1)],
    ]


def arrange(x_core, part):
    source = lax.broadcasted_iota(jnp.int32, (2 * part, 2 * part), 0)
    target = lax.broadcasted_iota(jnp.int32, (2 * part, 2 * part), 1)
    wanted = jnp.zeros_like(target)
    for plane, blocks in enumerate(arrival(x_core, part)):
        place = plane * part
        for first, size in blocks:
            inside = (target >= place) & (target < place + size)
            wanted = jnp.where(inside, target - place + plane * part + first, wanted)
            place += size
    return jnp.where(source == wanted, 1.0, 0.0).astype(jnp.bfloat16)


def own_part(half, refs, results, scratch):
    w_half_ref, kernel_ref, b_up_ref = refs
    x_ref, sum_ref = results
    column_ref, u_ref = scratch
    s, c = lax.axis_index("space"), lax.axis_index("ch")
    part, cols = w_half_ref.shape[1], u_ref.shape[3]

    def tap_of(tap):
        return jnp.concatenate([w_half_ref[tap], w_half_ref[16 + tap]], axis=0)

    bias = bias_of(b_up_ref, column_ref, [(half * part, part)] * 2)
    upsample(x_ref, tap_of, bias, u_ref, *ends(s, c))
    kernel = kernel_ref[...]
    for start in range(0, u_ref.shape[1] - 2, 2):
        for col_phase in (0, 1):
            sum_ref[col_phase, :, start * cols : (start + 2) * cols] = convolve(kernel, u_ref, start, col_phase)


def prepare_rows(paired, own_ref, x_ref, wide_ref, raw_ref, sem):
    copy = pltpu.make_async_copy(own_ref, raw_ref, sem)
    copy.start()
    copy.wait()
    if paired:
        c = lax.axis_index("ch")
        chans, rows, cols = own_ref.shape
        wide_ref[...] = raw_ref[...].astype(jnp.float32).reshape(chans * rows, cols)
        share = x_ref.shape[1] - 1
        for place in range(share):
            value = wide_ref[pl.ds(place + c * (rows - share), chans, stride=rows), :]
            store_row(x_ref, place + 1 - c, c * chans, value)
    else:
        for slot in range(own_ref.shape[0]):
            store_row(x_ref, slot, 0, raw_ref[slot].astype(jnp.float32))


def prepare_kernels(paired, w_half_ref, w_conv_ref, w_ref, kernel_ref, other_ref, halves_ref, v_ref, sems):
    s, c = lax.axis_index("space"), lax.axis_index("ch")
    skipped = (w_half_ref.shape[0] - 32) // 2
    copies = [
        pltpu.make_async_copy(w_conv_ref, v_ref, sems.at[0]),
        pltpu.make_async_copy(w_half_ref.at[pl.ds(skipped, 32)], w_ref, sems.at[1]),
    ]
    for copy in copies:
        copy.start()
    cout = w_conv_ref.shape[1]
    half, x_core = (c, lax.rem(s, 4)) if paired else (0, None)
    copies[0].wait()
    split_kernels(v_ref, halves_ref)
    kernel_ref[...] = halves_ref[half]
    matrix = arrange(x_core, cout // 2)
    for number in range(9):
        columns = pl.ds(number * cout, cout)
        moved = jnp.dot(halves_ref[1 - half, :, columns], matrix, preferred_element_type=jnp.float32)
        other_ref[:, columns] = moved.astype(jnp.bfloat16)
    copies[1].wait()


def paired_first(peer_ref, near_ref, far_ref, started_ref, *refs):
    refs, results, scratch = refs[:3], refs[3:5], refs[5:]
    x_ref = results[0]
    c = lax.axis_index("ch")
    share, chans, _ = peer_ref.shape
    for place in range(share):
        store_row(x_ref, place + 1 - c, (1 - c) * chans, peer_ref[place].astype(jnp.float32))
    slot = c * (x_ref.shape[1] - 1)
    store_row(x_ref, slot, c * chans, near_ref[...].astype(jnp.float32))
    store_row(x_ref, slot, (1 - c) * chans, far_ref[...].astype(jnp.float32))
    own_part(c, refs, results, scratch)


def gathered_first(started_ref, *refs):
    own_part(0, refs[:3], refs[3:5], refs[5:])


def second(paired, count, *refs):
    parts, refs = refs[:count], refs[count:]
    x_ref, sum_ref, other_ref, b_up_ref, b_conv_ref, out_ref, column_ref, u_ref, total_ref, made_ref, sems = refs
    s, c = lax.axis_index("space"), lax.axis_index("ch")
    cout, _, rows, _ = out_ref.shape
    part = cout // 2
    half, x_core = (1 - c, lax.rem(s, 4)) if paired else (1, None)
    cols = x_ref.shape[3]

    def tap_of(tap):
        return jnp.concatenate([part_ref[tap] for part_ref in parts], axis=0)

    blocks = [(half * part + at, size) for plane in arrival(x_core, part) for at, size in plane]
    bias = bias_of(b_up_ref, column_ref, blocks)
    upsample(x_ref, tap_of, bias, u_ref, *ends(s, c))
    source = lax.broadcasted_iota(jnp.int32, (2 * cols, 2 * cols), 0)
    target = lax.broadcasted_iota(jnp.int32, (2 * cols, 2 * cols), 1)
    wanted = jnp.where(source < cols, 2 * source, 2 * (source - cols) + 1)
    interleave = jnp.where(wanted == target, 1.0, 0.0).astype(jnp.bfloat16)
    kernel = other_ref[...]
    bias = column_of(b_conv_ref[...])
    bias = jnp.concatenate([bias, bias], axis=0)
    for start in range(0, rows, 2):
        halves = [
            convolve(kernel, u_ref, start, col_phase) + sum_ref[col_phase, :, start * cols : (start + 2) * cols]
            for col_phase in (0, 1)
        ]
        for number in (0, 1):
            pair = [
                (half[:, number * cols : (number + 1) * cols] + bias).astype(jnp.bfloat16) for half in halves
            ]
            mixed = jnp.dot(jnp.concatenate(pair, axis=1), interleave, preferred_element_type=jnp.float32)
            for side in (0, 1):
                total_ref[side, pl.ds(start + number, 2 * cout, stride=rows), :] = mixed[
                    :, side * cols : (side + 1) * cols
                ]
    copies = []
    for plane in (0, 1):
        for side in (0, 1):
            number = 2 * plane + side
            block = total_ref[side, pl.ds(plane * cout * rows, cout * rows), :]
            made_ref[number] = block.reshape(cout, rows, cols).astype(jnp.bfloat16)
            place = out_ref.at[:, plane, :, pl.ds(side * cols, cols)]
            copies.append(pltpu.make_async_copy(made_ref.at[number], place, sems.at[number]))
            copies[-1].start()
    for copy in copies:
        copy.wait()


def pieces(own_ref, w_up_ref, near_ref, far_ref, peer_ref, w_a_ref, w_b_ref, wide_ref, raw_ref, sems):
    s, c = lax.axis_index("space"), lax.axis_index("ch")
    raw = pltpu.make_async_copy(own_ref, raw_ref, sems.at[2])
    raw.start()
    firsts = [block[0] for plane in arrival(lax.rem(s, 4), w_up_ref.shape[1]) for block in plane[:1]]
    copies = []
    for plane, piece_ref in enumerate((w_a_ref, w_b_ref)):
        channels = pl.ds(pl.multiple_of(firsts[plane], 16), piece_ref.shape[1])
        source = w_up_ref.at[pl.ds(16 + 16 * plane, 16), channels]
        copies.append(pltpu.make_async_copy(source, piece_ref, sems.at[plane]))
        copies[-1].start()
    chans, rows, cols = own_ref.shape
    raw.wait()
    wide_ref[...] = raw_ref[...].astype(jnp.float32).reshape(chans * rows, cols)
    inner, outer = (1 - c) * (rows - 1), c * (rows - 1)
    near_ref[...] = wide_ref[pl.ds(inner, chans, stride=rows), :].astype(jnp.bfloat16)
    far_ref[...] = wide_ref[pl.ds(outer, chans, stride=rows), :].astype(jnp.bfloat16)
    share = peer_ref.shape[0]
    for place in range(share):
        row = wide_ref[pl.ds(place + (1 - c) * (rows - share), chans, stride=rows), :]
        peer_ref[place] = row.astype(jnp.bfloat16)
    for copy in copies:
        copy.wait()


def call_pieces(own, w_up):
    chans, rows, cols = own.shape
    part, cin = w_up.shape[1:]
    return pl.pallas_call(
        pieces,
        out_shape=(
            jax.ShapeDtypeStruct((chans, cols), jnp.bfloat16),
            jax.ShapeDtypeStruct((chans, cols), jnp.bfloat16),
            jax.ShapeDtypeStruct((rows // 2 + 1, chans, cols), jnp.bfloat16),
            jax.ShapeDtypeStruct((16, part // 4, cin), jnp.bfloat16),
            jax.ShapeDtypeStruct((16, part // 2, cin), jnp.bfloat16),
        ),
        in_specs=[ANY, ANY],
        out_specs=(VMEM,) * 5,
        scratch_shapes=[
            pltpu.VMEM((chans * rows, cols), jnp.float32),
            pltpu.VMEM((chans, rows, cols), jnp.bfloat16),
            pltpu.SemaphoreType.DMA((3,)),
        ],
        compiler_params=pltpu.CompilerParams(vmem_limit_bytes=LIMIT),
    )(in_hbm(own), in_hbm(w_up))


def in_hbm(operand):
    return pltpu.with_memory_space_constraint(operand, pltpu.HBM)


def cost(sizes):
    cin, cout, rows, cols = sizes
    flops = 2 * cout * 4 * cin * 2 * cols * (rows + 2) + 2 * 2 * cout * 9 * cout * 2 * cols * rows
    return pl.CostEstimate(flops=flops, bytes_accessed=8 * 2**20, transcendentals=0)


def call_rows(paired, own, sizes):
    cin, cout, rows, cols = sizes
    wide = own.shape[0] * own.shape[1] if paired else 8
    return pl.pallas_call(
        functools.partial(prepare_rows, paired),
        out_shape=jax.ShapeDtypeStruct((3, rows // 2 + 2, cin, cols), jnp.bfloat16),
        in_specs=[ANY],
        out_specs=VMEM,
        scratch_shapes=[
            pltpu.VMEM((wide, cols), jnp.float32),
            pltpu.VMEM(own.shape, jnp.bfloat16),
            pltpu.SemaphoreType.DMA,
        ],
        cost_estimate=pl.CostEstimate(flops=2**20, bytes_accessed=2 * 2**20, transcendentals=0),
        compiler_params=pltpu.CompilerParams(vmem_limit_bytes=LIMIT),
    )(in_hbm(own))


def call_kernels(paired, w_half, w_conv, sizes):
    cin, cout, rows, cols = sizes
    return pl.pallas_call(
        functools.partial(prepare_kernels, paired),
        out_shape=(
            jax.ShapeDtypeStruct((32, cout // 2, cin), jnp.bfloat16),
            jax.ShapeDtypeStruct((2 * cout, 9 * cout), jnp.bfloat16),
            jax.ShapeDtypeStruct((2 * cout, 9 * cout), jnp.bfloat16),
        ),
        in_specs=[ANY] * 2,
        out_specs=(VMEM,) * 3,
        scratch_shapes=[
            pltpu.VMEM((2, 2 * cout, 9 * cout), jnp.bfloat16),
            pltpu.VMEM((27, cout, cout), jnp.bfloat16),
            pltpu.SemaphoreType.DMA((2,)),
        ],
        cost_estimate=pl.CostEstimate(flops=2 * 18 * 256 * cout * cout, bytes_accessed=6 * 2**20, transcendentals=0),
        compiler_params=pltpu.CompilerParams(vmem_limit_bytes=LIMIT),
    )(in_hbm(w_half), in_hbm(w_conv))


def call_first(body, rows_in, prepared, b_up, sizes):
    cin, cout, rows, cols = sizes
    started, w_half, kernel = prepared
    return pl.pallas_call(
        body,
        out_shape=(
            jax.ShapeDtypeStruct(started.shape, jnp.bfloat16),
            jax.ShapeDtypeStruct((2, 2 * cout, rows * cols), jnp.float32),
        ),
        in_specs=[VMEM] * (len(rows_in) + 4),
        out_specs=(VMEM,) * 2,
        scratch_shapes=[
            pltpu.VMEM((cout, cout), jnp.float32),
            pltpu.VMEM((4, rows + 2, cout, cols), jnp.bfloat16),
        ],
        input_output_aliases={len(rows_in): 0},
        cost_estimate=cost(sizes),
        compiler_params=pltpu.CompilerParams(vmem_limit_bytes=LIMIT),
    )(*rows_in, started, w_half, kernel, b_up)


def call_second(paired, parts, results, biases, sizes):
    cin, cout, rows, cols = sizes
    return pl.pallas_call(
        functools.partial(second, paired, len(parts)),
        out_shape=jax.ShapeDtypeStruct((cout, 2, rows, 2 * cols), jnp.bfloat16),
        in_specs=[VMEM] * (len(parts) + 5),
        out_specs=ANY,
        scratch_shapes=[
            pltpu.VMEM((cout, cout), jnp.float32),
            pltpu.VMEM((4, rows + 2, cout, cols), jnp.bfloat16),
            pltpu.VMEM((2, 2 * cout * rows, cols), jnp.float32),
            pltpu.VMEM((4, cout, rows, cols), jnp.bfloat16),
            pltpu.SemaphoreType.DMA((4,)),
        ],
        cost_estimate=cost(sizes),
        compiler_params=pltpu.CompilerParams(vmem_limit_bytes=LIMIT),
    )(*parts, *results, *biases)


def paired(inputs, w_up, b_up, w_conv, b_conv, sizes):
    spaces = lax.axis_size("space")
    s, c = lax.axis_index("space"), lax.axis_index("ch")
    chans, _, held, cols = inputs.shape

    def at(space, ch):
        return space * 2 + ch

    across = [(at(i, j), at(i, 1 - j)) for i in range(spaces) for j in (0, 1)]
    cores = [(at(i, j), at(i ^ 1, j)) for i in range(spaces) for j in (0, 1)]
    pairs = [(at(i, j), at(i ^ 2, j)) for i in range(spaces) for j in (0, 1)]
    chain = [(at(i - 1, 0), at(i, 0)) for i in range(1, spaces)]
    chain += [(at(i + 1, 1), at(i, 1)) for i in range(spaces - 1)]

    outer = [(t, t + 1) for t in range(1, 2 * spaces - 1, 2)]
    outer += [(j, i) for i, j in outer]

    own = inputs.reshape(chans, held, cols)
    near, far, peer, w_a, w_b = call_pieces(own, w_up)
    own, w_conv, peer, w_a, far, near, w_b = lax.optimization_barrier((own, w_conv, peer, w_a, far, near, w_b))
    peer = lax.ppermute(peer, AXES, across)
    w_a = lax.ppermute(w_a, AXES, across)
    far = lax.ppermute(far, AXES, outer)
    near = lax.ppermute(near, AXES, chain)
    x = call_rows(True, own, sizes)
    x, w_b, w_conv, near, far = lax.optimization_barrier((x, w_b, w_conv, near, far))
    w_b = lax.ppermute(w_b, AXES, across)
    w_half, kernel, other = call_kernels(True, w_up, w_conv, sizes)
    w_ax = lax.ppermute(w_a, AXES, pairs)
    w_ac = lax.ppermute(w_a, AXES, cores)
    biases = (b_up[None], b_conv[None])
    x, total = call_first(paired_first, (peer, near, far), (x, w_half, kernel), biases[0], sizes)
    results = (x, total, other)
    w_b, w_ax, w_ac, *results = lax.optimization_barrier((w_b, w_ax, w_ac, *results))
    w_bc = lax.ppermute(w_b, AXES, cores)
    w_axc = lax.ppermute(w_ax, AXES, cores)
    return call_second(True, (w_a, w_ac, w_ax, w_axc, w_b, w_bc), results, biases, sizes)


def gathered(inputs, w_up, b_up, w_conv, b_conv, sizes):
    spaces, chs = lax.axis_size("space"), lax.axis_size("ch")
    c = lax.axis_index("ch")
    w_all = lax.all_gather(w_up[16:48], "ch", axis=1, tiled=True)
    part = w_all.shape[1] // 2
    rows = lax.all_gather(inputs[:, 0], "ch", axis=0, tiled=True).transpose(1, 0, 2)
    forward = [(i, i + 1) for i in range(spaces - 1)]
    backward = [(j, i) for i, j in forward]
    low = lax.ppermute(rows[-1:], "space", forward)
    high = lax.ppermute(rows[:1], "space", backward)
    rows = jnp.concatenate([low, rows, high], axis=0)
    share = inputs.shape[2] // chs
    rows = lax.dynamic_slice_in_dim(rows, c * share, share + 2, 0)
    biases = (b_up[None], b_conv[None])
    *prepared, other = call_kernels(False, w_all[:, :part], w_conv, sizes)
    prepared = (call_rows(False, rows, sizes), *prepared)
    results = (*call_first(gathered_first, (), prepared, biases[0], sizes), other)
    return call_second(False, (w_all[:16, part:], w_all[16:, part:]), results, biases, sizes)


def local(inputs, w_up, b_up, w_conv, b_conv):
    chs = lax.axis_size("ch")
    sizes = (w_up.shape[2], w_conv.shape[1], 2 * inputs.shape[2] // chs, inputs.shape[3])
    plan = paired if chs == 2 and lax.axis_size("space") % 4 == 0 else gathered
    return plan(inputs, w_up, b_up, w_conv, b_conv, sizes)


def solution(mesh):
    return jax.shard_map(
        local,
        mesh=mesh,
        in_specs=(P("ch", None, "space", None), P(None, "ch", None), P(), P(), P()),
        out_specs=P(None, None, ("space", "ch"), None),
        check_vma=False,
    )
```

```python
import functools

import jax
import jax.numpy as jnp
from jax import lax
from jax.experimental import pallas as pl
from jax.experimental.pallas import tpu as pltpu
from jax.sharding import PartitionSpec as P

AXES = ("space", "ch")
PHASES = (((1, 0), (3, -1)), ((2, 0), (0, 1)))
COLUMNS = ((3, 0, 1), (0, 1, 2))
VMEM = pl.BlockSpec(memory_space=pltpu.VMEM)
ANY = pl.BlockSpec(memory_space=pl.ANY)
LIMIT = 40 * 2**20


def column_of(bias):
    lanes = bias.shape[-1]
    return jnp.transpose(jnp.broadcast_to(bias, (lanes, lanes)))


def shifted(value, step):
    cols = value.shape[1]
    place = lax.broadcasted_iota(jnp.int32, value.shape, 1)
    edge = 0 if step == 1 else cols - 1
    return jnp.where(place == edge, 0.0, pltpu.roll(value, step % cols, 1))


def upsample(cell, tap_of, bias, u_ref, first, last):
    held, cols = u_ref.shape[1], u_ref.shape[3]
    for row_phase in (0, 1):
        for col_phase in (0, 1):
            taps = []
            for row_tap, row_shift in PHASES[row_phase]:
                for col_tap, col_shift in PHASES[col_phase]:
                    slot = row_shift + 1 - row_phase
                    taps.append((row_tap * 4 + col_tap, slot, col_shift % 3))
            kernel = jnp.concatenate([tap_of(tap) for tap, _, _ in taps], axis=1)
            for start in range(0, held // 2, 2):
                places = range(start, min(start + 2, held // 2))
                cells = jnp.concatenate(
                    [
                        jnp.concatenate([cell(copy, slot + place) for place in places], axis=1)
                        for _, slot, copy in taps
                    ],
                    axis=0,
                )
                summed = jnp.dot(kernel, cells, preferred_element_type=jnp.float32)
                for number, place in enumerate(places):
                    row = 2 * place + 1 - row_phase
                    value = summed[:, number * cols : (number + 1) * cols] + bias
                    value = jnp.maximum(value, 0.2 * value)
                    if row == 0:
                        value = jnp.where(first, 0.0, value)
                    if row == held - 1:
                        value = jnp.where(last, 0.0, value)
                    u_ref[col_phase, row] = value.astype(jnp.bfloat16)
                    moved = shifted(value, -1 if col_phase == 0 else 1)
                    u_ref[2 + col_phase, row] = moved.astype(jnp.bfloat16)


def convolve(kernel, u_ref, start, col_phase):
    cells = jnp.concatenate(
        [
            jnp.concatenate([u_ref[copy, start + row_tap], u_ref[copy, start + row_tap + 1]], 1)
            for row_tap in range(3)
            for copy in COLUMNS[col_phase]
        ],
        axis=0,
    )
    return jnp.dot(kernel, cells, preferred_element_type=jnp.float32)


def split_kernels(w_conv_ref, halves_ref):
    cout = w_conv_ref.shape[1]
    part = cout // 2
    low = lax.broadcasted_iota(jnp.int32, (cout, cout), 1) < part
    for row_tap in range(3):
        for col_tap in range(3):
            taps = [w_conv_ref[a * 9 + row_tap * 3 + col_tap].astype(jnp.float32) for a in range(3)]
            turned = [pltpu.roll(tap, part, 1) for tap in taps]
            columns = pl.ds((row_tap * 3 + col_tap) * cout, cout)
            for plane in (0, 1):
                near, far = 1 - plane, 2 - plane
                rows = pl.ds(plane * cout, cout)
                halves_ref[0, rows, columns] = jnp.where(low, taps[near], turned[far]).astype(jnp.bfloat16)
                halves_ref[1, rows, columns] = jnp.where(low, turned[near], taps[far]).astype(jnp.bfloat16)


def bias_of(bias_ref, column_ref, blocks):
    column_ref[...] = column_of(bias_ref[...])
    return jnp.concatenate([column_ref[pl.ds(pl.multiple_of(at, 16), size)] for at, size in blocks], axis=0)


def ends(s, c):
    first = (s == 0) & (c == 0)
    last = (s == lax.axis_size("space") - 1) & (c == lax.axis_size("ch") - 1)
    return first, last


def store_row(x_ref, slot, offset, value):
    where = pl.ds(pl.multiple_of(offset, 16), value.shape[0])
    x_ref[0, slot, where] = value.astype(jnp.bfloat16)
    x_ref[1, slot, where] = shifted(value, -1).astype(jnp.bfloat16)
    x_ref[2, slot, where] = shifted(value, 1).astype(jnp.bfloat16)


def arrival(x, part):
    if x is None:
        return [[(0, part)], [(0, part)]]
    quarter, half = part // 4, part // 2
    return [
        [(x * half, half), ((1 - x) * half, half)],
        [(x * quarter, quarter), ((1 - x) * quarter, quarter), (half, half)],
    ]


def arrange(x, part):
    source = lax.broadcasted_iota(jnp.int32, (2 * part, 2 * part), 0)
    target = lax.broadcasted_iota(jnp.int32, (2 * part, 2 * part), 1)
    wanted = jnp.zeros_like(target)
    for plane, blocks in enumerate(arrival(x, part)):
        place = plane * part
        for first, size in blocks:
            inside = (target >= place) & (target < place + size)
            wanted = jnp.where(inside, target - place + plane * part + first, wanted)
            place += size
    return jnp.where(source == wanted, 1.0, 0.0).astype(jnp.bfloat16)


def own_part(half, refs, results, scratch):
    w_half_ref, kernel_ref, b_up_ref = refs
    x_ref, sum_ref = results
    column_ref, u_ref = scratch
    s, c = lax.axis_index("space"), lax.axis_index("ch")
    part, cols = w_half_ref.shape[1], u_ref.shape[3]

    def tap_of(tap):
        return jnp.concatenate([w_half_ref[tap], w_half_ref[16 + tap]], axis=0)

    bias = bias_of(b_up_ref, column_ref, [(half * part, part)] * 2)
    upsample(lambda copy, slot: x_ref[copy, slot], tap_of, bias, u_ref, *ends(s, c))
    kernel = kernel_ref[...]
    for start in range(0, u_ref.shape[1] - 2, 2):
        for col_phase in (0, 1):
            sum_ref[col_phase, :, start * cols : (start + 2) * cols] = convolve(kernel, u_ref, start, col_phase)


def prepare_rows(paired, own_ref, x_ref, wide_ref, raw_ref, sem):
    copy = pltpu.make_async_copy(own_ref, raw_ref, sem)
    copy.start()
    copy.wait()
    if paired:
        c = lax.axis_index("ch")
        chans, rows, cols = own_ref.shape
        wide_ref[...] = raw_ref[...].astype(jnp.float32).reshape(chans * rows, cols)
        share = x_ref.shape[1] - 1
        for place in range(share):
            value = wide_ref[pl.ds(place + c * (rows - share), chans, stride=rows), :]
            store_row(x_ref, place + 1 - c, c * chans, value)
    else:
        for slot in range(own_ref.shape[0]):
            store_row(x_ref, slot, 0, raw_ref[slot].astype(jnp.float32))


def prepare_kernels(paired, w_half_ref, w_conv_ref, w_ref, kernel_ref, other_ref, halves_ref, v_ref, sems):
    s, c = lax.axis_index("space"), lax.axis_index("ch")
    skipped = (w_half_ref.shape[0] - 32) // 2
    copies = [
        pltpu.make_async_copy(w_conv_ref, v_ref, sems.at[0]),
        pltpu.make_async_copy(w_half_ref.at[pl.ds(skipped, 32)], w_ref, sems.at[1]),
    ]
    for copy in copies:
        copy.start()
    cout = w_conv_ref.shape[1]
    half, x = (c, lax.rem(s, 4) // 2) if paired else (0, None)
    copies[0].wait()
    split_kernels(v_ref, halves_ref)
    kernel_ref[...] = halves_ref[half]
    matrix = arrange(x, cout // 2)
    for number in range(9):
        columns = pl.ds(number * cout, cout)
        moved = jnp.dot(halves_ref[1 - half, :, columns], matrix, preferred_element_type=jnp.float32)
        other_ref[:, columns] = moved.astype(jnp.bfloat16)
    copies[1].wait()


def paired_first(peer_ref, near_ref, far_ref, started_ref, *refs):
    refs, results, scratch = refs[:3], refs[3:5], refs[5:]
    x_ref = results[0]
    c = lax.axis_index("ch")
    share, chans, _ = peer_ref.shape
    for place in range(share):
        store_row(x_ref, place + 1 - c, (1 - c) * chans, peer_ref[place].astype(jnp.float32))
    slot = c * (x_ref.shape[1] - 1)
    store_row(x_ref, slot, c * chans, near_ref[...].astype(jnp.float32))
    store_row(x_ref, slot, (1 - c) * chans, far_ref[...].astype(jnp.float32))
    own_part(c, refs, results, scratch)


def gathered_first(started_ref, *refs):
    own_part(0, refs[:3], refs[3:5], refs[5:])


def second(paired, count, *refs):
    parts, refs = refs[:count], refs[count:]
    x_ref, sum_ref, other_ref, b_up_ref, b_conv_ref, out_ref, column_ref, u_ref, total_ref, made_ref, sems = refs
    s, c = lax.axis_index("space"), lax.axis_index("ch")
    cout, _, rows, _ = out_ref.shape
    part = cout // 2
    half, x = (1 - c, lax.rem(s, 4) // 2) if paired else (1, None)
    cols = x_ref.shape[3]
    if paired:
        chans = x_ref.shape[2] // 2
        core = lax.rem(s, 2)
        sides = [pl.ds(pl.multiple_of(side * chans, 16), chans) for side in (core, 1 - core)]
        big = part // 2

        def tap_of(tap):
            columns = []
            for near_ref, far_ref, rest_ref in (parts[:3], parts[3:]):
                rows = [near_ref[tap, :big], far_ref[tap, :big], near_ref[tap, big:], far_ref[tap, big:], rest_ref[tap]]
                columns.append(jnp.concatenate(rows, axis=0))
            return jnp.concatenate(columns, axis=1)

        def cell(copy, slot):
            return jnp.concatenate([x_ref[copy, slot, side] for side in sides], axis=0)
    else:

        def tap_of(tap):
            return jnp.concatenate([part_ref[tap] for part_ref in parts], axis=0)

        def cell(copy, slot):
            return x_ref[copy, slot]

    blocks = [(half * part + at, size) for plane in arrival(x, part) for at, size in plane]
    bias = bias_of(b_up_ref, column_ref, blocks)
    upsample(cell, tap_of, bias, u_ref, *ends(s, c))
    source = lax.broadcasted_iota(jnp.int32, (2 * cols, 2 * cols), 0)
    target = lax.broadcasted_iota(jnp.int32, (2 * cols, 2 * cols), 1)
    wanted = jnp.where(source < cols, 2 * source, 2 * (source - cols) + 1)
    interleave = jnp.where(wanted == target, 1.0, 0.0).astype(jnp.bfloat16)
    kernel = other_ref[...]
    bias = column_of(b_conv_ref[...])
    bias = jnp.concatenate([bias, bias], axis=0)
    for start in range(0, rows, 2):
        halves = [
            convolve(kernel, u_ref, start, col_phase) + sum_ref[col_phase, :, start * cols : (start + 2) * cols]
            for col_phase in (0, 1)
        ]
        for number in (0, 1):
            pair = [
                (half[:, number * cols : (number + 1) * cols] + bias).astype(jnp.bfloat16) for half in halves
            ]
            mixed = jnp.dot(jnp.concatenate(pair, axis=1), interleave, preferred_element_type=jnp.float32)
            for side in (0, 1):
                total_ref[side, pl.ds(start + number, 2 * cout, stride=rows), :] = mixed[
                    :, side * cols : (side + 1) * cols
                ]
    copies = []
    for plane in (0, 1):
        for side in (0, 1):
            number = 2 * plane + side
            block = total_ref[side, pl.ds(plane * cout * rows, cout * rows), :]
            made_ref[number] = block.reshape(cout, rows, cols).astype(jnp.bfloat16)
            place = out_ref.at[:, plane, :, pl.ds(side * cols, cols)]
            copies.append(pltpu.make_async_copy(made_ref.at[number], place, sems.at[number]))
            copies[-1].start()
    for copy in copies:
        copy.wait()


def pieces(own_ref, w_up_ref, near_ref, far_ref, peer_ref, w_a_ref, w_b_ref, wide_ref, raw_ref, sems):
    s, c = lax.axis_index("space"), lax.axis_index("ch")
    raw = pltpu.make_async_copy(own_ref, raw_ref, sems.at[3])
    raw.start()
    me = lax.rem(s, 4)
    part, lanes = w_up_ref.shape[1], w_a_ref.shape[2]
    side = pl.ds(pl.multiple_of(lax.rem(me, 2) * lanes, lanes), lanes)
    (first, big), = arrival(me // 2, part)[0][:1]
    (second, small), _, (third, rest) = arrival(me // 2, part)[1]
    cuts = (
        (16, first, big, w_a_ref.at[:, pl.ds(0, big)]),
        (32, second, small, w_a_ref.at[:, pl.ds(big, small)]),
        (32, third, rest, w_b_ref),
    )
    copies = []
    for number, (tap, channel, count, place) in enumerate(cuts):
        source = w_up_ref.at[pl.ds(tap, 16), pl.ds(pl.multiple_of(channel, 16), count), side]
        copies.append(pltpu.make_async_copy(source, place, sems.at[number]))
        copies[-1].start()
    chans, rows, cols = own_ref.shape
    raw.wait()
    wide_ref[...] = raw_ref[...].astype(jnp.float32).reshape(chans * rows, cols)
    inner, outer = (1 - c) * (rows - 1), c * (rows - 1)
    near_ref[...] = wide_ref[pl.ds(inner, chans, stride=rows), :].astype(jnp.bfloat16)
    far_ref[...] = wide_ref[pl.ds(outer, chans, stride=rows), :].astype(jnp.bfloat16)
    share = peer_ref.shape[0]
    for place in range(share):
        row = wide_ref[pl.ds(place + (1 - c) * (rows - share), chans, stride=rows), :]
        peer_ref[place] = row.astype(jnp.bfloat16)
    for copy in copies:
        copy.wait()


def call_pieces(own, w_up):
    chans, rows, cols = own.shape
    part, cin = w_up.shape[1:]
    return pl.pallas_call(
        pieces,
        out_shape=(
            jax.ShapeDtypeStruct((chans, cols), jnp.bfloat16),
            jax.ShapeDtypeStruct((chans, cols), jnp.bfloat16),
            jax.ShapeDtypeStruct((rows // 2 + 1, chans, cols), jnp.bfloat16),
            jax.ShapeDtypeStruct((16, 3 * part // 4, cin // 2), jnp.bfloat16),
            jax.ShapeDtypeStruct((16, part // 2, cin // 2), jnp.bfloat16),
        ),
        in_specs=[ANY, ANY],
        out_specs=(VMEM,) * 5,
        scratch_shapes=[
            pltpu.VMEM((chans * rows, cols), jnp.float32),
            pltpu.VMEM((chans, rows, cols), jnp.bfloat16),
            pltpu.SemaphoreType.DMA((4,)),
        ],
        compiler_params=pltpu.CompilerParams(vmem_limit_bytes=LIMIT),
    )(in_hbm(own), in_hbm(w_up))


def in_hbm(operand):
    return pltpu.with_memory_space_constraint(operand, pltpu.HBM)


def cost(sizes):
    cin, cout, rows, cols = sizes
    flops = 2 * cout * 4 * cin * 2 * cols * (rows + 2) + 2 * 2 * cout * 9 * cout * 2 * cols * rows
    return pl.CostEstimate(flops=flops, bytes_accessed=8 * 2**20, transcendentals=0)


def call_rows(paired, own, sizes):
    cin, cout, rows, cols = sizes
    wide = own.shape[0] * own.shape[1] if paired else 8
    return pl.pallas_call(
        functools.partial(prepare_rows, paired),
        out_shape=jax.ShapeDtypeStruct((3, rows // 2 + 2, cin, cols), jnp.bfloat16),
        in_specs=[ANY],
        out_specs=VMEM,
        scratch_shapes=[
            pltpu.VMEM((wide, cols), jnp.float32),
            pltpu.VMEM(own.shape, jnp.bfloat16),
            pltpu.SemaphoreType.DMA,
        ],
        cost_estimate=pl.CostEstimate(flops=2**20, bytes_accessed=2 * 2**20, transcendentals=0),
        compiler_params=pltpu.CompilerParams(vmem_limit_bytes=LIMIT),
    )(in_hbm(own))


def call_kernels(paired, w_half, w_conv, sizes):
    cin, cout, rows, cols = sizes
    return pl.pallas_call(
        functools.partial(prepare_kernels, paired),
        out_shape=(
            jax.ShapeDtypeStruct((32, cout // 2, cin), jnp.bfloat16),
            jax.ShapeDtypeStruct((2 * cout, 9 * cout), jnp.bfloat16),
            jax.ShapeDtypeStruct((2 * cout, 9 * cout), jnp.bfloat16),
        ),
        in_specs=[ANY] * 2,
        out_specs=(VMEM,) * 3,
        scratch_shapes=[
            pltpu.VMEM((2, 2 * cout, 9 * cout), jnp.bfloat16),
            pltpu.VMEM((27, cout, cout), jnp.bfloat16),
            pltpu.SemaphoreType.DMA((2,)),
        ],
        cost_estimate=pl.CostEstimate(flops=2 * 18 * 256 * cout * cout, bytes_accessed=6 * 2**20, transcendentals=0),
        compiler_params=pltpu.CompilerParams(vmem_limit_bytes=LIMIT),
    )(in_hbm(w_half), in_hbm(w_conv))


def call_first(body, rows_in, prepared, b_up, sizes):
    cin, cout, rows, cols = sizes
    started, w_half, kernel = prepared
    return pl.pallas_call(
        body,
        out_shape=(
            jax.ShapeDtypeStruct(started.shape, jnp.bfloat16),
            jax.ShapeDtypeStruct((2, 2 * cout, rows * cols), jnp.float32),
        ),
        in_specs=[VMEM] * (len(rows_in) + 4),
        out_specs=(VMEM,) * 2,
        scratch_shapes=[
            pltpu.VMEM((cout, cout), jnp.float32),
            pltpu.VMEM((4, rows + 2, cout, cols), jnp.bfloat16),
        ],
        input_output_aliases={len(rows_in): 0},
        cost_estimate=cost(sizes),
        compiler_params=pltpu.CompilerParams(vmem_limit_bytes=LIMIT),
    )(*rows_in, started, w_half, kernel, b_up)


def call_second(paired, parts, results, biases, sizes):
    cin, cout, rows, cols = sizes
    return pl.pallas_call(
        functools.partial(second, paired, len(parts)),
        out_shape=jax.ShapeDtypeStruct((cout, 2, rows, 2 * cols), jnp.bfloat16),
        in_specs=[VMEM] * (len(parts) + 5),
        out_specs=ANY,
        scratch_shapes=[
            pltpu.VMEM((cout, cout), jnp.float32),
            pltpu.VMEM((4, rows + 2, cout, cols), jnp.bfloat16),
            pltpu.VMEM((2, 2 * cout * rows, cols), jnp.float32),
            pltpu.VMEM((4, cout, rows, cols), jnp.bfloat16),
            pltpu.SemaphoreType.DMA((4,)),
        ],
        cost_estimate=cost(sizes),
        compiler_params=pltpu.CompilerParams(vmem_limit_bytes=LIMIT),
    )(*parts, *results, *biases)


def paired(inputs, w_up, b_up, w_conv, b_conv, sizes):
    spaces = lax.axis_size("space")
    s, c = lax.axis_index("space"), lax.axis_index("ch")
    chans, _, held, cols = inputs.shape

    def at(space, ch):
        return space * 2 + ch

    across = [(at(i, j), at(i, 1 - j)) for i in range(spaces) for j in (0, 1)]
    cores = [(at(i, j), at(i ^ 1, j)) for i in range(spaces) for j in (0, 1)]
    pairs = [(at(i, j), at(i ^ 2, j)) for i in range(spaces) for j in (0, 1)]
    chain = [(at(i - 1, 0), at(i, 0)) for i in range(1, spaces)]
    chain += [(at(i + 1, 1), at(i, 1)) for i in range(spaces - 1)]

    outer = [(t, t + 1) for t in range(1, 2 * spaces - 1, 2)]
    outer += [(j, i) for i, j in outer]

    own = inputs.reshape(chans, held, cols)
    near, far, peer, w_a, w_b = call_pieces(own, w_up)
    own, w_conv, peer, w_a, far, near, w_b = lax.optimization_barrier((own, w_conv, peer, w_a, far, near, w_b))
    peer = lax.ppermute(peer, AXES, across)
    w_a = lax.ppermute(w_a, AXES, across)
    far = lax.ppermute(far, AXES, outer)
    near = lax.ppermute(near, AXES, chain)
    x = call_rows(True, own, sizes)
    x, w_a, w_b, w_conv, near, far = lax.optimization_barrier((x, w_a, w_b, w_conv, near, far))
    w_b = lax.ppermute(w_b, AXES, across)
    w_half, kernel, other = call_kernels(True, w_up, w_conv, sizes)
    w_ax = lax.ppermute(w_a, AXES, pairs)
    w_ac = lax.ppermute(w_a, AXES, cores)
    biases = (b_up[None], b_conv[None])
    x, total = call_first(paired_first, (peer, near, far), (x, w_half, kernel), biases[0], sizes)
    results = (x, total, other)
    w_b, w_ax, w_ac, *results = lax.optimization_barrier((w_b, w_ax, w_ac, *results))
    w_bc = lax.ppermute(w_b, AXES, cores)
    w_axc = lax.ppermute(w_ax, AXES, cores)
    return call_second(True, (w_a, w_ax, w_b, w_ac, w_axc, w_bc), results, biases, sizes)


def gathered(inputs, w_up, b_up, w_conv, b_conv, sizes):
    spaces, chs = lax.axis_size("space"), lax.axis_size("ch")
    c = lax.axis_index("ch")
    w_all = lax.all_gather(w_up[16:48], "ch", axis=1, tiled=True)
    part = w_all.shape[1] // 2
    rows = lax.all_gather(inputs[:, 0], "ch", axis=0, tiled=True).transpose(1, 0, 2)
    forward = [(i, i + 1) for i in range(spaces - 1)]
    backward = [(j, i) for i, j in forward]
    low = lax.ppermute(rows[-1:], "space", forward)
    high = lax.ppermute(rows[:1], "space", backward)
    rows = jnp.concatenate([low, rows, high], axis=0)
    share = inputs.shape[2] // chs
    rows = lax.dynamic_slice_in_dim(rows, c * share, share + 2, 0)
    biases = (b_up[None], b_conv[None])
    *prepared, other = call_kernels(False, w_all[:, :part], w_conv, sizes)
    prepared = (call_rows(False, rows, sizes), *prepared)
    results = (*call_first(gathered_first, (), prepared, biases[0], sizes), other)
    return call_second(False, (w_all[:16, part:], w_all[16:, part:]), results, biases, sizes)


def local(inputs, w_up, b_up, w_conv, b_conv):
    chs = lax.axis_size("ch")
    sizes = (w_up.shape[2], w_conv.shape[1], 2 * inputs.shape[2] // chs, inputs.shape[3])
    plan = paired if chs == 2 and lax.axis_size("space") % 4 == 0 else gathered
    return plan(inputs, w_up, b_up, w_conv, b_conv, sizes)


def solution(mesh):
    return jax.shard_map(
        local,
        mesh=mesh,
        in_specs=(P("ch", None, "space", None), P(None, "ch", None), P(), P(), P()),
        out_specs=P(None, None, ("space", "ch"), None),
        check_vma=False,
    )
```

```python
import functools

import jax
import jax.numpy as jnp
from jax import lax
from jax.experimental import pallas as pl
from jax.experimental.pallas import tpu as pltpu
from jax.sharding import PartitionSpec as P

AXES = ("space", "ch")
PHASES = (((1, 0), (3, -1)), ((2, 0), (0, 1)))
COLUMNS = ((3, 0, 1), (0, 1, 2))
VMEM = pl.BlockSpec(memory_space=pltpu.VMEM)
ANY = pl.BlockSpec(memory_space=pl.ANY)
LIMIT = 40 * 2**20


def column_of(bias):
    lanes = bias.shape[-1]
    return jnp.transpose(jnp.broadcast_to(bias, (lanes, lanes)))


def shifted(value, step):
    cols = value.shape[1]
    place = lax.broadcasted_iota(jnp.int32, value.shape, 1)
    edge = 0 if step == 1 else cols - 1
    return jnp.where(place == edge, 0.0, pltpu.roll(value, step % cols, 1))


def upsample(cell, tap_of, bias, u_ref, first, last):
    held, cols = u_ref.shape[1], u_ref.shape[3]
    for row_phase in (0, 1):
        for col_phase in (0, 1):
            taps = []
            for row_tap, row_shift in PHASES[row_phase]:
                for col_tap, col_shift in PHASES[col_phase]:
                    slot = row_shift + 1 - row_phase
                    taps.append((row_tap * 4 + col_tap, slot, col_shift % 3))
            kernel = jnp.concatenate([tap_of(tap) for tap, _, _ in taps], axis=1)
            for start in range(0, held // 2, 2):
                places = range(start, min(start + 2, held // 2))
                cells = jnp.concatenate(
                    [
                        jnp.concatenate([cell(copy, slot + place) for place in places], axis=1)
                        for _, slot, copy in taps
                    ],
                    axis=0,
                )
                summed = jnp.dot(kernel, cells, preferred_element_type=jnp.float32)
                for number, place in enumerate(places):
                    row = 2 * place + 1 - row_phase
                    value = summed[:, number * cols : (number + 1) * cols] + bias
                    value = jnp.maximum(value, 0.2 * value)
                    if row == 0:
                        value = jnp.where(first, 0.0, value)
                    if row == held - 1:
                        value = jnp.where(last, 0.0, value)
                    u_ref[col_phase, row] = value.astype(jnp.bfloat16)
                    moved = shifted(value, -1 if col_phase == 0 else 1)
                    u_ref[2 + col_phase, row] = moved.astype(jnp.bfloat16)


def convolve(kernel, u_ref, start, col_phase):
    cells = jnp.concatenate(
        [
            jnp.concatenate([u_ref[copy, start + row_tap], u_ref[copy, start + row_tap + 1]], 1)
            for row_tap in range(3)
            for copy in COLUMNS[col_phase]
        ],
        axis=0,
    )
    return jnp.dot(kernel, cells, preferred_element_type=jnp.float32)


def split_kernels(w_conv_ref, halves_ref):
    cout = w_conv_ref.shape[1]
    part = cout // 2
    low = lax.broadcasted_iota(jnp.int32, (cout, cout), 1) < part
    for row_tap in range(3):
        for col_tap in range(3):
            taps = [w_conv_ref[a * 9 + row_tap * 3 + col_tap].astype(jnp.float32) for a in range(3)]
            turned = [pltpu.roll(tap, part, 1) for tap in taps]
            columns = pl.ds((row_tap * 3 + col_tap) * cout, cout)
            for plane in (0, 1):
                near, far = 1 - plane, 2 - plane
                rows = pl.ds(plane * cout, cout)
                halves_ref[0, rows, columns] = jnp.where(low, taps[near], turned[far]).astype(jnp.bfloat16)
                halves_ref[1, rows, columns] = jnp.where(low, turned[near], taps[far]).astype(jnp.bfloat16)


def bias_of(bias_ref, column_ref, blocks):
    column_ref[...] = column_of(bias_ref[...])
    return jnp.concatenate([column_ref[pl.ds(pl.multiple_of(at, 16), size)] for at, size in blocks], axis=0)


def ends(s, c):
    first = (s == 0) & (c == 0)
    last = (s == lax.axis_size("space") - 1) & (c == lax.axis_size("ch") - 1)
    return first, last


def store_row(x_ref, slot, offset, value):
    where = pl.ds(pl.multiple_of(offset, 16), value.shape[0])
    x_ref[0, slot, where] = value.astype(jnp.bfloat16)
    x_ref[1, slot, where] = shifted(value, -1).astype(jnp.bfloat16)
    x_ref[2, slot, where] = shifted(value, 1).astype(jnp.bfloat16)


def arrival(x, part):
    if x is None:
        return [[(0, part)], [(0, part)]]
    quarter, half = part // 4, part // 2
    return [
        [(x * half, half), ((1 - x) * half, half)],
        [(x * quarter, quarter), ((1 - x) * quarter, quarter), (half, half)],
    ]


def arrange(x, part):
    source = lax.broadcasted_iota(jnp.int32, (2 * part, 2 * part), 0)
    target = lax.broadcasted_iota(jnp.int32, (2 * part, 2 * part), 1)
    wanted = jnp.zeros_like(target)
    for plane, blocks in enumerate(arrival(x, part)):
        place = plane * part
        for first, size in blocks:
            inside = (target >= place) & (target < place + size)
            wanted = jnp.where(inside, target - place + plane * part + first, wanted)
            place += size
    return jnp.where(source == wanted, 1.0, 0.0).astype(jnp.bfloat16)


def own_part(half, refs, results, scratch):
    w_half_ref, kernel_ref, b_up_ref = refs
    x_ref, sum_ref = results
    column_ref, u_ref = scratch
    s, c = lax.axis_index("space"), lax.axis_index("ch")
    part, cols = w_half_ref.shape[1], u_ref.shape[3]

    def tap_of(tap):
        return jnp.concatenate([w_half_ref[tap], w_half_ref[16 + tap]], axis=0)

    bias = bias_of(b_up_ref, column_ref, [(half * part, part)] * 2)
    upsample(lambda copy, slot: x_ref[copy, slot], tap_of, bias, u_ref, *ends(s, c))
    kernel = kernel_ref[...]
    for start in range(0, u_ref.shape[1] - 2, 2):
        for col_phase in (0, 1):
            sum_ref[col_phase, :, start * cols : (start + 2) * cols] = convolve(kernel, u_ref, start, col_phase)


def prepare(paired, own_ref, w_half_ref, w_conv_ref, x_ref, w_ref, kernel_ref, other_ref, *scratch):
    halves_ref, v_ref, wide_ref, raw_ref, sems = scratch
    s, c = lax.axis_index("space"), lax.axis_index("ch")
    skipped = (w_half_ref.shape[0] - 32) // 2
    copies = [
        pltpu.make_async_copy(own_ref, raw_ref, sems.at[0]),
        pltpu.make_async_copy(w_conv_ref, v_ref, sems.at[1]),
        pltpu.make_async_copy(w_half_ref.at[pl.ds(skipped, 32)], w_ref, sems.at[2]),
    ]
    for copy in copies:
        copy.start()
    copies[0].wait()
    if paired:
        chans, rows, cols = own_ref.shape
        wide_ref[...] = raw_ref[...].astype(jnp.float32).reshape(chans * rows, cols)
        share = x_ref.shape[1] - 1
        for place in range(share):
            value = wide_ref[pl.ds(place + c * (rows - share), chans, stride=rows), :]
            store_row(x_ref, place + 1 - c, c * chans, value)
    else:
        for slot in range(own_ref.shape[0]):
            store_row(x_ref, slot, 0, raw_ref[slot].astype(jnp.float32))
    cout = w_conv_ref.shape[1]
    half, x = (c, lax.rem(s, 4) // 2) if paired else (0, None)
    copies[1].wait()
    split_kernels(v_ref, halves_ref)
    kernel_ref[...] = halves_ref[half]
    matrix = arrange(x, cout // 2)
    for number in range(9):
        columns = pl.ds(number * cout, cout)
        moved = jnp.dot(halves_ref[1 - half, :, columns], matrix, preferred_element_type=jnp.float32)
        other_ref[:, columns] = moved.astype(jnp.bfloat16)
    copies[2].wait()


def paired_first(peer_ref, near_ref, far_ref, started_ref, *refs):
    refs, results, scratch = refs[:3], refs[3:5], refs[5:]
    x_ref = results[0]
    c = lax.axis_index("ch")
    share, chans, _ = peer_ref.shape
    for place in range(share):
        store_row(x_ref, place + 1 - c, (1 - c) * chans, peer_ref[place].astype(jnp.float32))
    slot = c * (x_ref.shape[1] - 1)
    store_row(x_ref, slot, c * chans, near_ref[...].astype(jnp.float32))
    store_row(x_ref, slot, (1 - c) * chans, far_ref[...].astype(jnp.float32))
    own_part(c, refs, results, scratch)


def gathered_first(started_ref, *refs):
    own_part(0, refs[:3], refs[3:5], refs[5:])


def second(paired, count, *refs):
    parts, refs = refs[:count], refs[count:]
    x_ref, sum_ref, other_ref, b_up_ref, b_conv_ref, out_ref, column_ref, u_ref, total_ref, made_ref, sems = refs
    s, c = lax.axis_index("space"), lax.axis_index("ch")
    cout, _, rows, _ = out_ref.shape
    part = cout // 2
    half, x = (1 - c, lax.rem(s, 4) // 2) if paired else (1, None)
    cols = x_ref.shape[3]
    if paired:
        chans = x_ref.shape[2] // 2
        core = lax.rem(s, 2)
        sides = [pl.ds(pl.multiple_of(side * chans, 16), chans) for side in (core, 1 - core)]
        big = part // 2

        def tap_of(tap):
            columns = []
            for near_ref, far_ref, rest_ref in (parts[:3], parts[3:]):
                rows = [near_ref[tap, :big], far_ref[tap, :big], near_ref[tap, big:], far_ref[tap, big:], rest_ref[tap]]
                columns.append(jnp.concatenate(rows, axis=0))
            return jnp.concatenate(columns, axis=1)

        def cell(copy, slot):
            return jnp.concatenate([x_ref[copy, slot, side] for side in sides], axis=0)
    else:

        def tap_of(tap):
            return jnp.concatenate([part_ref[tap] for part_ref in parts], axis=0)

        def cell(copy, slot):
            return x_ref[copy, slot]

    blocks = [(half * part + at, size) for plane in arrival(x, part) for at, size in plane]
    bias = bias_of(b_up_ref, column_ref, blocks)
    upsample(cell, tap_of, bias, u_ref, *ends(s, c))
    source = lax.broadcasted_iota(jnp.int32, (2 * cols, 2 * cols), 0)
    target = lax.broadcasted_iota(jnp.int32, (2 * cols, 2 * cols), 1)
    wanted = jnp.where(source < cols, 2 * source, 2 * (source - cols) + 1)
    interleave = jnp.where(wanted == target, 1.0, 0.0).astype(jnp.bfloat16)
    kernel = other_ref[...]
    bias = column_of(b_conv_ref[...])
    bias = jnp.concatenate([bias, bias], axis=0)
    for start in range(0, rows, 2):
        halves = [
            convolve(kernel, u_ref, start, col_phase) + sum_ref[col_phase, :, start * cols : (start + 2) * cols]
            for col_phase in (0, 1)
        ]
        for number in (0, 1):
            pair = [
                (half[:, number * cols : (number + 1) * cols] + bias).astype(jnp.bfloat16) for half in halves
            ]
            mixed = jnp.dot(jnp.concatenate(pair, axis=1), interleave, preferred_element_type=jnp.float32)
            for side in (0, 1):
                total_ref[side, pl.ds(start + number, 2 * cout, stride=rows), :] = mixed[
                    :, side * cols : (side + 1) * cols
                ]
    copies = []
    for plane in (0, 1):
        for side in (0, 1):
            number = 2 * plane + side
            block = total_ref[side, pl.ds(plane * cout * rows, cout * rows), :]
            made_ref[number] = block.reshape(cout, rows, cols).astype(jnp.bfloat16)
            place = out_ref.at[:, plane, :, pl.ds(side * cols, cols)]
            copies.append(pltpu.make_async_copy(made_ref.at[number], place, sems.at[number]))
            copies[-1].start()
    for copy in copies:
        copy.wait()


def pieces(own_ref, w_up_ref, near_ref, far_ref, peer_ref, w_a_ref, w_b_ref, wide_ref, raw_ref, sems):
    s, c = lax.axis_index("space"), lax.axis_index("ch")
    raw = pltpu.make_async_copy(own_ref, raw_ref, sems.at[3])
    raw.start()
    me = lax.rem(s, 4)
    part, lanes = w_up_ref.shape[1], w_a_ref.shape[2]
    side = pl.ds(pl.multiple_of(lax.rem(me, 2) * lanes, lanes), lanes)
    (first, big), = arrival(me // 2, part)[0][:1]
    (second, small), _, (third, rest) = arrival(me // 2, part)[1]
    cuts = (
        (16, first, big, w_a_ref.at[:, pl.ds(0, big)]),
        (32, second, small, w_a_ref.at[:, pl.ds(big, small)]),
        (32, third, rest, w_b_ref),
    )
    copies = []
    for number, (tap, channel, count, place) in enumerate(cuts):
        source = w_up_ref.at[pl.ds(tap, 16), pl.ds(pl.multiple_of(channel, 16), count), side]
        copies.append(pltpu.make_async_copy(source, place, sems.at[number]))
        copies[-1].start()
    chans, rows, cols = own_ref.shape
    raw.wait()
    wide_ref[...] = raw_ref[...].astype(jnp.float32).reshape(chans * rows, cols)
    inner, outer = (1 - c) * (rows - 1), c * (rows - 1)
    near_ref[...] = wide_ref[pl.ds(inner, chans, stride=rows), :].astype(jnp.bfloat16)
    far_ref[...] = wide_ref[pl.ds(outer, chans, stride=rows), :].astype(jnp.bfloat16)
    share = peer_ref.shape[0]
    for place in range(share):
        row = wide_ref[pl.ds(place + (1 - c) * (rows - share), chans, stride=rows), :]
        peer_ref[place] = row.astype(jnp.bfloat16)
    for copy in copies:
        copy.wait()


def call_pieces(own, w_up):
    chans, rows, cols = own.shape
    part, cin = w_up.shape[1:]
    return pl.pallas_call(
        pieces,
        out_shape=(
            jax.ShapeDtypeStruct((chans, cols), jnp.bfloat16),
            jax.ShapeDtypeStruct((chans, cols), jnp.bfloat16),
            jax.ShapeDtypeStruct((rows // 2 + 1, chans, cols), jnp.bfloat16),
            jax.ShapeDtypeStruct((16, 3 * part // 4, cin // 2), jnp.bfloat16),
            jax.ShapeDtypeStruct((16, part // 2, cin // 2), jnp.bfloat16),
        ),
        in_specs=[ANY, ANY],
        out_specs=(VMEM,) * 5,
        scratch_shapes=[
            pltpu.VMEM((chans * rows, cols), jnp.float32),
            pltpu.VMEM((chans, rows, cols), jnp.bfloat16),
            pltpu.SemaphoreType.DMA((4,)),
        ],
        compiler_params=pltpu.CompilerParams(vmem_limit_bytes=LIMIT),
    )(in_hbm(own), in_hbm(w_up))


def in_hbm(operand):
    return pltpu.with_memory_space_constraint(operand, pltpu.HBM)


def cost(sizes):
    cin, cout, rows, cols = sizes
    flops = 2 * cout * 4 * cin * 2 * cols * (rows + 2) + 2 * 2 * cout * 9 * cout * 2 * cols * rows
    return pl.CostEstimate(flops=flops, bytes_accessed=8 * 2**20, transcendentals=0)


def call_prepare(paired, own, w_half, w_conv, sizes):
    cin, cout, rows, cols = sizes
    wide = own.shape[0] * own.shape[1] if paired else 8
    return pl.pallas_call(
        functools.partial(prepare, paired),
        out_shape=(
            jax.ShapeDtypeStruct((3, rows // 2 + 2, cin, cols), jnp.bfloat16),
            jax.ShapeDtypeStruct((32, cout // 2, cin), jnp.bfloat16),
            jax.ShapeDtypeStruct((2 * cout, 9 * cout), jnp.bfloat16),
            jax.ShapeDtypeStruct((2 * cout, 9 * cout), jnp.bfloat16),
        ),
        in_specs=[ANY] * 3,
        out_specs=(VMEM,) * 4,
        scratch_shapes=[
            pltpu.VMEM((2, 2 * cout, 9 * cout), jnp.bfloat16),
            pltpu.VMEM((27, cout, cout), jnp.bfloat16),
            pltpu.VMEM((wide, cols), jnp.float32),
            pltpu.VMEM(own.shape, jnp.bfloat16),
            pltpu.SemaphoreType.DMA((3,)),
        ],
        cost_estimate=pl.CostEstimate(flops=2 * 18 * 256 * cout * cout, bytes_accessed=8 * 2**20, transcendentals=0),
        compiler_params=pltpu.CompilerParams(vmem_limit_bytes=LIMIT),
    )(in_hbm(own), in_hbm(w_half), in_hbm(w_conv))


def call_first(body, rows_in, prepared, b_up, sizes):
    cin, cout, rows, cols = sizes
    started, w_half, kernel = prepared
    return pl.pallas_call(
        body,
        out_shape=(
            jax.ShapeDtypeStruct(started.shape, jnp.bfloat16),
            jax.ShapeDtypeStruct((2, 2 * cout, rows * cols), jnp.float32),
        ),
        in_specs=[VMEM] * (len(rows_in) + 4),
        out_specs=(VMEM,) * 2,
        scratch_shapes=[
            pltpu.VMEM((cout, cout), jnp.float32),
            pltpu.VMEM((4, rows + 2, cout, cols), jnp.bfloat16),
        ],
        input_output_aliases={len(rows_in): 0},
        cost_estimate=cost(sizes),
        compiler_params=pltpu.CompilerParams(vmem_limit_bytes=LIMIT),
    )(*rows_in, started, w_half, kernel, b_up)


def call_second(paired, parts, results, biases, sizes):
    cin, cout, rows, cols = sizes
    return pl.pallas_call(
        functools.partial(second, paired, len(parts)),
        out_shape=jax.ShapeDtypeStruct((cout, 2, rows, 2 * cols), jnp.bfloat16),
        in_specs=[VMEM] * (len(parts) + 5),
        out_specs=ANY,
        scratch_shapes=[
            pltpu.VMEM((cout, cout), jnp.float32),
            pltpu.VMEM((4, rows + 2, cout, cols), jnp.bfloat16),
            pltpu.VMEM((2, 2 * cout * rows, cols), jnp.float32),
            pltpu.VMEM((4, cout, rows, cols), jnp.bfloat16),
            pltpu.SemaphoreType.DMA((4,)),
        ],
        cost_estimate=cost(sizes),
        compiler_params=pltpu.CompilerParams(vmem_limit_bytes=LIMIT),
    )(*parts, *results, *biases)


def paired(inputs, w_up, b_up, w_conv, b_conv, sizes):
    spaces = lax.axis_size("space")
    s, c = lax.axis_index("space"), lax.axis_index("ch")
    chans, _, held, cols = inputs.shape

    def at(space, ch):
        return space * 2 + ch

    across = [(at(i, j), at(i, 1 - j)) for i in range(spaces) for j in (0, 1)]
    cores = [(at(i, j), at(i ^ 1, j)) for i in range(spaces) for j in (0, 1)]
    pairs = [(at(i, j), at(i ^ 2, j)) for i in range(spaces) for j in (0, 1)]
    chain = [(at(i - 1, 0), at(i, 0)) for i in range(1, spaces)]
    chain += [(at(i + 1, 1), at(i, 1)) for i in range(spaces - 1)]

    own = inputs.reshape(chans, held, cols)
    near, far, peer, w_a, w_b = call_pieces(own, w_up)
    far = lax.ppermute(far, AXES, across)
    far, near, own, w_conv, w_a, peer, w_b = lax.optimization_barrier((far, near, own, w_conv, w_a, peer, w_b))
    w_a = lax.ppermute(w_a, AXES, across)
    peer = lax.ppermute(peer, AXES, across)
    w_b = lax.ppermute(w_b, AXES, across)
    near = lax.ppermute(near, AXES, chain)
    far = lax.ppermute(far, AXES, chain)
    x, w_half, kernel, other = call_prepare(True, own, w_up, w_conv, sizes)
    w_ax = lax.ppermute(w_a, AXES, pairs)
    w_ac = lax.ppermute(w_a, AXES, cores)
    biases = (b_up[None], b_conv[None])
    x, total = call_first(paired_first, (peer, near, far), (x, w_half, kernel), biases[0], sizes)
    results = (x, total, other)
    w_b, w_ax, w_ac, *results = lax.optimization_barrier((w_b, w_ax, w_ac, *results))
    w_bc = lax.ppermute(w_b, AXES, cores)
    w_axc = lax.ppermute(w_ax, AXES, cores)
    return call_second(True, (w_a, w_ax, w_b, w_ac, w_axc, w_bc), results, biases, sizes)


def gathered(inputs, w_up, b_up, w_conv, b_conv, sizes):
    spaces, chs = lax.axis_size("space"), lax.axis_size("ch")
    c = lax.axis_index("ch")
    w_all = lax.all_gather(w_up[16:48], "ch", axis=1, tiled=True)
    part = w_all.shape[1] // 2
    rows = lax.all_gather(inputs[:, 0], "ch", axis=0, tiled=True).transpose(1, 0, 2)
    forward = [(i, i + 1) for i in range(spaces - 1)]
    backward = [(j, i) for i, j in forward]
    low = lax.ppermute(rows[-1:], "space", forward)
    high = lax.ppermute(rows[:1], "space", backward)
    rows = jnp.concatenate([low, rows, high], axis=0)
    share = inputs.shape[2] // chs
    rows = lax.dynamic_slice_in_dim(rows, c * share, share + 2, 0)
    biases = (b_up[None], b_conv[None])
    *prepared, other = call_prepare(False, rows, w_all[:, :part], w_conv, sizes)
    results = (*call_first(gathered_first, (), prepared, biases[0], sizes), other)
    return call_second(False, (w_all[:16, part:], w_all[16:, part:]), results, biases, sizes)


def local(inputs, w_up, b_up, w_conv, b_conv):
    chs = lax.axis_size("ch")
    sizes = (w_up.shape[2], w_conv.shape[1], 2 * inputs.shape[2] // chs, inputs.shape[3])
    plan = paired if chs == 2 and lax.axis_size("space") % 4 == 0 else gathered
    return plan(inputs, w_up, b_up, w_conv, b_conv, sizes)


def solution(mesh):
    return jax.shard_map(
        local,
        mesh=mesh,
        in_specs=(P("ch", None, "space", None), P(None, "ch", None), P(), P(), P()),
        out_specs=P(None, None, ("space", "ch"), None),
        check_vma=False,
    )
```

```python
import functools

import jax
import jax.numpy as jnp
from jax import lax
from jax.experimental import pallas as pl
from jax.experimental.pallas import tpu as pltpu
from jax.sharding import PartitionSpec as P

AXES = ("space", "ch")
PHASES = (((1, 0), (3, -1)), ((2, 0), (0, 1)))
COLUMNS = ((3, 0, 1), (0, 1, 2))
VMEM = pl.BlockSpec(memory_space=pltpu.VMEM)
ANY = pl.BlockSpec(memory_space=pl.ANY)
LIMIT = 40 * 2**20


def column_of(bias):
    lanes = bias.shape[-1]
    return jnp.transpose(jnp.broadcast_to(bias, (lanes, lanes)))


def shifted(value, step):
    cols = value.shape[1]
    place = lax.broadcasted_iota(jnp.int32, value.shape, 1)
    edge = 0 if step == 1 else cols - 1
    return jnp.where(place == edge, 0.0, pltpu.roll(value, step % cols, 1))


def upsample(cell, tap_of, bias, u_ref, first, last):
    held, cols = u_ref.shape[1], u_ref.shape[3]
    for row_phase in (0, 1):
        for col_phase in (0, 1):
            taps = []
            for row_tap, row_shift in PHASES[row_phase]:
                for col_tap, col_shift in PHASES[col_phase]:
                    slot = row_shift + 1 - row_phase
                    taps.append((row_tap * 4 + col_tap, slot, col_shift % 3))
            kernel = jnp.concatenate([tap_of(tap) for tap, _, _ in taps], axis=1)
            for start in range(0, held // 2, 2):
                places = range(start, min(start + 2, held // 2))
                cells = jnp.concatenate(
                    [
                        jnp.concatenate([cell(copy, slot + place) for place in places], axis=1)
                        for _, slot, copy in taps
                    ],
                    axis=0,
                )
                summed = jnp.dot(kernel, cells, preferred_element_type=jnp.float32)
                for number, place in enumerate(places):
                    row = 2 * place + 1 - row_phase
                    value = summed[:, number * cols : (number + 1) * cols] + bias
                    value = jnp.maximum(value, 0.2 * value)
                    if row == 0:
                        value = jnp.where(first, 0.0, value)
                    if row == held - 1:
                        value = jnp.where(last, 0.0, value)
                    u_ref[col_phase, row] = value.astype(jnp.bfloat16)
                    moved = shifted(value, -1 if col_phase == 0 else 1)
                    u_ref[2 + col_phase, row] = moved.astype(jnp.bfloat16)


def convolve(kernel, u_ref, start, col_phase):
    cells = jnp.concatenate(
        [
            jnp.concatenate([u_ref[copy, start + row_tap], u_ref[copy, start + row_tap + 1]], 1)
            for row_tap in range(3)
            for copy in COLUMNS[col_phase]
        ],
        axis=0,
    )
    return jnp.dot(kernel, cells, preferred_element_type=jnp.float32)


def split_kernels(w_conv_ref, halves_ref):
    cout = w_conv_ref.shape[1]
    part = cout // 2
    low = lax.broadcasted_iota(jnp.int32, (cout, cout), 1) < part
    for row_tap in range(3):
        for col_tap in range(3):
            taps = [w_conv_ref[a * 9 + row_tap * 3 + col_tap].astype(jnp.float32) for a in range(3)]
            turned = [pltpu.roll(tap, part, 1) for tap in taps]
            columns = pl.ds((row_tap * 3 + col_tap) * cout, cout)
            for plane in (0, 1):
                near, far = 1 - plane, 2 - plane
                rows = pl.ds(plane * cout, cout)
                halves_ref[0, rows, columns] = jnp.where(low, taps[near], turned[far]).astype(jnp.bfloat16)
                halves_ref[1, rows, columns] = jnp.where(low, turned[near], taps[far]).astype(jnp.bfloat16)


def bias_of(bias_ref, column_ref, blocks):
    column_ref[...] = column_of(bias_ref[...])
    return jnp.concatenate([column_ref[pl.ds(pl.multiple_of(at, 16), size)] for at, size in blocks], axis=0)


def ends(s, c):
    first = (s == 0) & (c == 0)
    last = (s == lax.axis_size("space") - 1) & (c == lax.axis_size("ch") - 1)
    return first, last


def store_row(x_ref, slot, offset, value):
    where = pl.ds(pl.multiple_of(offset, 16), value.shape[0])
    x_ref[0, slot, where] = value.astype(jnp.bfloat16)
    x_ref[1, slot, where] = shifted(value, -1).astype(jnp.bfloat16)
    x_ref[2, slot, where] = shifted(value, 1).astype(jnp.bfloat16)


def arrival(x, part):
    if x is None:
        return [[(0, part)], [(0, part)]]
    quarter, half = part // 4, part // 2
    return [
        [(x * half, half), ((1 - x) * half, half)],
        [(x * quarter, quarter), ((1 - x) * quarter, quarter), (half, half)],
    ]


def arrange(x, part):
    source = lax.broadcasted_iota(jnp.int32, (2 * part, 2 * part), 0)
    target = lax.broadcasted_iota(jnp.int32, (2 * part, 2 * part), 1)
    wanted = jnp.zeros_like(target)
    for plane, blocks in enumerate(arrival(x, part)):
        place = plane * part
        for first, size in blocks:
            inside = (target >= place) & (target < place + size)
            wanted = jnp.where(inside, target - place + plane * part + first, wanted)
            place += size
    return jnp.where(source == wanted, 1.0, 0.0).astype(jnp.bfloat16)


def own_part(half, refs, results, scratch):
    w_half_ref, kernel_ref, b_up_ref = refs
    x_ref, sum_ref = results
    column_ref, u_ref = scratch
    s, c = lax.axis_index("space"), lax.axis_index("ch")
    part, cols = w_half_ref.shape[1], u_ref.shape[3]

    def tap_of(tap):
        return jnp.concatenate([w_half_ref[tap], w_half_ref[16 + tap]], axis=0)

    bias = bias_of(b_up_ref, column_ref, [(half * part, part)] * 2)
    upsample(lambda copy, slot: x_ref[copy, slot], tap_of, bias, u_ref, *ends(s, c))
    kernel = kernel_ref[...]
    for start in range(0, u_ref.shape[1] - 2, 2):
        for col_phase in (0, 1):
            sum_ref[col_phase, :, start * cols : (start + 2) * cols] = convolve(kernel, u_ref, start, col_phase)


def prepare(paired, own_ref, w_half_ref, w_conv_ref, x_ref, w_ref, kernel_ref, other_ref, *scratch):
    halves_ref, v_ref, wide_ref, raw_ref, sems = scratch
    s, c = lax.axis_index("space"), lax.axis_index("ch")
    skipped = (w_half_ref.shape[0] - 32) // 2
    copies = [
        pltpu.make_async_copy(own_ref, raw_ref, sems.at[0]),
        pltpu.make_async_copy(w_conv_ref, v_ref, sems.at[1]),
        pltpu.make_async_copy(w_half_ref.at[pl.ds(skipped, 32)], w_ref, sems.at[2]),
    ]
    for copy in copies:
        copy.start()
    copies[0].wait()
    if paired:
        chans, rows, cols = own_ref.shape
        wide_ref[...] = raw_ref[...].astype(jnp.float32).reshape(chans * rows, cols)
        share = x_ref.shape[1] - 1
        for place in range(share):
            value = wide_ref[pl.ds(place + c * (rows - share), chans, stride=rows), :]
            store_row(x_ref, place + 1 - c, c * chans, value)
    else:
        for slot in range(own_ref.shape[0]):
            store_row(x_ref, slot, 0, raw_ref[slot].astype(jnp.float32))
    cout = w_conv_ref.shape[1]
    half, x = (c, lax.rem(s, 4) // 2) if paired else (0, None)
    copies[1].wait()
    split_kernels(v_ref, halves_ref)
    kernel_ref[...] = halves_ref[half]
    matrix = arrange(x, cout // 2)
    for number in range(9):
        columns = pl.ds(number * cout, cout)
        moved = jnp.dot(halves_ref[1 - half, :, columns], matrix, preferred_element_type=jnp.float32)
        other_ref[:, columns] = moved.astype(jnp.bfloat16)
    copies[2].wait()


def paired_first(peer_ref, near_ref, far_ref, started_ref, *refs):
    refs, results, scratch = refs[:3], refs[3:5], refs[5:]
    x_ref = results[0]
    c = lax.axis_index("ch")
    share, chans, _ = peer_ref.shape
    for place in range(share):
        store_row(x_ref, place + 1 - c, (1 - c) * chans, peer_ref[place].astype(jnp.float32))
    slot = c * (x_ref.shape[1] - 1)
    store_row(x_ref, slot, c * chans, near_ref[...].astype(jnp.float32))
    store_row(x_ref, slot, (1 - c) * chans, far_ref[...].astype(jnp.float32))
    own_part(c, refs, results, scratch)


def gathered_first(started_ref, *refs):
    own_part(0, refs[:3], refs[3:5], refs[5:])


def second(paired, count, *refs):
    parts, refs = refs[:count], refs[count:]
    x_ref, sum_ref, other_ref, b_up_ref, b_conv_ref, out_ref, column_ref, u_ref, total_ref, made_ref, sems = refs
    s, c = lax.axis_index("space"), lax.axis_index("ch")
    cout, _, rows, _ = out_ref.shape
    part = cout // 2
    half, x = (1 - c, lax.rem(s, 4) // 2) if paired else (1, None)
    cols = x_ref.shape[3]
    if paired:
        chans = x_ref.shape[2] // 2
        core = lax.rem(s, 2)
        sides = [pl.ds(pl.multiple_of(side * chans, 16), chans) for side in (core, 1 - core)]
        big = part // 2

        def tap_of(tap):
            columns = []
            for near_ref, far_ref, rest_ref in (parts[:3], parts[3:]):
                rows = [near_ref[tap, :big], far_ref[tap, :big], near_ref[tap, big:], far_ref[tap, big:], rest_ref[tap]]
                columns.append(jnp.concatenate(rows, axis=0))
            return jnp.concatenate(columns, axis=1)

        def cell(copy, slot):
            return jnp.concatenate([x_ref[copy, slot, side] for side in sides], axis=0)
    else:

        def tap_of(tap):
            return jnp.concatenate([part_ref[tap] for part_ref in parts], axis=0)

        def cell(copy, slot):
            return x_ref[copy, slot]

    blocks = [(half * part + at, size) for plane in arrival(x, part) for at, size in plane]
    bias = bias_of(b_up_ref, column_ref, blocks)
    upsample(cell, tap_of, bias, u_ref, *ends(s, c))
    source = lax.broadcasted_iota(jnp.int32, (2 * cols, 2 * cols), 0)
    target = lax.broadcasted_iota(jnp.int32, (2 * cols, 2 * cols), 1)
    wanted = jnp.where(source < cols, 2 * source, 2 * (source - cols) + 1)
    interleave = jnp.where(wanted == target, 1.0, 0.0).astype(jnp.bfloat16)
    kernel = other_ref[...]
    bias = column_of(b_conv_ref[...])
    bias = jnp.concatenate([bias, bias], axis=0)
    for start in range(0, rows, 2):
        halves = [
            convolve(kernel, u_ref, start, col_phase) + sum_ref[col_phase, :, start * cols : (start + 2) * cols]
            for col_phase in (0, 1)
        ]
        for number in (0, 1):
            pair = [
                (half[:, number * cols : (number + 1) * cols] + bias).astype(jnp.bfloat16) for half in halves
            ]
            mixed = jnp.dot(jnp.concatenate(pair, axis=1), interleave, preferred_element_type=jnp.float32)
            for side in (0, 1):
                total_ref[side, pl.ds(start + number, 2 * cout, stride=rows), :] = mixed[
                    :, side * cols : (side + 1) * cols
                ]
    copies = []
    for plane in (0, 1):
        for side in (0, 1):
            number = 2 * plane + side
            block = total_ref[side, pl.ds(plane * cout * rows, cout * rows), :]
            made_ref[number] = block.reshape(cout, rows, cols).astype(jnp.bfloat16)
            place = out_ref.at[:, plane, :, pl.ds(side * cols, cols)]
            copies.append(pltpu.make_async_copy(made_ref.at[number], place, sems.at[number]))
            copies[-1].start()
    for copy in copies:
        copy.wait()


def pieces(own_ref, w_up_ref, near_ref, far_ref, peer_ref, w_a_ref, w_b_ref, wide_ref, raw_ref, sems):
    s, c = lax.axis_index("space"), lax.axis_index("ch")
    raw = pltpu.make_async_copy(own_ref, raw_ref, sems.at[3])
    raw.start()
    me = lax.rem(s, 4)
    part, lanes = w_up_ref.shape[1], w_a_ref.shape[2]
    side = pl.ds(pl.multiple_of(lax.rem(me, 2) * lanes, lanes), lanes)
    (first, big), = arrival(me // 2, part)[0][:1]
    (second, small), _, (third, rest) = arrival(me // 2, part)[1]
    cuts = (
        (16, first, big, w_a_ref.at[:, pl.ds(0, big)]),
        (32, second, small, w_a_ref.at[:, pl.ds(big, small)]),
        (32, third, rest, w_b_ref),
    )
    copies = []
    for number, (tap, channel, count, place) in enumerate(cuts):
        source = w_up_ref.at[pl.ds(tap, 16), pl.ds(pl.multiple_of(channel, 16), count), side]
        copies.append(pltpu.make_async_copy(source, place, sems.at[number]))
        copies[-1].start()
    chans, rows, cols = own_ref.shape
    raw.wait()
    wide_ref[...] = raw_ref[...].astype(jnp.float32).reshape(chans * rows, cols)
    inner, outer = (1 - c) * (rows - 1), c * (rows - 1)
    near_ref[...] = wide_ref[pl.ds(inner, chans, stride=rows), :].astype(jnp.bfloat16)
    far_ref[...] = wide_ref[pl.ds(outer, chans, stride=rows), :].astype(jnp.bfloat16)
    share = peer_ref.shape[0]
    for place in range(share):
        row = wide_ref[pl.ds(place + (1 - c) * (rows - share), chans, stride=rows), :]
        peer_ref[place] = row.astype(jnp.bfloat16)
    for copy in copies:
        copy.wait()


def call_pieces(own, w_up):
    chans, rows, cols = own.shape
    part, cin = w_up.shape[1:]
    return pl.pallas_call(
        pieces,
        out_shape=(
            jax.ShapeDtypeStruct((chans, cols), jnp.bfloat16),
            jax.ShapeDtypeStruct((chans, cols), jnp.bfloat16),
            jax.ShapeDtypeStruct((rows // 2 + 1, chans, cols), jnp.bfloat16),
            jax.ShapeDtypeStruct((16, 3 * part // 4, cin // 2), jnp.bfloat16),
            jax.ShapeDtypeStruct((16, part // 2, cin // 2), jnp.bfloat16),
        ),
        in_specs=[ANY, ANY],
        out_specs=(VMEM,) * 5,
        scratch_shapes=[
            pltpu.VMEM((chans * rows, cols), jnp.float32),
            pltpu.VMEM((chans, rows, cols), jnp.bfloat16),
            pltpu.SemaphoreType.DMA((4,)),
        ],
        compiler_params=pltpu.CompilerParams(vmem_limit_bytes=LIMIT),
    )(in_hbm(own), in_hbm(w_up))


def in_hbm(operand):
    return pltpu.with_memory_space_constraint(operand, pltpu.HBM)


def cost(sizes):
    cin, cout, rows, cols = sizes
    flops = 2 * cout * 4 * cin * 2 * cols * (rows + 2) + 2 * 2 * cout * 9 * cout * 2 * cols * rows
    return pl.CostEstimate(flops=flops, bytes_accessed=8 * 2**20, transcendentals=0)


def call_prepare(paired, own, w_half, w_conv, sizes):
    cin, cout, rows, cols = sizes
    wide = own.shape[0] * own.shape[1] if paired else 8
    return pl.pallas_call(
        functools.partial(prepare, paired),
        out_shape=(
            jax.ShapeDtypeStruct((3, rows // 2 + 2, cin, cols), jnp.bfloat16),
            jax.ShapeDtypeStruct((32, cout // 2, cin), jnp.bfloat16),
            jax.ShapeDtypeStruct((2 * cout, 9 * cout), jnp.bfloat16),
            jax.ShapeDtypeStruct((2 * cout, 9 * cout), jnp.bfloat16),
        ),
        in_specs=[ANY] * 3,
        out_specs=(VMEM,) * 4,
        scratch_shapes=[
            pltpu.VMEM((2, 2 * cout, 9 * cout), jnp.bfloat16),
            pltpu.VMEM((27, cout, cout), jnp.bfloat16),
            pltpu.VMEM((wide, cols), jnp.float32),
            pltpu.VMEM(own.shape, jnp.bfloat16),
            pltpu.SemaphoreType.DMA((3,)),
        ],
        cost_estimate=pl.CostEstimate(flops=2 * 18 * 256 * cout * cout, bytes_accessed=8 * 2**20, transcendentals=0),
        compiler_params=pltpu.CompilerParams(vmem_limit_bytes=LIMIT),
    )(in_hbm(own), in_hbm(w_half), in_hbm(w_conv))


def call_first(body, rows_in, prepared, b_up, sizes):
    cin, cout, rows, cols = sizes
    started, w_half, kernel = prepared
    return pl.pallas_call(
        body,
        out_shape=(
            jax.ShapeDtypeStruct(started.shape, jnp.bfloat16),
            jax.ShapeDtypeStruct((2, 2 * cout, rows * cols), jnp.float32),
        ),
        in_specs=[VMEM] * (len(rows_in) + 4),
        out_specs=(VMEM,) * 2,
        scratch_shapes=[
            pltpu.VMEM((cout, cout), jnp.float32),
            pltpu.VMEM((4, rows + 2, cout, cols), jnp.bfloat16),
        ],
        input_output_aliases={len(rows_in): 0},
        cost_estimate=cost(sizes),
        compiler_params=pltpu.CompilerParams(vmem_limit_bytes=LIMIT),
    )(*rows_in, started, w_half, kernel, b_up)


def call_second(paired, parts, results, biases, sizes):
    cin, cout, rows, cols = sizes
    return pl.pallas_call(
        functools.partial(second, paired, len(parts)),
        out_shape=jax.ShapeDtypeStruct((cout, 2, rows, 2 * cols), jnp.bfloat16),
        in_specs=[VMEM] * (len(parts) + 5),
        out_specs=ANY,
        scratch_shapes=[
            pltpu.VMEM((cout, cout), jnp.float32),
            pltpu.VMEM((4, rows + 2, cout, cols), jnp.bfloat16),
            pltpu.VMEM((2, 2 * cout * rows, cols), jnp.float32),
            pltpu.VMEM((4, cout, rows, cols), jnp.bfloat16),
            pltpu.SemaphoreType.DMA((4,)),
        ],
        cost_estimate=cost(sizes),
        compiler_params=pltpu.CompilerParams(vmem_limit_bytes=LIMIT),
    )(*parts, *results, *biases)


def paired(inputs, w_up, b_up, w_conv, b_conv, sizes):
    spaces = lax.axis_size("space")
    s, c = lax.axis_index("space"), lax.axis_index("ch")
    chans, _, held, cols = inputs.shape

    def at(space, ch):
        return space * 2 + ch

    across = [(at(i, j), at(i, 1 - j)) for i in range(spaces) for j in (0, 1)]
    cores = [(at(i, j), at(i ^ 1, j)) for i in range(spaces) for j in (0, 1)]
    pairs = [(at(i, j), at(i ^ 2, j)) for i in range(spaces) for j in (0, 1)]
    chain = [(at(i - 1, 0), at(i, 0)) for i in range(1, spaces)]
    chain += [(at(i + 1, 1), at(i, 1)) for i in range(spaces - 1)]

    outer = [(t, t + 1) for t in range(1, 2 * spaces - 1, 2)]
    outer += [(j, i) for i, j in outer]

    own = inputs.reshape(chans, held, cols)
    near, far, peer, w_a, w_b = call_pieces(own, w_up)
    own, w_conv, peer, w_a, far, near, w_b = lax.optimization_barrier((own, w_conv, peer, w_a, far, near, w_b))
    peer = lax.ppermute(peer, AXES, across)
    w_a = lax.ppermute(w_a, AXES, across)
    far = lax.ppermute(far, AXES, outer)
    near = lax.ppermute(near, AXES, chain)
    x, w_half, kernel, other = call_prepare(True, own, w_up, w_conv, sizes)
    x, w_a, w_b, near, far = lax.optimization_barrier((x, w_a, w_b, near, far))
    w_b = lax.ppermute(w_b, AXES, across)
    w_ax = lax.ppermute(w_a, AXES, pairs)
    w_ac = lax.ppermute(w_a, AXES, cores)
    biases = (b_up[None], b_conv[None])
    x, total = call_first(paired_first, (peer, near, far), (x, w_half, kernel), biases[0], sizes)
    results = (x, total, other)
    w_b, w_ax, w_ac, *results = lax.optimization_barrier((w_b, w_ax, w_ac, *results))
    w_bc = lax.ppermute(w_b, AXES, cores)
    w_axc = lax.ppermute(w_ax, AXES, cores)
    return call_second(True, (w_a, w_ax, w_b, w_ac, w_axc, w_bc), results, biases, sizes)


def gathered(inputs, w_up, b_up, w_conv, b_conv, sizes):
    spaces, chs = lax.axis_size("space"), lax.axis_size("ch")
    c = lax.axis_index("ch")
    w_all = lax.all_gather(w_up[16:48], "ch", axis=1, tiled=True)
    part = w_all.shape[1] // 2
    rows = lax.all_gather(inputs[:, 0], "ch", axis=0, tiled=True).transpose(1, 0, 2)
    forward = [(i, i + 1) for i in range(spaces - 1)]
    backward = [(j, i) for i, j in forward]
    low = lax.ppermute(rows[-1:], "space", forward)
    high = lax.ppermute(rows[:1], "space", backward)
    rows = jnp.concatenate([low, rows, high], axis=0)
    share = inputs.shape[2] // chs
    rows = lax.dynamic_slice_in_dim(rows, c * share, share + 2, 0)
    biases = (b_up[None], b_conv[None])
    *prepared, other = call_prepare(False, rows, w_all[:, :part], w_conv, sizes)
    results = (*call_first(gathered_first, (), prepared, biases[0], sizes), other)
    return call_second(False, (w_all[:16, part:], w_all[16:, part:]), results, biases, sizes)


def local(inputs, w_up, b_up, w_conv, b_conv):
    chs = lax.axis_size("ch")
    sizes = (w_up.shape[2], w_conv.shape[1], 2 * inputs.shape[2] // chs, inputs.shape[3])
    plan = paired if chs == 2 and lax.axis_size("space") % 4 == 0 else gathered
    return plan(inputs, w_up, b_up, w_conv, b_conv, sizes)


def solution(mesh):
    return jax.shard_map(
        local,
        mesh=mesh,
        in_specs=(P("ch", None, "space", None), P(None, "ch", None), P(), P(), P()),
        out_specs=P(None, None, ("space", "ch"), None),
        check_vma=False,
    )
```

```python
import functools

import jax
import jax.numpy as jnp
from jax import lax
from jax.experimental import pallas as pl
from jax.experimental.pallas import tpu as pltpu
from jax.sharding import PartitionSpec as P

AXES = ("space", "ch")
PHASES = (((1, 0), (3, -1)), ((2, 0), (0, 1)))
COLUMNS = ((3, 0, 1), (0, 1, 2))
VMEM = pl.BlockSpec(memory_space=pltpu.VMEM)
ANY = pl.BlockSpec(memory_space=pl.ANY)
LIMIT = 40 * 2**20


def column_of(bias):
    lanes = bias.shape[-1]
    return jnp.transpose(jnp.broadcast_to(bias, (lanes, lanes)))


def shifted(value, step):
    cols = value.shape[1]
    place = lax.broadcasted_iota(jnp.int32, value.shape, 1)
    edge = 0 if step == 1 else cols - 1
    return jnp.where(place == edge, 0.0, pltpu.roll(value, step % cols, 1))


def upsample(cell, tap_of, bias, u_ref, first, last):
    held, cols = u_ref.shape[1], u_ref.shape[3]
    for row_phase in (0, 1):
        for col_phase in (0, 1):
            taps = []
            for row_tap, row_shift in PHASES[row_phase]:
                for col_tap, col_shift in PHASES[col_phase]:
                    slot = row_shift + 1 - row_phase
                    taps.append((row_tap * 4 + col_tap, slot, col_shift % 3))
            kernel = jnp.concatenate([tap_of(tap) for tap, _, _ in taps], axis=1)
            for start in range(0, held // 2, 2):
                places = range(start, min(start + 2, held // 2))
                cells = jnp.concatenate(
                    [
                        jnp.concatenate([cell(copy, slot + place) for place in places], axis=1)
                        for _, slot, copy in taps
                    ],
                    axis=0,
                )
                summed = jnp.dot(kernel, cells, preferred_element_type=jnp.float32)
                for number, place in enumerate(places):
                    row = 2 * place + 1 - row_phase
                    value = summed[:, number * cols : (number + 1) * cols] + bias
                    value = jnp.maximum(value, 0.2 * value)
                    if row == 0:
                        value = jnp.where(first, 0.0, value)
                    if row == held - 1:
                        value = jnp.where(last, 0.0, value)
                    u_ref[col_phase, row] = value.astype(jnp.bfloat16)
                    moved = shifted(value, -1 if col_phase == 0 else 1)
                    u_ref[2 + col_phase, row] = moved.astype(jnp.bfloat16)


def convolve(kernel, u_ref, start, col_phase):
    cells = jnp.concatenate(
        [
            jnp.concatenate([u_ref[copy, start + row_tap], u_ref[copy, start + row_tap + 1]], 1)
            for row_tap in range(3)
            for copy in COLUMNS[col_phase]
        ],
        axis=0,
    )
    return jnp.dot(kernel, cells, preferred_element_type=jnp.float32)


def split_kernels(w_conv_ref, halves_ref):
    cout = w_conv_ref.shape[1]
    part = cout // 2
    low = lax.broadcasted_iota(jnp.int32, (cout, cout), 1) < part
    for row_tap in range(3):
        for col_tap in range(3):
            taps = [w_conv_ref[a * 9 + row_tap * 3 + col_tap].astype(jnp.float32) for a in range(3)]
            turned = [pltpu.roll(tap, part, 1) for tap in taps]
            columns = pl.ds((row_tap * 3 + col_tap) * cout, cout)
            for plane in (0, 1):
                near, far = 1 - plane, 2 - plane
                rows = pl.ds(plane * cout, cout)
                halves_ref[0, rows, columns] = jnp.where(low, taps[near], turned[far]).astype(jnp.bfloat16)
                halves_ref[1, rows, columns] = jnp.where(low, turned[near], taps[far]).astype(jnp.bfloat16)


def bias_of(bias_ref, column_ref, blocks):
    column_ref[...] = column_of(bias_ref[...])
    return jnp.concatenate([column_ref[pl.ds(pl.multiple_of(at, 16), size)] for at, size in blocks], axis=0)


def ends(s, c):
    first = (s == 0) & (c == 0)
    last = (s == lax.axis_size("space") - 1) & (c == lax.axis_size("ch") - 1)
    return first, last


def store_row(x_ref, slot, offset, value):
    where = pl.ds(pl.multiple_of(offset, 16), value.shape[0])
    x_ref[0, slot, where] = value.astype(jnp.bfloat16)
    x_ref[1, slot, where] = shifted(value, -1).astype(jnp.bfloat16)
    x_ref[2, slot, where] = shifted(value, 1).astype(jnp.bfloat16)


def arrival(x, part):
    if x is None:
        return [[(0, part)], [(0, part)]]
    quarter, half = part // 4, part // 2
    return [
        [(x * half, half), ((1 - x) * half, half)],
        [(x * quarter, quarter), ((1 - x) * quarter, quarter), (half, half)],
    ]


def arrange(x, part):
    source = lax.broadcasted_iota(jnp.int32, (2 * part, 2 * part), 0)
    target = lax.broadcasted_iota(jnp.int32, (2 * part, 2 * part), 1)
    wanted = jnp.zeros_like(target)
    for plane, blocks in enumerate(arrival(x, part)):
        place = plane * part
        for first, size in blocks:
            inside = (target >= place) & (target < place + size)
            wanted = jnp.where(inside, target - place + plane * part + first, wanted)
            place += size
    return jnp.where(source == wanted, 1.0, 0.0).astype(jnp.bfloat16)


def own_part(half, refs, results, scratch):
    w_half_ref, kernel_ref, b_up_ref = refs
    x_ref, sum_ref = results
    column_ref, u_ref = scratch
    s, c = lax.axis_index("space"), lax.axis_index("ch")
    part, cols = w_half_ref.shape[1], u_ref.shape[3]

    def tap_of(tap):
        return jnp.concatenate([w_half_ref[tap], w_half_ref[16 + tap]], axis=0)

    bias = bias_of(b_up_ref, column_ref, [(half * part, part)] * 2)
    upsample(lambda copy, slot: x_ref[copy, slot], tap_of, bias, u_ref, *ends(s, c))
    kernel = kernel_ref[...]
    for start in range(0, u_ref.shape[1] - 2, 2):
        for col_phase in (0, 1):
            sum_ref[col_phase, :, start * cols : (start + 2) * cols] = convolve(kernel, u_ref, start, col_phase)


def prepare(paired, own_ref, w_half_ref, w_conv_ref, x_ref, w_ref, kernel_ref, other_ref, *scratch):
    halves_ref, v_ref, wide_ref, raw_ref, sems = scratch
    s, c = lax.axis_index("space"), lax.axis_index("ch")
    skipped = (w_half_ref.shape[0] - 32) // 2
    copies = [
        pltpu.make_async_copy(own_ref, raw_ref, sems.at[0]),
        pltpu.make_async_copy(w_conv_ref, v_ref, sems.at[1]),
        pltpu.make_async_copy(w_half_ref.at[pl.ds(skipped, 32)], w_ref, sems.at[2]),
    ]
    for copy in copies:
        copy.start()
    copies[0].wait()
    if paired:
        chans, rows, cols = own_ref.shape
        wide_ref[...] = raw_ref[...].astype(jnp.float32).reshape(chans * rows, cols)
        share = x_ref.shape[1] - 1
        for place in range(share):
            value = wide_ref[pl.ds(place + c * (rows - share), chans, stride=rows), :]
            store_row(x_ref, place + 1 - c, c * chans, value)
    else:
        for slot in range(own_ref.shape[0]):
            store_row(x_ref, slot, 0, raw_ref[slot].astype(jnp.float32))
    cout = w_conv_ref.shape[1]
    half, x = (c, lax.rem(s, 4) // 2) if paired else (0, None)
    copies[1].wait()
    split_kernels(v_ref, halves_ref)
    kernel_ref[...] = halves_ref[half]
    matrix = arrange(x, cout // 2)
    for number in range(9):
        columns = pl.ds(number * cout, cout)
        moved = jnp.dot(halves_ref[1 - half, :, columns], matrix, preferred_element_type=jnp.float32)
        other_ref[:, columns] = moved.astype(jnp.bfloat16)
    copies[2].wait()


def paired_first(peer_ref, near_ref, far_ref, started_ref, *refs):
    refs, results, scratch = refs[:3], refs[3:5], refs[5:]
    x_ref = results[0]
    c = lax.axis_index("ch")
    share, chans, _ = peer_ref.shape
    for place in range(share):
        store_row(x_ref, place + 1 - c, (1 - c) * chans, peer_ref[place].astype(jnp.float32))
    slot = c * (x_ref.shape[1] - 1)
    store_row(x_ref, slot, c * chans, near_ref[...].astype(jnp.float32))
    store_row(x_ref, slot, (1 - c) * chans, far_ref[...].astype(jnp.float32))
    own_part(c, refs, results, scratch)


def gathered_first(started_ref, *refs):
    own_part(0, refs[:3], refs[3:5], refs[5:])


def second(paired, count, *refs):
    parts, refs = refs[:count], refs[count:]
    x_ref, sum_ref, other_ref, b_up_ref, b_conv_ref, out_ref, column_ref, u_ref, total_ref, made_ref, sems = refs
    s, c = lax.axis_index("space"), lax.axis_index("ch")
    cout, _, rows, _ = out_ref.shape
    part = cout // 2
    half, x = (1 - c, lax.rem(s, 4) // 2) if paired else (1, None)
    cols = x_ref.shape[3]
    if paired:
        chans = x_ref.shape[2] // 2
        core = lax.rem(s, 2)
        sides = [pl.ds(pl.multiple_of(side * chans, 16), chans) for side in (core, 1 - core)]
        big = part // 2

        def tap_of(tap):
            columns = []
            for near_ref, far_ref, rest_ref in (parts[:3], parts[3:]):
                rows = [near_ref[tap, :big], far_ref[tap, :big], near_ref[tap, big:], far_ref[tap, big:], rest_ref[tap]]
                columns.append(jnp.concatenate(rows, axis=0))
            return jnp.concatenate(columns, axis=1)

        def cell(copy, slot):
            return jnp.concatenate([x_ref[copy, slot, side] for side in sides], axis=0)
    else:

        def tap_of(tap):
            return jnp.concatenate([part_ref[tap] for part_ref in parts], axis=0)

        def cell(copy, slot):
            return x_ref[copy, slot]

    blocks = [(half * part + at, size) for plane in arrival(x, part) for at, size in plane]
    bias = bias_of(b_up_ref, column_ref, blocks)
    upsample(cell, tap_of, bias, u_ref, *ends(s, c))
    source = lax.broadcasted_iota(jnp.int32, (2 * cols, 2 * cols), 0)
    target = lax.broadcasted_iota(jnp.int32, (2 * cols, 2 * cols), 1)
    wanted = jnp.where(source < cols, 2 * source, 2 * (source - cols) + 1)
    interleave = jnp.where(wanted == target, 1.0, 0.0).astype(jnp.bfloat16)
    kernel = other_ref[...]
    bias = column_of(b_conv_ref[...])
    bias = jnp.concatenate([bias, bias], axis=0)
    for start in range(0, rows, 2):
        halves = [
            convolve(kernel, u_ref, start, col_phase) + sum_ref[col_phase, :, start * cols : (start + 2) * cols]
            for col_phase in (0, 1)
        ]
        for number in (0, 1):
            pair = [
                (half[:, number * cols : (number + 1) * cols] + bias).astype(jnp.bfloat16) for half in halves
            ]
            mixed = jnp.dot(jnp.concatenate(pair, axis=1), interleave, preferred_element_type=jnp.float32)
            for side in (0, 1):
                total_ref[side, pl.ds(start + number, 2 * cout, stride=rows), :] = mixed[
                    :, side * cols : (side + 1) * cols
                ]
    copies = []
    for plane in (0, 1):
        for side in (0, 1):
            number = 2 * plane + side
            block = total_ref[side, pl.ds(plane * cout * rows, cout * rows), :]
            made_ref[number] = block.reshape(cout, rows, cols).astype(jnp.bfloat16)
            place = out_ref.at[:, plane, :, pl.ds(side * cols, cols)]
            copies.append(pltpu.make_async_copy(made_ref.at[number], place, sems.at[number]))
            copies[-1].start()
    for copy in copies:
        copy.wait()


def pieces(own_ref, w_up_ref, near_ref, far_ref, peer_ref, w_a_ref, w_b_ref, wide_ref, raw_ref, sems):
    s, c = lax.axis_index("space"), lax.axis_index("ch")
    raw = pltpu.make_async_copy(own_ref, raw_ref, sems.at[3])
    raw.start()
    me = lax.rem(s, 4)
    part, lanes = w_up_ref.shape[1], w_a_ref.shape[2]
    side = pl.ds(pl.multiple_of(lax.rem(me, 2) * lanes, lanes), lanes)
    (first, big), = arrival(me // 2, part)[0][:1]
    (second, small), _, (third, rest) = arrival(me // 2, part)[1]
    cuts = (
        (16, first, big, w_a_ref.at[:, pl.ds(0, big)]),
        (32, second, small, w_a_ref.at[:, pl.ds(big, small)]),
        (32, third, rest, w_b_ref),
    )
    copies = []
    for number, (tap, channel, count, place) in enumerate(cuts):
        source = w_up_ref.at[pl.ds(tap, 16), pl.ds(pl.multiple_of(channel, 16), count), side]
        copies.append(pltpu.make_async_copy(source, place, sems.at[number]))
        copies[-1].start()
    chans, rows, cols = own_ref.shape
    raw.wait()
    wide_ref[...] = raw_ref[...].astype(jnp.float32).reshape(chans * rows, cols)
    inner, outer = (1 - c) * (rows - 1), c * (rows - 1)
    near_ref[...] = wide_ref[pl.ds(inner, chans, stride=rows), :].astype(jnp.bfloat16)
    far_ref[...] = wide_ref[pl.ds(outer, chans, stride=rows), :].astype(jnp.bfloat16)
    share = peer_ref.shape[0]
    for place in range(share):
        row = wide_ref[pl.ds(place + (1 - c) * (rows - share), chans, stride=rows), :]
        peer_ref[place] = row.astype(jnp.bfloat16)
    for copy in copies:
        copy.wait()


def call_pieces(own, w_up):
    chans, rows, cols = own.shape
    part, cin = w_up.shape[1:]
    return pl.pallas_call(
        pieces,
        out_shape=(
            jax.ShapeDtypeStruct((chans, cols), jnp.bfloat16),
            jax.ShapeDtypeStruct((chans, cols), jnp.bfloat16),
            jax.ShapeDtypeStruct((rows // 2 + 1, chans, cols), jnp.bfloat16),
            jax.ShapeDtypeStruct((16, 3 * part // 4, cin // 2), jnp.bfloat16),
            jax.ShapeDtypeStruct((16, part // 2, cin // 2), jnp.bfloat16),
        ),
        in_specs=[ANY, ANY],
        out_specs=(VMEM,) * 5,
        scratch_shapes=[
            pltpu.VMEM((chans * rows, cols), jnp.float32),
            pltpu.VMEM((chans, rows, cols), jnp.bfloat16),
            pltpu.SemaphoreType.DMA((4,)),
        ],
        compiler_params=pltpu.CompilerParams(vmem_limit_bytes=LIMIT),
    )(in_hbm(own), in_hbm(w_up))


def in_hbm(operand):
    return pltpu.with_memory_space_constraint(operand, pltpu.HBM)


def cost(sizes):
    cin, cout, rows, cols = sizes
    flops = 2 * cout * 4 * cin * 2 * cols * (rows + 2) + 2 * 2 * cout * 9 * cout * 2 * cols * rows
    return pl.CostEstimate(flops=flops, bytes_accessed=8 * 2**20, transcendentals=0)


def call_prepare(paired, own, w_half, w_conv, sizes):
    cin, cout, rows, cols = sizes
    wide = own.shape[0] * own.shape[1] if paired else 8
    return pl.pallas_call(
        functools.partial(prepare, paired),
        out_shape=(
            jax.ShapeDtypeStruct((3, rows // 2 + 2, cin, cols), jnp.bfloat16),
            jax.ShapeDtypeStruct((32, cout // 2, cin), jnp.bfloat16),
            jax.ShapeDtypeStruct((2 * cout, 9 * cout), jnp.bfloat16),
            jax.ShapeDtypeStruct((2 * cout, 9 * cout), jnp.bfloat16),
        ),
        in_specs=[ANY] * 3,
        out_specs=(VMEM,) * 4,
        scratch_shapes=[
            pltpu.VMEM((2, 2 * cout, 9 * cout), jnp.bfloat16),
            pltpu.VMEM((27, cout, cout), jnp.bfloat16),
            pltpu.VMEM((wide, cols), jnp.float32),
            pltpu.VMEM(own.shape, jnp.bfloat16),
            pltpu.SemaphoreType.DMA((3,)),
        ],
        cost_estimate=pl.CostEstimate(flops=2 * 18 * 256 * cout * cout, bytes_accessed=8 * 2**20, transcendentals=0),
        compiler_params=pltpu.CompilerParams(vmem_limit_bytes=LIMIT),
    )(in_hbm(own), in_hbm(w_half), in_hbm(w_conv))


def call_first(body, rows_in, prepared, b_up, sizes):
    cin, cout, rows, cols = sizes
    started, w_half, kernel = prepared
    return pl.pallas_call(
        body,
        out_shape=(
            jax.ShapeDtypeStruct(started.shape, jnp.bfloat16),
            jax.ShapeDtypeStruct((2, 2 * cout, rows * cols), jnp.float32),
        ),
        in_specs=[VMEM] * (len(rows_in) + 4),
        out_specs=(VMEM,) * 2,
        scratch_shapes=[
            pltpu.VMEM((cout, cout), jnp.float32),
            pltpu.VMEM((4, rows + 2, cout, cols), jnp.bfloat16),
        ],
        input_output_aliases={len(rows_in): 0},
        cost_estimate=cost(sizes),
        compiler_params=pltpu.CompilerParams(vmem_limit_bytes=LIMIT),
    )(*rows_in, started, w_half, kernel, b_up)


def call_second(paired, parts, results, biases, sizes):
    cin, cout, rows, cols = sizes
    return pl.pallas_call(
        functools.partial(second, paired, len(parts)),
        out_shape=jax.ShapeDtypeStruct((cout, 2, rows, 2 * cols), jnp.bfloat16),
        in_specs=[VMEM] * (len(parts) + 5),
        out_specs=ANY,
        scratch_shapes=[
            pltpu.VMEM((cout, cout), jnp.float32),
            pltpu.VMEM((4, rows + 2, cout, cols), jnp.bfloat16),
            pltpu.VMEM((2, 2 * cout * rows, cols), jnp.float32),
            pltpu.VMEM((4, cout, rows, cols), jnp.bfloat16),
            pltpu.SemaphoreType.DMA((4,)),
        ],
        cost_estimate=cost(sizes),
        compiler_params=pltpu.CompilerParams(vmem_limit_bytes=LIMIT),
    )(*parts, *results, *biases)


def paired(inputs, w_up, b_up, w_conv, b_conv, sizes):
    spaces = lax.axis_size("space")
    s, c = lax.axis_index("space"), lax.axis_index("ch")
    chans, _, held, cols = inputs.shape

    def at(space, ch):
        return space * 2 + ch

    across = [(at(i, j), at(i, 1 - j)) for i in range(spaces) for j in (0, 1)]
    cores = [(at(i, j), at(i ^ 1, j)) for i in range(spaces) for j in (0, 1)]
    pairs = [(at(i, j), at(i ^ 2, j)) for i in range(spaces) for j in (0, 1)]
    chain = [(at(i - 1, 0), at(i, 0)) for i in range(1, spaces)]
    chain += [(at(i + 1, 1), at(i, 1)) for i in range(spaces - 1)]

    outer = [(t, t + 1) for t in range(1, 2 * spaces - 1, 2)]
    outer += [(j, i) for i, j in outer]

    own = inputs.reshape(chans, held, cols)
    near, far, peer, w_a, w_b = call_pieces(own, w_up)
    own, w_conv, peer, w_a, far, near, w_b = lax.optimization_barrier((own, w_conv, peer, w_a, far, near, w_b))
    peer = lax.ppermute(peer, AXES, across)
    w_a = lax.ppermute(w_a, AXES, across)
    far = lax.ppermute(far, AXES, outer)
    near = lax.ppermute(near, AXES, chain)
    w_a, w_b, own, w_conv = lax.optimization_barrier((w_a, w_b, own, w_conv))
    w_ax = lax.ppermute(w_a, AXES, pairs)
    w_b = lax.ppermute(w_b, AXES, across)
    w_ac = lax.ppermute(w_a, AXES, cores)
    x, w_half, kernel, other = call_prepare(True, own, w_up, w_conv, sizes)
    biases = (b_up[None], b_conv[None])
    x, total = call_first(paired_first, (peer, near, far), (x, w_half, kernel), biases[0], sizes)
    results = (x, total, other)
    w_b, w_ax, w_ac, *results = lax.optimization_barrier((w_b, w_ax, w_ac, *results))
    w_bc = lax.ppermute(w_b, AXES, cores)
    w_axc = lax.ppermute(w_ax, AXES, cores)
    return call_second(True, (w_a, w_ax, w_b, w_ac, w_axc, w_bc), results, biases, sizes)


def gathered(inputs, w_up, b_up, w_conv, b_conv, sizes):
    spaces, chs = lax.axis_size("space"), lax.axis_size("ch")
    c = lax.axis_index("ch")
    w_all = lax.all_gather(w_up[16:48], "ch", axis=1, tiled=True)
    part = w_all.shape[1] // 2
    rows = lax.all_gather(inputs[:, 0], "ch", axis=0, tiled=True).transpose(1, 0, 2)
    forward = [(i, i + 1) for i in range(spaces - 1)]
    backward = [(j, i) for i, j in forward]
    low = lax.ppermute(rows[-1:], "space", forward)
    high = lax.ppermute(rows[:1], "space", backward)
    rows = jnp.concatenate([low, rows, high], axis=0)
    share = inputs.shape[2] // chs
    rows = lax.dynamic_slice_in_dim(rows, c * share, share + 2, 0)
    biases = (b_up[None], b_conv[None])
    *prepared, other = call_prepare(False, rows, w_all[:, :part], w_conv, sizes)
    results = (*call_first(gathered_first, (), prepared, biases[0], sizes), other)
    return call_second(False, (w_all[:16, part:], w_all[16:, part:]), results, biases, sizes)


def local(inputs, w_up, b_up, w_conv, b_conv):
    chs = lax.axis_size("ch")
    sizes = (w_up.shape[2], w_conv.shape[1], 2 * inputs.shape[2] // chs, inputs.shape[3])
    plan = paired if chs == 2 and lax.axis_size("space") % 4 == 0 else gathered
    return plan(inputs, w_up, b_up, w_conv, b_conv, sizes)


def solution(mesh):
    return jax.shard_map(
        local,
        mesh=mesh,
        in_specs=(P("ch", None, "space", None), P(None, "ch", None), P(), P(), P()),
        out_specs=P(None, None, ("space", "ch"), None),
        check_vma=False,
    )
```

```python
import functools

import jax
import jax.numpy as jnp
from jax import lax
from jax.experimental import pallas as pl
from jax.experimental.pallas import tpu as pltpu
from jax.sharding import PartitionSpec as P

AXES = ("space", "ch")
PHASES = (((1, 0), (3, -1)), ((2, 0), (0, 1)))
COLUMNS = ((3, 0, 1), (0, 1, 2))
VMEM = pl.BlockSpec(memory_space=pltpu.VMEM)
ANY = pl.BlockSpec(memory_space=pl.ANY)
LIMIT = 40 * 2**20


def column_of(bias):
    lanes = bias.shape[-1]
    return jnp.transpose(jnp.broadcast_to(bias, (lanes, lanes)))


def shifted(value, step):
    cols = value.shape[1]
    place = lax.broadcasted_iota(jnp.int32, value.shape, 1)
    edge = 0 if step == 1 else cols - 1
    return jnp.where(place == edge, 0.0, pltpu.roll(value, step % cols, 1))


def upsample(cell, tap_of, bias, u_ref, first, last):
    held, cols = u_ref.shape[1], u_ref.shape[3]
    for row_phase in (0, 1):
        for col_phase in (0, 1):
            taps = []
            for row_tap, row_shift in PHASES[row_phase]:
                for col_tap, col_shift in PHASES[col_phase]:
                    slot = row_shift + 1 - row_phase
                    taps.append((row_tap * 4 + col_tap, slot, col_shift % 3))
            kernel = jnp.concatenate([tap_of(tap) for tap, _, _ in taps], axis=1)
            for start in range(0, held // 2, 2):
                places = range(start, min(start + 2, held // 2))
                cells = jnp.concatenate(
                    [
                        jnp.concatenate([cell(copy, slot + place) for place in places], axis=1)
                        for _, slot, copy in taps
                    ],
                    axis=0,
                )
                summed = jnp.dot(kernel, cells, preferred_element_type=jnp.float32)
                for number, place in enumerate(places):
                    row = 2 * place + 1 - row_phase
                    value = summed[:, number * cols : (number + 1) * cols] + bias
                    value = jnp.maximum(value, 0.2 * value)
                    if row == 0:
                        value = jnp.where(first, 0.0, value)
                    if row == held - 1:
                        value = jnp.where(last, 0.0, value)
                    u_ref[col_phase, row] = value.astype(jnp.bfloat16)
                    moved = shifted(value, -1 if col_phase == 0 else 1)
                    u_ref[2 + col_phase, row] = moved.astype(jnp.bfloat16)


def convolve(kernel, u_ref, start, col_phase):
    cells = jnp.concatenate(
        [
            jnp.concatenate([u_ref[copy, start + row_tap], u_ref[copy, start + row_tap + 1]], 1)
            for row_tap in range(3)
            for copy in COLUMNS[col_phase]
        ],
        axis=0,
    )
    return jnp.dot(kernel, cells, preferred_element_type=jnp.float32)


def split_kernels(w_conv_ref, halves_ref):
    cout = w_conv_ref.shape[1]
    part = cout // 2
    low = lax.broadcasted_iota(jnp.int32, (cout, cout), 1) < part
    for row_tap in range(3):
        for col_tap in range(3):
            taps = [w_conv_ref[a * 9 + row_tap * 3 + col_tap].astype(jnp.float32) for a in range(3)]
            turned = [pltpu.roll(tap, part, 1) for tap in taps]
            columns = pl.ds((row_tap * 3 + col_tap) * cout, cout)
            for plane in (0, 1):
                near, far = 1 - plane, 2 - plane
                rows = pl.ds(plane * cout, cout)
                halves_ref[0, rows, columns] = jnp.where(low, taps[near], turned[far]).astype(jnp.bfloat16)
                halves_ref[1, rows, columns] = jnp.where(low, turned[near], taps[far]).astype(jnp.bfloat16)


def bias_of(bias_ref, column_ref, blocks):
    column_ref[...] = column_of(bias_ref[...])
    return jnp.concatenate([column_ref[pl.ds(pl.multiple_of(at, 16), size)] for at, size in blocks], axis=0)


def ends(s, c):
    first = (s == 0) & (c == 0)
    last = (s == lax.axis_size("space") - 1) & (c == lax.axis_size("ch") - 1)
    return first, last


def store_row(x_ref, slot, offset, value):
    where = pl.ds(pl.multiple_of(offset, 16), value.shape[0])
    x_ref[0, slot, where] = value.astype(jnp.bfloat16)
    x_ref[1, slot, where] = shifted(value, -1).astype(jnp.bfloat16)
    x_ref[2, slot, where] = shifted(value, 1).astype(jnp.bfloat16)


def arrival(x, part):
    if x is None:
        return [[(0, part)], [(0, part)]]
    half = part // 2
    return [[(x * half, half), ((1 - x) * half, half)]] * 2


def arrange(x, part):
    source = lax.broadcasted_iota(jnp.int32, (2 * part, 2 * part), 0)
    target = lax.broadcasted_iota(jnp.int32, (2 * part, 2 * part), 1)
    wanted = jnp.zeros_like(target)
    for plane, blocks in enumerate(arrival(x, part)):
        place = plane * part
        for first, size in blocks:
            inside = (target >= place) & (target < place + size)
            wanted = jnp.where(inside, target - place + plane * part + first, wanted)
            place += size
    return jnp.where(source == wanted, 1.0, 0.0).astype(jnp.bfloat16)


def own_part(half, refs, results, scratch):
    w_half_ref, kernel_ref, b_up_ref = refs
    x_ref, sum_ref = results
    column_ref, u_ref = scratch
    s, c = lax.axis_index("space"), lax.axis_index("ch")
    part, cols = w_half_ref.shape[1], u_ref.shape[3]

    def tap_of(tap):
        return jnp.concatenate([w_half_ref[tap], w_half_ref[16 + tap]], axis=0)

    bias = bias_of(b_up_ref, column_ref, [(half * part, part)] * 2)
    upsample(lambda copy, slot: x_ref[copy, slot], tap_of, bias, u_ref, *ends(s, c))
    kernel = kernel_ref[...]
    for start in range(0, u_ref.shape[1] - 2, 2):
        for col_phase in (0, 1):
            sum_ref[col_phase, :, start * cols : (start + 2) * cols] = convolve(kernel, u_ref, start, col_phase)


def prepare(paired, own_ref, w_half_ref, w_conv_ref, x_ref, w_ref, kernel_ref, other_ref, *scratch):
    halves_ref, v_ref, wide_ref, raw_ref, sems = scratch
    s, c = lax.axis_index("space"), lax.axis_index("ch")
    skipped = (w_half_ref.shape[0] - 32) // 2
    copies = [
        pltpu.make_async_copy(own_ref, raw_ref, sems.at[0]),
        pltpu.make_async_copy(w_conv_ref, v_ref, sems.at[1]),
        pltpu.make_async_copy(w_half_ref.at[pl.ds(skipped, 32)], w_ref, sems.at[2]),
    ]
    for copy in copies:
        copy.start()
    copies[0].wait()
    if paired:
        chans, rows, cols = own_ref.shape
        wide_ref[...] = raw_ref[...].astype(jnp.float32).reshape(chans * rows, cols)
        share = x_ref.shape[1] - 1
        for place in range(share):
            value = wide_ref[pl.ds(place + c * (rows - share), chans, stride=rows), :]
            store_row(x_ref, place + 1 - c, c * chans, value)
    else:
        for slot in range(own_ref.shape[0]):
            store_row(x_ref, slot, 0, raw_ref[slot].astype(jnp.float32))
    cout = w_conv_ref.shape[1]
    half, x = (c, lax.rem(s, 4) // 2) if paired else (0, None)
    copies[1].wait()
    split_kernels(v_ref, halves_ref)
    kernel_ref[...] = halves_ref[half]
    matrix = arrange(x, cout // 2)
    for number in range(9):
        columns = pl.ds(number * cout, cout)
        moved = jnp.dot(halves_ref[1 - half, :, columns], matrix, preferred_element_type=jnp.float32)
        other_ref[:, columns] = moved.astype(jnp.bfloat16)
    copies[2].wait()


def paired_first(peer_ref, near_ref, far_ref, started_ref, *refs):
    refs, results, scratch = refs[:3], refs[3:5], refs[5:]
    x_ref = results[0]
    c = lax.axis_index("ch")
    share, chans, _ = peer_ref.shape
    for place in range(share):
        store_row(x_ref, place + 1 - c, (1 - c) * chans, peer_ref[place].astype(jnp.float32))
    slot = c * (x_ref.shape[1] - 1)
    store_row(x_ref, slot, c * chans, near_ref[...].astype(jnp.float32))
    store_row(x_ref, slot, (1 - c) * chans, far_ref[...].astype(jnp.float32))
    own_part(c, refs, results, scratch)


def gathered_first(started_ref, *refs):
    own_part(0, refs[:3], refs[3:5], refs[5:])


def second(paired, count, *refs):
    parts, refs = refs[:count], refs[count:]
    x_ref, sum_ref, other_ref, b_up_ref, b_conv_ref, out_ref, column_ref, u_ref, total_ref, made_ref, sems = refs
    s, c = lax.axis_index("space"), lax.axis_index("ch")
    cout, _, rows, _ = out_ref.shape
    part = cout // 2
    half, x = (1 - c, lax.rem(s, 4) // 2) if paired else (1, None)
    cols = x_ref.shape[3]
    if paired:
        chans = x_ref.shape[2] // 2
        core = lax.rem(s, 2)
        sides = [pl.ds(pl.multiple_of(side * chans, 16), chans) for side in (core, 1 - core)]
        big = part // 2

        def tap_of(tap):
            columns = []
            for near_ref, far_ref in (parts[:2], parts[2:]):
                rows = [near_ref[tap, :big], far_ref[tap, :big], near_ref[tap, big:], far_ref[tap, big:]]
                columns.append(jnp.concatenate(rows, axis=0))
            return jnp.concatenate(columns, axis=1)

        def cell(copy, slot):
            return jnp.concatenate([x_ref[copy, slot, side] for side in sides], axis=0)
    else:

        def tap_of(tap):
            return jnp.concatenate([part_ref[tap] for part_ref in parts], axis=0)

        def cell(copy, slot):
            return x_ref[copy, slot]

    blocks = [(half * part + at, size) for plane in arrival(x, part) for at, size in plane]
    bias = bias_of(b_up_ref, column_ref, blocks)
    upsample(cell, tap_of, bias, u_ref, *ends(s, c))
    source = lax.broadcasted_iota(jnp.int32, (2 * cols, 2 * cols), 0)
    target = lax.broadcasted_iota(jnp.int32, (2 * cols, 2 * cols), 1)
    wanted = jnp.where(source < cols, 2 * source, 2 * (source - cols) + 1)
    interleave = jnp.where(wanted == target, 1.0, 0.0).astype(jnp.bfloat16)
    kernel = other_ref[...]
    bias = column_of(b_conv_ref[...])
    bias = jnp.concatenate([bias, bias], axis=0)
    for start in range(0, rows, 2):
        halves = [
            convolve(kernel, u_ref, start, col_phase) + sum_ref[col_phase, :, start * cols : (start + 2) * cols]
            for col_phase in (0, 1)
        ]
        for number in (0, 1):
            pair = [
                (half[:, number * cols : (number + 1) * cols] + bias).astype(jnp.bfloat16) for half in halves
            ]
            mixed = jnp.dot(jnp.concatenate(pair, axis=1), interleave, preferred_element_type=jnp.float32)
            for side in (0, 1):
                total_ref[side, pl.ds(start + number, 2 * cout, stride=rows), :] = mixed[
                    :, side * cols : (side + 1) * cols
                ]
    copies = []
    for plane in (0, 1):
        for side in (0, 1):
            number = 2 * plane + side
            block = total_ref[side, pl.ds(plane * cout * rows, cout * rows), :]
            made_ref[number] = block.reshape(cout, rows, cols).astype(jnp.bfloat16)
            place = out_ref.at[:, plane, :, pl.ds(side * cols, cols)]
            copies.append(pltpu.make_async_copy(made_ref.at[number], place, sems.at[number]))
            copies[-1].start()
    for copy in copies:
        copy.wait()


def pieces(own_ref, w_up_ref, near_ref, far_ref, peer_ref, w_a_ref, wide_ref, raw_ref, sems):
    s, c = lax.axis_index("space"), lax.axis_index("ch")
    raw = pltpu.make_async_copy(own_ref, raw_ref, sems.at[3])
    raw.start()
    me = lax.rem(s, 4)
    part, lanes = w_up_ref.shape[1], w_a_ref.shape[2]
    side = pl.ds(pl.multiple_of(lax.rem(me, 2) * lanes, lanes), lanes)
    cuts = [
        (16 + 16 * plane, *blocks[0], w_a_ref.at[:, pl.ds(plane * blocks[0][1], blocks[0][1])])
        for plane, blocks in enumerate(arrival(me // 2, part))
    ]
    copies = []
    for number, (tap, channel, count, place) in enumerate(cuts):
        source = w_up_ref.at[pl.ds(tap, 16), pl.ds(pl.multiple_of(channel, 16), count), side]
        copies.append(pltpu.make_async_copy(source, place, sems.at[number]))
        copies[-1].start()
    chans, rows, cols = own_ref.shape
    raw.wait()
    wide_ref[...] = raw_ref[...].astype(jnp.float32).reshape(chans * rows, cols)
    inner, outer = (1 - c) * (rows - 1), c * (rows - 1)
    near_ref[...] = wide_ref[pl.ds(inner, chans, stride=rows), :].astype(jnp.bfloat16)
    far_ref[...] = wide_ref[pl.ds(outer, chans, stride=rows), :].astype(jnp.bfloat16)
    share = peer_ref.shape[0]
    for place in range(share):
        row = wide_ref[pl.ds(place + (1 - c) * (rows - share), chans, stride=rows), :]
        peer_ref[place] = row.astype(jnp.bfloat16)
    for copy in copies:
        copy.wait()


def call_pieces(own, w_up):
    chans, rows, cols = own.shape
    part, cin = w_up.shape[1:]
    return pl.pallas_call(
        pieces,
        out_shape=(
            jax.ShapeDtypeStruct((chans, cols), jnp.bfloat16),
            jax.ShapeDtypeStruct((chans, cols), jnp.bfloat16),
            jax.ShapeDtypeStruct((rows // 2 + 1, chans, cols), jnp.bfloat16),
            jax.ShapeDtypeStruct((16, part, cin // 2), jnp.bfloat16),
        ),
        in_specs=[ANY, ANY],
        out_specs=(VMEM,) * 4,
        scratch_shapes=[
            pltpu.VMEM((chans * rows, cols), jnp.float32),
            pltpu.VMEM((chans, rows, cols), jnp.bfloat16),
            pltpu.SemaphoreType.DMA((4,)),
        ],
        compiler_params=pltpu.CompilerParams(vmem_limit_bytes=LIMIT),
    )(in_hbm(own), in_hbm(w_up))


def in_hbm(operand):
    return pltpu.with_memory_space_constraint(operand, pltpu.HBM)


def cost(sizes):
    cin, cout, rows, cols = sizes
    flops = 2 * cout * 4 * cin * 2 * cols * (rows + 2) + 2 * 2 * cout * 9 * cout * 2 * cols * rows
    return pl.CostEstimate(flops=flops, bytes_accessed=8 * 2**20, transcendentals=0)


def call_prepare(paired, own, w_half, w_conv, sizes):
    cin, cout, rows, cols = sizes
    wide = own.shape[0] * own.shape[1] if paired else 8
    return pl.pallas_call(
        functools.partial(prepare, paired),
        out_shape=(
            jax.ShapeDtypeStruct((3, rows // 2 + 2, cin, cols), jnp.bfloat16),
            jax.ShapeDtypeStruct((32, cout // 2, cin), jnp.bfloat16),
            jax.ShapeDtypeStruct((2 * cout, 9 * cout), jnp.bfloat16),
            jax.ShapeDtypeStruct((2 * cout, 9 * cout), jnp.bfloat16),
        ),
        in_specs=[ANY] * 3,
        out_specs=(VMEM,) * 4,
        scratch_shapes=[
            pltpu.VMEM((2, 2 * cout, 9 * cout), jnp.bfloat16),
            pltpu.VMEM((27, cout, cout), jnp.bfloat16),
            pltpu.VMEM((wide, cols), jnp.float32),
            pltpu.VMEM(own.shape, jnp.bfloat16),
            pltpu.SemaphoreType.DMA((3,)),
        ],
        cost_estimate=pl.CostEstimate(flops=2 * 18 * 256 * cout * cout, bytes_accessed=8 * 2**20, transcendentals=0),
        compiler_params=pltpu.CompilerParams(vmem_limit_bytes=LIMIT),
    )(in_hbm(own), in_hbm(w_half), in_hbm(w_conv))


def call_first(body, rows_in, prepared, b_up, sizes):
    cin, cout, rows, cols = sizes
    started, w_half, kernel = prepared
    return pl.pallas_call(
        body,
        out_shape=(
            jax.ShapeDtypeStruct(started.shape, jnp.bfloat16),
            jax.ShapeDtypeStruct((2, 2 * cout, rows * cols), jnp.float32),
        ),
        in_specs=[VMEM] * (len(rows_in) + 4),
        out_specs=(VMEM,) * 2,
        scratch_shapes=[
            pltpu.VMEM((cout, cout), jnp.float32),
            pltpu.VMEM((4, rows + 2, cout, cols), jnp.bfloat16),
        ],
        input_output_aliases={len(rows_in): 0},
        cost_estimate=cost(sizes),
        compiler_params=pltpu.CompilerParams(vmem_limit_bytes=LIMIT),
    )(*rows_in, started, w_half, kernel, b_up)


def call_second(paired, parts, results, biases, sizes):
    cin, cout, rows, cols = sizes
    return pl.pallas_call(
        functools.partial(second, paired, len(parts)),
        out_shape=jax.ShapeDtypeStruct((cout, 2, rows, 2 * cols), jnp.bfloat16),
        in_specs=[VMEM] * (len(parts) + 5),
        out_specs=ANY,
        scratch_shapes=[
            pltpu.VMEM((cout, cout), jnp.float32),
            pltpu.VMEM((4, rows + 2, cout, cols), jnp.bfloat16),
            pltpu.VMEM((2, 2 * cout * rows, cols), jnp.float32),
            pltpu.VMEM((4, cout, rows, cols), jnp.bfloat16),
            pltpu.SemaphoreType.DMA((4,)),
        ],
        cost_estimate=cost(sizes),
        compiler_params=pltpu.CompilerParams(vmem_limit_bytes=LIMIT),
    )(*parts, *results, *biases)


def paired(inputs, w_up, b_up, w_conv, b_conv, sizes):
    spaces = lax.axis_size("space")
    s, c = lax.axis_index("space"), lax.axis_index("ch")
    chans, _, held, cols = inputs.shape

    def at(space, ch):
        return space * 2 + ch

    across = [(at(i, j), at(i, 1 - j)) for i in range(spaces) for j in (0, 1)]
    cores = [(at(i, j), at(i ^ 1, j)) for i in range(spaces) for j in (0, 1)]
    pairs = [(at(i, j), at(i ^ 2, j)) for i in range(spaces) for j in (0, 1)]
    chain = [(at(i - 1, 0), at(i, 0)) for i in range(1, spaces)]
    chain += [(at(i + 1, 1), at(i, 1)) for i in range(spaces - 1)]

    outer = [(t, t + 1) for t in range(1, 2 * spaces - 1, 2)]
    outer += [(j, i) for i, j in outer]

    own = inputs.reshape(chans, held, cols)
    near, far, peer, w_a = call_pieces(own, w_up)
    own, w_conv, peer, w_a, far, near = lax.optimization_barrier((own, w_conv, peer, w_a, far, near))
    peer = lax.ppermute(peer, AXES, across)
    w_a = lax.ppermute(w_a, AXES, across)
    far = lax.ppermute(far, AXES, outer)
    near = lax.ppermute(near, AXES, chain)
    w_a, own, w_conv = lax.optimization_barrier((w_a, own, w_conv))
    w_ax = lax.ppermute(w_a, AXES, pairs)
    w_ac = lax.ppermute(w_a, AXES, cores)
    x, w_half, kernel, other = call_prepare(True, own, w_up, w_conv, sizes)
    biases = (b_up[None], b_conv[None])
    x, total = call_first(paired_first, (peer, near, far), (x, w_half, kernel), biases[0], sizes)
    results = (x, total, other)
    w_ax, w_ac, *results = lax.optimization_barrier((w_ax, w_ac, *results))
    w_axc = lax.ppermute(w_ax, AXES, cores)
    return call_second(True, (w_a, w_ax, w_ac, w_axc), results, biases, sizes)


def gathered(inputs, w_up, b_up, w_conv, b_conv, sizes):
    spaces, chs = lax.axis_size("space"), lax.axis_size("ch")
    c = lax.axis_index("ch")
    w_all = lax.all_gather(w_up[16:48], "ch", axis=1, tiled=True)
    part = w_all.shape[1] // 2
    rows = lax.all_gather(inputs[:, 0], "ch", axis=0, tiled=True).transpose(1, 0, 2)
    forward = [(i, i + 1) for i in range(spaces - 1)]
    backward = [(j, i) for i, j in forward]
    low = lax.ppermute(rows[-1:], "space", forward)
    high = lax.ppermute(rows[:1], "space", backward)
    rows = jnp.concatenate([low, rows, high], axis=0)
    share = inputs.shape[2] // chs
    rows = lax.dynamic_slice_in_dim(rows, c * share, share + 2, 0)
    biases = (b_up[None], b_conv[None])
    *prepared, other = call_prepare(False, rows, w_all[:, :part], w_conv, sizes)
    results = (*call_first(gathered_first, (), prepared, biases[0], sizes), other)
    return call_second(False, (w_all[:16, part:], w_all[16:, part:]), results, biases, sizes)


def local(inputs, w_up, b_up, w_conv, b_conv):
    chs = lax.axis_size("ch")
    sizes = (w_up.shape[2], w_conv.shape[1], 2 * inputs.shape[2] // chs, inputs.shape[3])
    plan = paired if chs == 2 and lax.axis_size("space") % 4 == 0 else gathered
    return plan(inputs, w_up, b_up, w_conv, b_conv, sizes)


def solution(mesh):
    return jax.shard_map(
        local,
        mesh=mesh,
        in_specs=(P("ch", None, "space", None), P(None, "ch", None), P(), P(), P()),
        out_specs=P(None, None, ("space", "ch"), None),
        check_vma=False,
    )
```

```python
import functools

import jax
import jax.numpy as jnp
from jax import lax
from jax.experimental import pallas as pl
from jax.experimental.pallas import tpu as pltpu
from jax.sharding import PartitionSpec as P

AXES = ("space", "ch")
PHASES = (((1, 0), (3, -1)), ((2, 0), (0, 1)))
COLUMNS = ((3, 0, 1), (0, 1, 2))
VMEM = pl.BlockSpec(memory_space=pltpu.VMEM)
ANY = pl.BlockSpec(memory_space=pl.ANY)
LIMIT = 40 * 2**20


def column_of(bias):
    lanes = bias.shape[-1]
    return jnp.transpose(jnp.broadcast_to(bias, (lanes, lanes)))


def shifted(value, step):
    cols = value.shape[1]
    place = lax.broadcasted_iota(jnp.int32, value.shape, 1)
    edge = 0 if step == 1 else cols - 1
    return jnp.where(place == edge, jnp.zeros_like(value), pltpu.roll(value, step % cols, 1))


def upsample(cell, tap_of, bias, u_ref, first, last):
    held, cols = u_ref.shape[1], u_ref.shape[3]
    for row_phase in (0, 1):
        for col_phase in (0, 1):
            taps = []
            for row_tap, row_shift in PHASES[row_phase]:
                for col_tap, col_shift in PHASES[col_phase]:
                    slot = row_shift + 1 - row_phase
                    taps.append((row_tap * 4 + col_tap, slot, col_shift % 3))
            kernel = jnp.concatenate([tap_of(tap) for tap, _, _ in taps], axis=1)
            for start in range(0, held // 2, 2):
                places = range(start, min(start + 2, held // 2))
                cells = jnp.concatenate(
                    [
                        jnp.concatenate([cell(copy, slot + place) for place in places], axis=1)
                        for _, slot, copy in taps
                    ],
                    axis=0,
                )
                summed = jnp.dot(kernel, cells, preferred_element_type=jnp.float32)
                for number, place in enumerate(places):
                    row = 2 * place + 1 - row_phase
                    value = summed[:, number * cols : (number + 1) * cols] + bias
                    value = jnp.maximum(value, 0.2 * value)
                    if row == 0:
                        value = jnp.where(first, 0.0, value)
                    if row == held - 1:
                        value = jnp.where(last, 0.0, value)
                    value = value.astype(jnp.bfloat16)
                    u_ref[col_phase, row] = value
                    u_ref[2 + col_phase, row] = shifted(value, -1 if col_phase == 0 else 1)


def convolve(kernel, u_ref, start, col_phase):
    cells = jnp.concatenate(
        [
            jnp.concatenate([u_ref[copy, start + row_tap], u_ref[copy, start + row_tap + 1]], 1)
            for row_tap in range(3)
            for copy in COLUMNS[col_phase]
        ],
        axis=0,
    )
    return jnp.dot(kernel, cells, preferred_element_type=jnp.float32)


def split_kernels(w_conv_ref, halves_ref):
    cout = w_conv_ref.shape[1]
    part = cout // 2
    low = lax.broadcasted_iota(jnp.int32, (cout, cout), 1) < part
    for row_tap in range(3):
        for col_tap in range(3):
            taps = [w_conv_ref[a * 9 + row_tap * 3 + col_tap].astype(jnp.float32) for a in range(3)]
            turned = [pltpu.roll(tap, part, 1) for tap in taps]
            columns = pl.ds((row_tap * 3 + col_tap) * cout, cout)
            for plane in (0, 1):
                near, far = 1 - plane, 2 - plane
                rows = pl.ds(plane * cout, cout)
                halves_ref[0, rows, columns] = jnp.where(low, taps[near], turned[far]).astype(jnp.bfloat16)
                halves_ref[1, rows, columns] = jnp.where(low, turned[near], taps[far]).astype(jnp.bfloat16)


def bias_of(bias_ref, column_ref, blocks):
    column_ref[...] = column_of(bias_ref[...])
    return jnp.concatenate([column_ref[pl.ds(pl.multiple_of(at, 16), size)] for at, size in blocks], axis=0)


def ends(s, c):
    first = (s == 0) & (c == 0)
    last = (s == lax.axis_size("space") - 1) & (c == lax.axis_size("ch") - 1)
    return first, last


def store_row(x_ref, slot, offset, value):
    where = pl.ds(pl.multiple_of(offset, 16), value.shape[0])
    x_ref[0, slot, where] = value.astype(jnp.bfloat16)
    x_ref[1, slot, where] = shifted(value, -1).astype(jnp.bfloat16)
    x_ref[2, slot, where] = shifted(value, 1).astype(jnp.bfloat16)


def arrival(x, part):
    if x is None:
        return [[(0, part)], [(0, part)]]
    quarter, half = part // 4, part // 2
    return [
        [(x * half, half), ((1 - x) * half, half)],
        [(x * quarter, quarter), ((1 - x) * quarter, quarter), (half, half)],
    ]


def arrange(x, part):
    source = lax.broadcasted_iota(jnp.int32, (2 * part, 2 * part), 0)
    target = lax.broadcasted_iota(jnp.int32, (2 * part, 2 * part), 1)
    wanted = jnp.zeros_like(target)
    for plane, blocks in enumerate(arrival(x, part)):
        place = plane * part
        for first, size in blocks:
            inside = (target >= place) & (target < place + size)
            wanted = jnp.where(inside, target - place + plane * part + first, wanted)
            place += size
    return jnp.where(source == wanted, 1.0, 0.0).astype(jnp.bfloat16)


def own_part(half, refs, results, scratch):
    w_half_ref, kernel_ref, b_up_ref = refs
    x_ref, sum_ref = results
    column_ref, u_ref = scratch
    s, c = lax.axis_index("space"), lax.axis_index("ch")
    part, cols = w_half_ref.shape[1], u_ref.shape[3]

    def tap_of(tap):
        return jnp.concatenate([w_half_ref[tap], w_half_ref[16 + tap]], axis=0)

    bias = bias_of(b_up_ref, column_ref, [(half * part, part)] * 2)
    upsample(lambda copy, slot: x_ref[copy, slot], tap_of, bias, u_ref, *ends(s, c))
    kernel = kernel_ref[...]
    for start in range(0, u_ref.shape[1] - 2, 2):
        for col_phase in (0, 1):
            sum_ref[col_phase, :, start * cols : (start + 2) * cols] = convolve(kernel, u_ref, start, col_phase)


def prepare(paired, own_ref, w_half_ref, w_conv_ref, x_ref, w_ref, kernel_ref, other_ref, *scratch):
    halves_ref, v_ref, wide_ref, raw_ref, sems = scratch
    s, c = lax.axis_index("space"), lax.axis_index("ch")
    skipped = (w_half_ref.shape[0] - 32) // 2
    copies = [
        pltpu.make_async_copy(own_ref, raw_ref, sems.at[0]),
        pltpu.make_async_copy(w_conv_ref, v_ref, sems.at[1]),
        pltpu.make_async_copy(w_half_ref.at[pl.ds(skipped, 32)], w_ref, sems.at[2]),
    ]
    for copy in copies:
        copy.start()
    copies[0].wait()
    if paired:
        chans, rows, cols = own_ref.shape
        wide_ref[...] = raw_ref[...].astype(jnp.float32).reshape(chans * rows, cols)
        share = x_ref.shape[1] - 1
        for place in range(share):
            value = wide_ref[pl.ds(place + c * (rows - share), chans, stride=rows), :]
            store_row(x_ref, place + 1 - c, c * chans, value)
    else:
        for slot in range(own_ref.shape[0]):
            store_row(x_ref, slot, 0, raw_ref[slot].astype(jnp.float32))
    cout = w_conv_ref.shape[1]
    half, x = (c, lax.rem(s, 4) // 2) if paired else (0, None)
    copies[1].wait()
    split_kernels(v_ref, halves_ref)
    kernel_ref[...] = halves_ref[half]
    matrix = arrange(x, cout // 2)
    for number in range(9):
        columns = pl.ds(number * cout, cout)
        moved = jnp.dot(halves_ref[1 - half, :, columns], matrix, preferred_element_type=jnp.float32)
        other_ref[:, columns] = moved.astype(jnp.bfloat16)
    copies[2].wait()


def paired_first(peer_ref, near_ref, far_ref, started_ref, *refs):
    refs, results, scratch = refs[:3], refs[3:5], refs[5:]
    x_ref = results[0]
    c = lax.axis_index("ch")
    share, chans, _ = peer_ref.shape
    for place in range(share):
        store_row(x_ref, place + 1 - c, (1 - c) * chans, peer_ref[place].astype(jnp.float32))
    slot = c * (x_ref.shape[1] - 1)
    store_row(x_ref, slot, c * chans, near_ref[...].astype(jnp.float32))
    store_row(x_ref, slot, (1 - c) * chans, far_ref[...].astype(jnp.float32))
    own_part(c, refs, results, scratch)


def gathered_first(started_ref, *refs):
    own_part(0, refs[:3], refs[3:5], refs[5:])


def second(paired, count, *refs):
    parts, refs = refs[:count], refs[count:]
    x_ref, sum_ref, other_ref, b_up_ref, b_conv_ref, out_ref, column_ref, u_ref, total_ref, made_ref, sems = refs
    s, c = lax.axis_index("space"), lax.axis_index("ch")
    cout, _, rows, _ = out_ref.shape
    part = cout // 2
    half, x = (1 - c, lax.rem(s, 4) // 2) if paired else (1, None)
    cols = x_ref.shape[3]
    if paired:
        chans = x_ref.shape[2] // 2
        core = lax.rem(s, 2)
        sides = [pl.ds(pl.multiple_of(side * chans, 16), chans) for side in (core, 1 - core)]
        big = part // 2

        def tap_of(tap):
            columns = []
            for near_ref, far_ref, rest_ref in (parts[:3], parts[3:]):
                rows = [near_ref[tap, :big], far_ref[tap, :big], near_ref[tap, big:], far_ref[tap, big:], rest_ref[tap]]
                columns.append(jnp.concatenate(rows, axis=0))
            return jnp.concatenate(columns, axis=1)

        def cell(copy, slot):
            return jnp.concatenate([x_ref[copy, slot, side] for side in sides], axis=0)
    else:

        def tap_of(tap):
            return jnp.concatenate([part_ref[tap] for part_ref in parts], axis=0)

        def cell(copy, slot):
            return x_ref[copy, slot]

    blocks = [(half * part + at, size) for plane in arrival(x, part) for at, size in plane]
    bias = bias_of(b_up_ref, column_ref, blocks)
    upsample(cell, tap_of, bias, u_ref, *ends(s, c))
    source = lax.broadcasted_iota(jnp.int32, (2 * cols, 2 * cols), 0)
    target = lax.broadcasted_iota(jnp.int32, (2 * cols, 2 * cols), 1)
    wanted = jnp.where(source < cols, 2 * source, 2 * (source - cols) + 1)
    interleave = jnp.where(wanted == target, 1.0, 0.0).astype(jnp.bfloat16)
    kernel = other_ref[...]
    bias = column_of(b_conv_ref[...])
    bias = jnp.concatenate([bias, bias], axis=0)
    for start in range(0, rows, 2):
        halves = [
            convolve(kernel, u_ref, start, col_phase) + sum_ref[col_phase, :, start * cols : (start + 2) * cols]
            for col_phase in (0, 1)
        ]
        for number in (0, 1):
            pair = [
                (half[:, number * cols : (number + 1) * cols] + bias).astype(jnp.bfloat16) for half in halves
            ]
            mixed = jnp.dot(jnp.concatenate(pair, axis=1), interleave, preferred_element_type=jnp.float32)
            for side in (0, 1):
                total_ref[side, pl.ds(start + number, 2 * cout, stride=rows), :] = mixed[
                    :, side * cols : (side + 1) * cols
                ]
    copies = []
    for plane in (0, 1):
        for side in (0, 1):
            number = 2 * plane + side
            block = total_ref[side, pl.ds(plane * cout * rows, cout * rows), :]
            made_ref[number] = block.reshape(cout, rows, cols).astype(jnp.bfloat16)
            place = out_ref.at[:, plane, :, pl.ds(side * cols, cols)]
            copies.append(pltpu.make_async_copy(made_ref.at[number], place, sems.at[number]))
            copies[-1].start()
    for copy in copies:
        copy.wait()


def pieces(own_ref, w_up_ref, near_ref, far_ref, peer_ref, w_a_ref, w_b_ref, wide_ref, raw_ref, sems):
    s, c = lax.axis_index("space"), lax.axis_index("ch")
    raw = pltpu.make_async_copy(own_ref, raw_ref, sems.at[3])
    raw.start()
    me = lax.rem(s, 4)
    part, lanes = w_up_ref.shape[1], w_a_ref.shape[2]
    side = pl.ds(pl.multiple_of(lax.rem(me, 2) * lanes, lanes), lanes)
    (first, big), = arrival(me // 2, part)[0][:1]
    (second, small), _, (third, rest) = arrival(me // 2, part)[1]
    cuts = (
        (16, first, big, w_a_ref.at[:, pl.ds(0, big)]),
        (32, second, small, w_a_ref.at[:, pl.ds(big, small)]),
        (32, third, rest, w_b_ref),
    )
    copies = []
    for number, (tap, channel, count, place) in enumerate(cuts):
        source = w_up_ref.at[pl.ds(tap, 16), pl.ds(pl.multiple_of(channel, 16), count), side]
        copies.append(pltpu.make_async_copy(source, place, sems.at[number]))
        copies[-1].start()
    chans, rows, cols = own_ref.shape
    raw.wait()
    wide_ref[...] = raw_ref[...].astype(jnp.float32).reshape(chans * rows, cols)
    inner, outer = (1 - c) * (rows - 1), c * (rows - 1)
    near_ref[...] = wide_ref[pl.ds(inner, chans, stride=rows), :].astype(jnp.bfloat16)
    far_ref[...] = wide_ref[pl.ds(outer, chans, stride=rows), :].astype(jnp.bfloat16)
    share = peer_ref.shape[0]
    for place in range(share):
        row = wide_ref[pl.ds(place + (1 - c) * (rows - share), chans, stride=rows), :]
        peer_ref[place] = row.astype(jnp.bfloat16)
    for copy in copies:
        copy.wait()


def call_pieces(own, w_up):
    chans, rows, cols = own.shape
    part, cin = w_up.shape[1:]
    return pl.pallas_call(
        pieces,
        out_shape=(
            jax.ShapeDtypeStruct((chans, cols), jnp.bfloat16),
            jax.ShapeDtypeStruct((chans, cols), jnp.bfloat16),
            jax.ShapeDtypeStruct((rows // 2 + 1, chans, cols), jnp.bfloat16),
            jax.ShapeDtypeStruct((16, 3 * part // 4, cin // 2), jnp.bfloat16),
            jax.ShapeDtypeStruct((16, part // 2, cin // 2), jnp.bfloat16),
        ),
        in_specs=[ANY, ANY],
        out_specs=(VMEM,) * 5,
        scratch_shapes=[
            pltpu.VMEM((chans * rows, cols), jnp.float32),
            pltpu.VMEM((chans, rows, cols), jnp.bfloat16),
            pltpu.SemaphoreType.DMA((4,)),
        ],
        compiler_params=pltpu.CompilerParams(vmem_limit_bytes=LIMIT),
    )(in_hbm(own), in_hbm(w_up))


def in_hbm(operand):
    return pltpu.with_memory_space_constraint(operand, pltpu.HBM)


def cost(sizes):
    cin, cout, rows, cols = sizes
    flops = 2 * cout * 4 * cin * 2 * cols * (rows + 2) + 2 * 2 * cout * 9 * cout * 2 * cols * rows
    return pl.CostEstimate(flops=flops, bytes_accessed=8 * 2**20, transcendentals=0)


def call_prepare(paired, own, w_half, w_conv, sizes):
    cin, cout, rows, cols = sizes
    wide = own.shape[0] * own.shape[1] if paired else 8
    return pl.pallas_call(
        functools.partial(prepare, paired),
        out_shape=(
            jax.ShapeDtypeStruct((3, rows // 2 + 2, cin, cols), jnp.bfloat16),
            jax.ShapeDtypeStruct((32, cout // 2, cin), jnp.bfloat16),
            jax.ShapeDtypeStruct((2 * cout, 9 * cout), jnp.bfloat16),
            jax.ShapeDtypeStruct((2 * cout, 9 * cout), jnp.bfloat16),
        ),
        in_specs=[ANY] * 3,
        out_specs=(VMEM,) * 4,
        scratch_shapes=[
            pltpu.VMEM((2, 2 * cout, 9 * cout), jnp.bfloat16),
            pltpu.VMEM((27, cout, cout), jnp.bfloat16),
            pltpu.VMEM((wide, cols), jnp.float32),
            pltpu.VMEM(own.shape, jnp.bfloat16),
            pltpu.SemaphoreType.DMA((3,)),
        ],
        cost_estimate=pl.CostEstimate(flops=2 * 18 * 256 * cout * cout, bytes_accessed=8 * 2**20, transcendentals=0),
        compiler_params=pltpu.CompilerParams(vmem_limit_bytes=LIMIT),
    )(in_hbm(own), in_hbm(w_half), in_hbm(w_conv))


def call_first(body, rows_in, prepared, b_up, sizes):
    cin, cout, rows, cols = sizes
    started, w_half, kernel = prepared
    return pl.pallas_call(
        body,
        out_shape=(
            jax.ShapeDtypeStruct(started.shape, jnp.bfloat16),
            jax.ShapeDtypeStruct((2, 2 * cout, rows * cols), jnp.float32),
        ),
        in_specs=[VMEM] * (len(rows_in) + 4),
        out_specs=(VMEM,) * 2,
        scratch_shapes=[
            pltpu.VMEM((cout, cout), jnp.float32),
            pltpu.VMEM((4, rows + 2, cout, cols), jnp.bfloat16),
        ],
        input_output_aliases={len(rows_in): 0},
        cost_estimate=cost(sizes),
        compiler_params=pltpu.CompilerParams(vmem_limit_bytes=LIMIT),
    )(*rows_in, started, w_half, kernel, b_up)


def call_second(paired, parts, results, biases, sizes):
    cin, cout, rows, cols = sizes
    return pl.pallas_call(
        functools.partial(second, paired, len(parts)),
        out_shape=jax.ShapeDtypeStruct((cout, 2, rows, 2 * cols), jnp.bfloat16),
        in_specs=[VMEM] * (len(parts) + 5),
        out_specs=ANY,
        scratch_shapes=[
            pltpu.VMEM((cout, cout), jnp.float32),
            pltpu.VMEM((4, rows + 2, cout, cols), jnp.bfloat16),
            pltpu.VMEM((2, 2 * cout * rows, cols), jnp.float32),
            pltpu.VMEM((4, cout, rows, cols), jnp.bfloat16),
            pltpu.SemaphoreType.DMA((4,)),
        ],
        cost_estimate=cost(sizes),
        compiler_params=pltpu.CompilerParams(vmem_limit_bytes=LIMIT),
    )(*parts, *results, *biases)


def paired(inputs, w_up, b_up, w_conv, b_conv, sizes):
    spaces = lax.axis_size("space")
    s, c = lax.axis_index("space"), lax.axis_index("ch")
    chans, _, held, cols = inputs.shape

    def at(space, ch):
        return space * 2 + ch

    across = [(at(i, j), at(i, 1 - j)) for i in range(spaces) for j in (0, 1)]
    cores = [(at(i, j), at(i ^ 1, j)) for i in range(spaces) for j in (0, 1)]
    pairs = [(at(i, j), at(i ^ 2, j)) for i in range(spaces) for j in (0, 1)]
    chain = [(at(i - 1, 0), at(i, 0)) for i in range(1, spaces)]
    chain += [(at(i + 1, 1), at(i, 1)) for i in range(spaces - 1)]

    outer = [(t, t + 1) for t in range(1, 2 * spaces - 1, 2)]
    outer += [(j, i) for i, j in outer]

    own = inputs.reshape(chans, held, cols)
    near, far, peer, w_a, w_b = call_pieces(own, w_up)
    own, w_conv, peer, w_a, far, near, w_b = lax.optimization_barrier((own, w_conv, peer, w_a, far, near, w_b))
    peer = lax.ppermute(peer, AXES, across)
    w_a = lax.ppermute(w_a, AXES, across)
    far = lax.ppermute(far, AXES, outer)
    near = lax.ppermute(near, AXES, chain)
    w_a, w_b, own, w_conv = lax.optimization_barrier((w_a, w_b, own, w_conv))
    w_ax = lax.ppermute(w_a, AXES, pairs)
    w_b = lax.ppermute(w_b, AXES, across)
    w_ac = lax.ppermute(w_a, AXES, cores)
    x, w_half, kernel, other = call_prepare(True, own, w_up, w_conv, sizes)
    biases = (b_up[None], b_conv[None])
    x, total = call_first(paired_first, (peer, near, far), (x, w_half, kernel), biases[0], sizes)
    results = (x, total, other)
    w_b, w_ax, w_ac, *results = lax.optimization_barrier((w_b, w_ax, w_ac, *results))
    w_bc = lax.ppermute(w_b, AXES, cores)
    w_axc = lax.ppermute(w_ax, AXES, cores)
    return call_second(True, (w_a, w_ax, w_b, w_ac, w_axc, w_bc), results, biases, sizes)


def gathered(inputs, w_up, b_up, w_conv, b_conv, sizes):
    spaces, chs = lax.axis_size("space"), lax.axis_size("ch")
    c = lax.axis_index("ch")
    w_all = lax.all_gather(w_up[16:48], "ch", axis=1, tiled=True)
    part = w_all.shape[1] // 2
    rows = lax.all_gather(inputs[:, 0], "ch", axis=0, tiled=True).transpose(1, 0, 2)
    forward = [(i, i + 1) for i in range(spaces - 1)]
    backward = [(j, i) for i, j in forward]
    low = lax.ppermute(rows[-1:], "space", forward)
    high = lax.ppermute(rows[:1], "space", backward)
    rows = jnp.concatenate([low, rows, high], axis=0)
    share = inputs.shape[2] // chs
    rows = lax.dynamic_slice_in_dim(rows, c * share, share + 2, 0)
    biases = (b_up[None], b_conv[None])
    *prepared, other = call_prepare(False, rows, w_all[:, :part], w_conv, sizes)
    results = (*call_first(gathered_first, (), prepared, biases[0], sizes), other)
    return call_second(False, (w_all[:16, part:], w_all[16:, part:]), results, biases, sizes)


def local(inputs, w_up, b_up, w_conv, b_conv):
    chs = lax.axis_size("ch")
    sizes = (w_up.shape[2], w_conv.shape[1], 2 * inputs.shape[2] // chs, inputs.shape[3])
    plan = paired if chs == 2 and lax.axis_size("space") % 4 == 0 else gathered
    return plan(inputs, w_up, b_up, w_conv, b_conv, sizes)


def solution(mesh):
    return jax.shard_map(
        local,
        mesh=mesh,
        in_specs=(P("ch", None, "space", None), P(None, "ch", None), P(), P(), P()),
        out_specs=P(None, None, ("space", "ch"), None),
        check_vma=False,
    )
```

```python
import functools

import jax
import jax.numpy as jnp
from jax import lax
from jax.experimental import pallas as pl
from jax.experimental.pallas import tpu as pltpu
from jax.sharding import PartitionSpec as P

AXES = ("space", "ch")
PHASES = (((1, 0), (3, -1)), ((2, 0), (0, 1)))
COLUMNS = ((3, 0, 1), (0, 1, 2))
VMEM = pl.BlockSpec(memory_space=pltpu.VMEM)
ANY = pl.BlockSpec(memory_space=pl.ANY)
LIMIT = 40 * 2**20


def column_of(bias):
    lanes = bias.shape[-1]
    return jnp.transpose(jnp.broadcast_to(bias, (lanes, lanes)))


def shifted(value, step):
    cols = value.shape[1]
    place = lax.broadcasted_iota(jnp.int32, value.shape, 1)
    edge = 0 if step == 1 else cols - 1
    return jnp.where(place == edge, jnp.zeros_like(value), pltpu.roll(value, step % cols, 1))


def upsample(cell, tap_of, bias, u_ref, first, last):
    held, cols = u_ref.shape[1], u_ref.shape[3]
    for row_phase in (0, 1):
        for col_phase in (0, 1):
            taps = []
            for row_tap, row_shift in PHASES[row_phase]:
                for col_tap, col_shift in PHASES[col_phase]:
                    slot = row_shift + 1 - row_phase
                    taps.append((row_tap * 4 + col_tap, slot, col_shift % 3))
            kernel = jnp.concatenate([tap_of(tap) for tap, _, _ in taps], axis=1)
            for start in range(0, held // 2, 2):
                places = range(start, min(start + 2, held // 2))
                cells = jnp.concatenate(
                    [
                        jnp.concatenate([cell(copy, slot + place) for place in places], axis=1)
                        for _, slot, copy in taps
                    ],
                    axis=0,
                )
                summed = jnp.dot(kernel, cells, preferred_element_type=jnp.float32)
                for number, place in enumerate(places):
                    row = 2 * place + 1 - row_phase
                    value = summed[:, number * cols : (number + 1) * cols] + bias
                    value = jnp.maximum(value, 0.2 * value)
                    if row == 0:
                        value = jnp.where(first, 0.0, value)
                    if row == held - 1:
                        value = jnp.where(last, 0.0, value)
                    value = value.astype(jnp.bfloat16)
                    u_ref[col_phase, row] = value
                    u_ref[2 + col_phase, row] = shifted(value, -1 if col_phase == 0 else 1)


def convolve(kernel, u_ref, start, col_phase):
    cells = jnp.concatenate(
        [
            jnp.concatenate([u_ref[copy, start + row_tap], u_ref[copy, start + row_tap + 1]], 1)
            for row_tap in range(3)
            for copy in COLUMNS[col_phase]
        ],
        axis=0,
    )
    return jnp.dot(kernel, cells, preferred_element_type=jnp.float32)


def split_kernels(w_conv_ref, halves_ref):
    cout = w_conv_ref.shape[1]
    part = cout // 2
    low = lax.broadcasted_iota(jnp.int32, (cout, cout), 1) < part
    for row_tap in range(3):
        for col_tap in range(3):
            taps = [w_conv_ref[a * 9 + row_tap * 3 + col_tap].astype(jnp.float32) for a in range(3)]
            turned = [pltpu.roll(tap, part, 1) for tap in taps]
            columns = pl.ds((row_tap * 3 + col_tap) * cout, cout)
            for plane in (0, 1):
                near, far = 1 - plane, 2 - plane
                rows = pl.ds(plane * cout, cout)
                halves_ref[0, rows, columns] = jnp.where(low, taps[near], turned[far]).astype(jnp.bfloat16)
                halves_ref[1, rows, columns] = jnp.where(low, turned[near], taps[far]).astype(jnp.bfloat16)


def bias_of(bias_ref, column_ref, blocks):
    column_ref[...] = column_of(bias_ref[...])
    return jnp.concatenate([column_ref[pl.ds(pl.multiple_of(at, 16), size)] for at, size in blocks], axis=0)


def ends(s, c):
    first = (s == 0) & (c == 0)
    last = (s == lax.axis_size("space") - 1) & (c == lax.axis_size("ch") - 1)
    return first, last


def store_row(x_ref, slot, offset, value):
    where = pl.ds(pl.multiple_of(offset, 16), value.shape[0])
    x_ref[0, slot, where] = value.astype(jnp.bfloat16)
    x_ref[1, slot, where] = shifted(value, -1).astype(jnp.bfloat16)
    x_ref[2, slot, where] = shifted(value, 1).astype(jnp.bfloat16)


def arrival(x, part):
    if x is None:
        return [[(0, part)], [(0, part)]]
    quarter, half = part // 4, part // 2
    return [
        [(x * half, half), ((1 - x) * half, half)],
        [(x * quarter, quarter), ((1 - x) * quarter, quarter), (half, half)],
    ]


def arrange(x, part):
    source = lax.broadcasted_iota(jnp.int32, (2 * part, 2 * part), 0)
    target = lax.broadcasted_iota(jnp.int32, (2 * part, 2 * part), 1)
    wanted = jnp.zeros_like(target)
    for plane, blocks in enumerate(arrival(x, part)):
        place = plane * part
        for first, size in blocks:
            inside = (target >= place) & (target < place + size)
            wanted = jnp.where(inside, target - place + plane * part + first, wanted)
            place += size
    return jnp.where(source == wanted, 1.0, 0.0).astype(jnp.bfloat16)


def own_part(half, refs, results, scratch):
    w_half_ref, kernel_ref, b_up_ref = refs
    x_ref, sum_ref = results
    column_ref, u_ref = scratch
    s, c = lax.axis_index("space"), lax.axis_index("ch")
    part, cols = w_half_ref.shape[1], u_ref.shape[3]

    def tap_of(tap):
        return jnp.concatenate([w_half_ref[tap], w_half_ref[16 + tap]], axis=0)

    bias = bias_of(b_up_ref, column_ref, [(half * part, part)] * 2)
    upsample(lambda copy, slot: x_ref[copy, slot], tap_of, bias, u_ref, *ends(s, c))
    kernel = kernel_ref[...]
    for start in range(0, u_ref.shape[1] - 2, 2):
        for col_phase in (0, 1):
            sum_ref[col_phase, :, start * cols : (start + 2) * cols] = convolve(kernel, u_ref, start, col_phase)


def prepare(paired, own_ref, w_half_ref, w_conv_ref, x_ref, w_ref, kernel_ref, other_ref, *scratch):
    halves_ref, v_ref, wide_ref, raw_ref, sems = scratch
    s, c = lax.axis_index("space"), lax.axis_index("ch")
    skipped = (w_half_ref.shape[0] - 32) // 2
    copies = [
        pltpu.make_async_copy(own_ref, raw_ref, sems.at[0]),
        pltpu.make_async_copy(w_conv_ref, v_ref, sems.at[1]),
        pltpu.make_async_copy(w_half_ref.at[pl.ds(skipped, 32)], w_ref, sems.at[2]),
    ]
    for copy in copies:
        copy.start()
    copies[0].wait()
    if paired:
        chans, rows, cols = own_ref.shape
        wide_ref[...] = raw_ref[...].astype(jnp.float32).reshape(chans * rows, cols)
        share = x_ref.shape[1] - 1
        for place in range(share):
            value = wide_ref[pl.ds(place + c * (rows - share), chans, stride=rows), :]
            store_row(x_ref, place + 1 - c, c * chans, value)
    else:
        for slot in range(own_ref.shape[0]):
            store_row(x_ref, slot, 0, raw_ref[slot].astype(jnp.float32))
    cout = w_conv_ref.shape[1]
    half, x = (c, lax.rem(s, 4) // 2) if paired else (0, None)
    copies[1].wait()
    split_kernels(v_ref, halves_ref)
    kernel_ref[...] = halves_ref[half]
    matrix = arrange(x, cout // 2)
    for number in range(9):
        columns = pl.ds(number * cout, cout)
        moved = jnp.dot(halves_ref[1 - half, :, columns], matrix, preferred_element_type=jnp.float32)
        other_ref[:, columns] = moved.astype(jnp.bfloat16)
    copies[2].wait()


def paired_first(peer_ref, near_ref, far_ref, started_ref, *refs):
    refs, results, scratch = refs[:3], refs[3:5], refs[5:]
    x_ref = results[0]
    c = lax.axis_index("ch")
    share, chans, _ = peer_ref.shape
    for place in range(share):
        store_row(x_ref, place + 1 - c, (1 - c) * chans, peer_ref[place].astype(jnp.float32))
    slot = c * (x_ref.shape[1] - 1)
    store_row(x_ref, slot, c * chans, near_ref[...].astype(jnp.float32))
    store_row(x_ref, slot, (1 - c) * chans, far_ref[...].astype(jnp.float32))
    own_part(c, refs, results, scratch)


def gathered_first(started_ref, *refs):
    own_part(0, refs[:3], refs[3:5], refs[5:])


def second(paired, count, *refs):
    parts, refs = refs[:count], refs[count:]
    x_ref, sum_ref, other_ref, b_up_ref, b_conv_ref, out_ref, column_ref, u_ref, total_ref, made_ref, sems = refs
    s, c = lax.axis_index("space"), lax.axis_index("ch")
    cout, _, rows, _ = out_ref.shape
    part = cout // 2
    half, x = (1 - c, lax.rem(s, 4) // 2) if paired else (1, None)
    cols = x_ref.shape[3]
    if paired:
        chans = x_ref.shape[2] // 2
        core = lax.rem(s, 2)
        sides = [pl.ds(pl.multiple_of(side * chans, 16), chans) for side in (core, 1 - core)]
        big = part // 2

        def tap_of(tap):
            columns = []
            for near_ref, far_ref, rest_ref in (parts[:3], parts[3:]):
                rows = [near_ref[tap, :big], far_ref[tap, :big], near_ref[tap, big:], far_ref[tap, big:], rest_ref[tap]]
                columns.append(jnp.concatenate(rows, axis=0))
            return jnp.concatenate(columns, axis=1)

        def cell(copy, slot):
            return jnp.concatenate([x_ref[copy, slot, side] for side in sides], axis=0)
    else:

        def tap_of(tap):
            return jnp.concatenate([part_ref[tap] for part_ref in parts], axis=0)

        def cell(copy, slot):
            return x_ref[copy, slot]

    blocks = [(half * part + at, size) for plane in arrival(x, part) for at, size in plane]
    bias = bias_of(b_up_ref, column_ref, blocks)
    upsample(cell, tap_of, bias, u_ref, *ends(s, c))
    source = lax.broadcasted_iota(jnp.int32, (2 * cols, 2 * cols), 0)
    target = lax.broadcasted_iota(jnp.int32, (2 * cols, 2 * cols), 1)
    wanted = jnp.where(source < cols, 2 * source, 2 * (source - cols) + 1)
    interleave = jnp.where(wanted == target, 1.0, 0.0).astype(jnp.bfloat16)
    kernel = other_ref[...]
    bias = column_of(b_conv_ref[...])
    bias = jnp.concatenate([bias, bias], axis=0)
    for start in range(0, rows, 2):
        halves = [
            convolve(kernel, u_ref, start, col_phase) + sum_ref[col_phase, :, start * cols : (start + 2) * cols]
            for col_phase in (0, 1)
        ]
        for number in (0, 1):
            pair = [
                (half[:, number * cols : (number + 1) * cols] + bias).astype(jnp.bfloat16) for half in halves
            ]
            mixed = jnp.dot(jnp.concatenate(pair, axis=1), interleave, preferred_element_type=jnp.float32)
            for side in (0, 1):
                total_ref[side, pl.ds(start + number, 2 * cout, stride=rows), :] = mixed[
                    :, side * cols : (side + 1) * cols
                ]
    copies = []
    for plane in (0, 1):
        for side in (0, 1):
            number = 2 * plane + side
            block = total_ref[side, pl.ds(plane * cout * rows, cout * rows), :]
            made_ref[number] = block.reshape(cout, rows, cols).astype(jnp.bfloat16)
            place = out_ref.at[:, plane, :, pl.ds(side * cols, cols)]
            copies.append(pltpu.make_async_copy(made_ref.at[number], place, sems.at[number]))
            copies[-1].start()
    for copy in copies:
        copy.wait()


def pieces(own_ref, w_up_ref, near_ref, far_ref, peer_ref, w_a_ref, w_b_ref, wide_ref, raw_ref, sems):
    s, c = lax.axis_index("space"), lax.axis_index("ch")
    raw = pltpu.make_async_copy(own_ref, raw_ref, sems.at[3])
    raw.start()
    me = lax.rem(s, 4)
    part, lanes = w_up_ref.shape[1], w_a_ref.shape[2]
    side = pl.ds(pl.multiple_of(lax.rem(me, 2) * lanes, lanes), lanes)
    (first, big), = arrival(me // 2, part)[0][:1]
    (second, small), _, (third, rest) = arrival(me // 2, part)[1]
    cuts = (
        (16, first, big, w_a_ref.at[:, pl.ds(0, big)]),
        (32, second, small, w_a_ref.at[:, pl.ds(big, small)]),
        (32, third, rest, w_b_ref),
    )
    copies = []
    for number, (tap, channel, count, place) in enumerate(cuts):
        source = w_up_ref.at[pl.ds(tap, 16), pl.ds(pl.multiple_of(channel, 16), count), side]
        copies.append(pltpu.make_async_copy(source, place, sems.at[number]))
        copies[-1].start()
    chans, rows, cols = own_ref.shape
    raw.wait()
    wide_ref[...] = raw_ref[...].astype(jnp.float32).reshape(chans * rows, cols)
    inner, outer = (1 - c) * (rows - 1), c * (rows - 1)
    near_ref[...] = wide_ref[pl.ds(inner, chans, stride=rows), :].astype(jnp.bfloat16)
    far_ref[...] = wide_ref[pl.ds(outer, chans, stride=rows), :].astype(jnp.bfloat16)
    share = peer_ref.shape[0]
    for place in range(share):
        row = wide_ref[pl.ds(place + (1 - c) * (rows - share), chans, stride=rows), :]
        peer_ref[place] = row.astype(jnp.bfloat16)
    for copy in copies:
        copy.wait()


def call_pieces(own, w_up):
    chans, rows, cols = own.shape
    part, cin = w_up.shape[1:]
    return pl.pallas_call(
        pieces,
        out_shape=(
            jax.ShapeDtypeStruct((chans, cols), jnp.bfloat16),
            jax.ShapeDtypeStruct((chans, cols), jnp.bfloat16),
            jax.ShapeDtypeStruct((rows // 2 + 1, chans, cols), jnp.bfloat16),
            jax.ShapeDtypeStruct((16, 3 * part // 4, cin // 2), jnp.bfloat16),
            jax.ShapeDtypeStruct((16, part // 2, cin // 2), jnp.bfloat16),
        ),
        in_specs=[ANY, ANY],
        out_specs=(VMEM,) * 5,
        scratch_shapes=[
            pltpu.VMEM((chans * rows, cols), jnp.float32),
            pltpu.VMEM((chans, rows, cols), jnp.bfloat16),
            pltpu.SemaphoreType.DMA((4,)),
        ],
        compiler_params=pltpu.CompilerParams(vmem_limit_bytes=LIMIT),
    )(in_hbm(own), in_hbm(w_up))


def in_hbm(operand):
    return pltpu.with_memory_space_constraint(operand, pltpu.HBM)


def cost(sizes):
    cin, cout, rows, cols = sizes
    flops = 2 * cout * 4 * cin * 2 * cols * (rows + 2) + 2 * 2 * cout * 9 * cout * 2 * cols * rows
    return pl.CostEstimate(flops=flops, bytes_accessed=8 * 2**20, transcendentals=0)


def call_prepare(paired, own, w_half, w_conv, sizes):
    cin, cout, rows, cols = sizes
    wide = own.shape[0] * own.shape[1] if paired else 8
    return pl.pallas_call(
        functools.partial(prepare, paired),
        out_shape=(
            jax.ShapeDtypeStruct((3, rows // 2 + 2, cin, cols), jnp.bfloat16),
            jax.ShapeDtypeStruct((32, cout // 2, cin), jnp.bfloat16),
            jax.ShapeDtypeStruct((2 * cout, 9 * cout), jnp.bfloat16),
            jax.ShapeDtypeStruct((2 * cout, 9 * cout), jnp.bfloat16),
        ),
        in_specs=[ANY] * 3,
        out_specs=(VMEM,) * 4,
        scratch_shapes=[
            pltpu.VMEM((2, 2 * cout, 9 * cout), jnp.bfloat16),
            pltpu.VMEM((27, cout, cout), jnp.bfloat16),
            pltpu.VMEM((wide, cols), jnp.float32),
            pltpu.VMEM(own.shape, jnp.bfloat16),
            pltpu.SemaphoreType.DMA((3,)),
        ],
        cost_estimate=pl.CostEstimate(flops=2 * 18 * 256 * cout * cout, bytes_accessed=8 * 2**20, transcendentals=0),
        compiler_params=pltpu.CompilerParams(vmem_limit_bytes=LIMIT),
    )(in_hbm(own), in_hbm(w_half), in_hbm(w_conv))


def call_first(body, rows_in, prepared, b_up, sizes):
    cin, cout, rows, cols = sizes
    started, w_half, kernel = prepared
    return pl.pallas_call(
        body,
        out_shape=(
            jax.ShapeDtypeStruct(started.shape, jnp.bfloat16),
            jax.ShapeDtypeStruct((2, 2 * cout, rows * cols), jnp.float32),
        ),
        in_specs=[VMEM] * (len(rows_in) + 4),
        out_specs=(VMEM,) * 2,
        scratch_shapes=[
            pltpu.VMEM((cout, cout), jnp.float32),
            pltpu.VMEM((4, rows + 2, cout, cols), jnp.bfloat16),
        ],
        input_output_aliases={len(rows_in): 0},
        cost_estimate=cost(sizes),
        compiler_params=pltpu.CompilerParams(vmem_limit_bytes=LIMIT),
    )(*rows_in, started, w_half, kernel, b_up)


def call_second(paired, parts, results, biases, sizes):
    cin, cout, rows, cols = sizes
    return pl.pallas_call(
        functools.partial(second, paired, len(parts)),
        out_shape=jax.ShapeDtypeStruct((cout, 2, rows, 2 * cols), jnp.bfloat16),
        in_specs=[VMEM] * (len(parts) + 5),
        out_specs=ANY,
        scratch_shapes=[
            pltpu.VMEM((cout, cout), jnp.float32),
            pltpu.VMEM((4, rows + 2, cout, cols), jnp.bfloat16),
            pltpu.VMEM((2, 2 * cout * rows, cols), jnp.float32),
            pltpu.VMEM((4, cout, rows, cols), jnp.bfloat16),
            pltpu.SemaphoreType.DMA((4,)),
        ],
        cost_estimate=cost(sizes),
        compiler_params=pltpu.CompilerParams(vmem_limit_bytes=LIMIT),
    )(*parts, *results, *biases)


def paired(inputs, w_up, b_up, w_conv, b_conv, sizes):
    spaces = lax.axis_size("space")
    s, c = lax.axis_index("space"), lax.axis_index("ch")
    chans, _, held, cols = inputs.shape

    def at(space, ch):
        return space * 2 + ch

    across = [(at(i, j), at(i, 1 - j)) for i in range(spaces) for j in (0, 1)]
    cores = [(at(i, j), at(i ^ 1, j)) for i in range(spaces) for j in (0, 1)]
    pairs = [(at(i, j), at(i ^ 2, j)) for i in range(spaces) for j in (0, 1)]
    chain = [(at(i - 1, 0), at(i, 0)) for i in range(1, spaces)]
    chain += [(at(i + 1, 1), at(i, 1)) for i in range(spaces - 1)]

    outer = [(t, t + 1) for t in range(1, 2 * spaces - 1, 2)]
    outer += [(j, i) for i, j in outer]

    own = inputs.reshape(chans, held, cols)
    near, far, peer, w_a, w_b = call_pieces(own, w_up)
    own, w_conv, peer, w_a, far, near, w_b = lax.optimization_barrier((own, w_conv, peer, w_a, far, near, w_b))
    peer = lax.ppermute(peer, AXES, across)
    w_a = lax.ppermute(w_a, AXES, across)
    far = lax.ppermute(far, AXES, outer)
    near = lax.ppermute(near, AXES, chain)
    w_a, w_b, own, w_conv = lax.optimization_barrier((w_a, w_b, own, w_conv))
    w_ax = lax.ppermute(w_a, AXES, pairs)
    w_b = lax.ppermute(w_b, AXES, across)
    w_ac = lax.ppermute(w_a, AXES, cores)
    x, w_half, kernel, other = call_prepare(True, own, w_up, w_conv, sizes)
    biases = (b_up[None], b_conv[None])
    x, total = call_first(paired_first, (peer, near, far), (x, w_half, kernel), biases[0], sizes)
    results = (x, total, other)
    w_ax, w_ac, *results = lax.optimization_barrier((w_ax, w_ac, *results))
    w_axc = lax.ppermute(w_ax, AXES, cores)
    w_b, *results = lax.optimization_barrier((w_b, *results))
    w_bc = lax.ppermute(w_b, AXES, cores)
    return call_second(True, (w_a, w_ax, w_b, w_ac, w_axc, w_bc), results, biases, sizes)


def gathered(inputs, w_up, b_up, w_conv, b_conv, sizes):
    spaces, chs = lax.axis_size("space"), lax.axis_size("ch")
    c = lax.axis_index("ch")
    w_all = lax.all_gather(w_up[16:48], "ch", axis=1, tiled=True)
    part = w_all.shape[1] // 2
    rows = lax.all_gather(inputs[:, 0], "ch", axis=0, tiled=True).transpose(1, 0, 2)
    forward = [(i, i + 1) for i in range(spaces - 1)]
    backward = [(j, i) for i, j in forward]
    low = lax.ppermute(rows[-1:], "space", forward)
    high = lax.ppermute(rows[:1], "space", backward)
    rows = jnp.concatenate([low, rows, high], axis=0)
    share = inputs.shape[2] // chs
    rows = lax.dynamic_slice_in_dim(rows, c * share, share + 2, 0)
    biases = (b_up[None], b_conv[None])
    *prepared, other = call_prepare(False, rows, w_all[:, :part], w_conv, sizes)
    results = (*call_first(gathered_first, (), prepared, biases[0], sizes), other)
    return call_second(False, (w_all[:16, part:], w_all[16:, part:]), results, biases, sizes)


def local(inputs, w_up, b_up, w_conv, b_conv):
    chs = lax.axis_size("ch")
    sizes = (w_up.shape[2], w_conv.shape[1], 2 * inputs.shape[2] // chs, inputs.shape[3])
    plan = paired if chs == 2 and lax.axis_size("space") % 4 == 0 else gathered
    return plan(inputs, w_up, b_up, w_conv, b_conv, sizes)


def solution(mesh):
    return jax.shard_map(
        local,
        mesh=mesh,
        in_specs=(P("ch", None, "space", None), P(None, "ch", None), P(), P(), P()),
        out_specs=P(None, None, ("space", "ch"), None),
        check_vma=False,
    )
```

```python
import functools

import jax
import jax.numpy as jnp
from jax import lax
from jax.experimental import pallas as pl
from jax.experimental.pallas import tpu as pltpu
from jax.sharding import PartitionSpec as P

AXES = ("space", "ch")
PHASES = (((1, 0), (3, -1)), ((2, 0), (0, 1)))
COLUMNS = ((3, 0, 1), (0, 1, 2))
VMEM = pl.BlockSpec(memory_space=pltpu.VMEM)
ANY = pl.BlockSpec(memory_space=pl.ANY)
LIMIT = 40 * 2**20


def column_of(bias):
    lanes = bias.shape[-1]
    return jnp.transpose(jnp.broadcast_to(bias, (lanes, lanes)))


def shifted(value, step):
    cols = value.shape[1]
    place = lax.broadcasted_iota(jnp.int32, value.shape, 1)
    edge = 0 if step == 1 else cols - 1
    return jnp.where(place == edge, jnp.zeros_like(value), pltpu.roll(value, step % cols, 1))


def upsample(cell, tap_of, bias, u_ref, first, last):
    held, cols = u_ref.shape[1], u_ref.shape[3]
    for row_phase in (0, 1):
        for col_phase in (0, 1):
            taps = []
            for row_tap, row_shift in PHASES[row_phase]:
                for col_tap, col_shift in PHASES[col_phase]:
                    slot = row_shift + 1 - row_phase
                    taps.append((row_tap * 4 + col_tap, slot, col_shift % 3))
            kernel = jnp.concatenate([tap_of(tap) for tap, _, _ in taps], axis=1)
            for places in (range(held // 2),):
                cells = jnp.concatenate(
                    [
                        jnp.concatenate([cell(copy, slot + place) for place in places], axis=1)
                        for _, slot, copy in taps
                    ],
                    axis=0,
                )
                summed = jnp.dot(kernel, cells, preferred_element_type=jnp.float32)
                for number, place in enumerate(places):
                    row = 2 * place + 1 - row_phase
                    value = summed[:, number * cols : (number + 1) * cols] + bias
                    value = jnp.maximum(value, 0.2 * value)
                    if row == 0:
                        value = jnp.where(first, 0.0, value)
                    if row == held - 1:
                        value = jnp.where(last, 0.0, value)
                    value = value.astype(jnp.bfloat16)
                    u_ref[col_phase, row] = value
                    u_ref[2 + col_phase, row] = shifted(value, -1 if col_phase == 0 else 1)


def convolve(kernel, u_ref, start, col_phase):
    cells = jnp.concatenate(
        [
            jnp.concatenate([u_ref[copy, start + row_tap], u_ref[copy, start + row_tap + 1]], 1)
            for row_tap in range(3)
            for copy in COLUMNS[col_phase]
        ],
        axis=0,
    )
    return jnp.dot(kernel, cells, preferred_element_type=jnp.float32)


def split_kernels(w_conv_ref, halves_ref):
    cout = w_conv_ref.shape[1]
    part = cout // 2
    low = lax.broadcasted_iota(jnp.int32, (cout, cout), 1) < part
    for row_tap in range(3):
        for col_tap in range(3):
            taps = [w_conv_ref[a * 9 + row_tap * 3 + col_tap].astype(jnp.float32) for a in range(3)]
            turned = [pltpu.roll(tap, part, 1) for tap in taps]
            columns = pl.ds((row_tap * 3 + col_tap) * cout, cout)
            for plane in (0, 1):
                near, far = 1 - plane, 2 - plane
                rows = pl.ds(plane * cout, cout)
                halves_ref[0, rows, columns] = jnp.where(low, taps[near], turned[far]).astype(jnp.bfloat16)
                halves_ref[1, rows, columns] = jnp.where(low, turned[near], taps[far]).astype(jnp.bfloat16)


def bias_of(bias_ref, column_ref, blocks):
    column_ref[...] = column_of(bias_ref[...])
    return jnp.concatenate([column_ref[pl.ds(pl.multiple_of(at, 16), size)] for at, size in blocks], axis=0)


def ends(s, c):
    first = (s == 0) & (c == 0)
    last = (s == lax.axis_size("space") - 1) & (c == lax.axis_size("ch") - 1)
    return first, last


def store_row(x_ref, slot, offset, value):
    where = pl.ds(pl.multiple_of(offset, 16), value.shape[0])
    x_ref[0, slot, where] = value.astype(jnp.bfloat16)
    x_ref[1, slot, where] = shifted(value, -1).astype(jnp.bfloat16)
    x_ref[2, slot, where] = shifted(value, 1).astype(jnp.bfloat16)


def arrival(x, part):
    if x is None:
        return [[(0, part)], [(0, part)]]
    quarter, half = part // 4, part // 2
    return [
        [(x * half, half), ((1 - x) * half, half)],
        [(x * quarter, quarter), ((1 - x) * quarter, quarter), (half, half)],
    ]


def arrange(x, part):
    source = lax.broadcasted_iota(jnp.int32, (2 * part, 2 * part), 0)
    target = lax.broadcasted_iota(jnp.int32, (2 * part, 2 * part), 1)
    wanted = jnp.zeros_like(target)
    for plane, blocks in enumerate(arrival(x, part)):
        place = plane * part
        for first, size in blocks:
            inside = (target >= place) & (target < place + size)
            wanted = jnp.where(inside, target - place + plane * part + first, wanted)
            place += size
    return jnp.where(source == wanted, 1.0, 0.0).astype(jnp.bfloat16)


def own_part(half, refs, results, scratch):
    w_half_ref, kernel_ref, b_up_ref = refs
    x_ref, sum_ref = results
    column_ref, u_ref = scratch
    s, c = lax.axis_index("space"), lax.axis_index("ch")
    part, cols = w_half_ref.shape[1], u_ref.shape[3]

    def tap_of(tap):
        return jnp.concatenate([w_half_ref[tap], w_half_ref[16 + tap]], axis=0)

    bias = bias_of(b_up_ref, column_ref, [(half * part, part)] * 2)
    upsample(lambda copy, slot: x_ref[copy, slot], tap_of, bias, u_ref, *ends(s, c))
    kernel = kernel_ref[...]
    for start in range(0, u_ref.shape[1] - 2, 2):
        for col_phase in (0, 1):
            sum_ref[col_phase, :, start * cols : (start + 2) * cols] = convolve(kernel, u_ref, start, col_phase)


def prepare(paired, own_ref, w_half_ref, w_conv_ref, x_ref, w_ref, kernel_ref, other_ref, *scratch):
    halves_ref, v_ref, wide_ref, raw_ref, sems = scratch
    s, c = lax.axis_index("space"), lax.axis_index("ch")
    skipped = (w_half_ref.shape[0] - 32) // 2
    copies = [
        pltpu.make_async_copy(own_ref, raw_ref, sems.at[0]),
        pltpu.make_async_copy(w_conv_ref, v_ref, sems.at[1]),
        pltpu.make_async_copy(w_half_ref.at[pl.ds(skipped, 32)], w_ref, sems.at[2]),
    ]
    for copy in copies:
        copy.start()
    copies[0].wait()
    if paired:
        chans, rows, cols = own_ref.shape
        wide_ref[...] = raw_ref[...].astype(jnp.float32).reshape(chans * rows, cols)
        share = x_ref.shape[1] - 1
        for place in range(share):
            value = wide_ref[pl.ds(place + c * (rows - share), chans, stride=rows), :]
            store_row(x_ref, place + 1 - c, c * chans, value)
    else:
        for slot in range(own_ref.shape[0]):
            store_row(x_ref, slot, 0, raw_ref[slot].astype(jnp.float32))
    cout = w_conv_ref.shape[1]
    half, x = (c, lax.rem(s, 4) // 2) if paired else (0, None)
    copies[1].wait()
    split_kernels(v_ref, halves_ref)
    kernel_ref[...] = halves_ref[half]
    matrix = arrange(x, cout // 2)
    for number in range(9):
        columns = pl.ds(number * cout, cout)
        moved = jnp.dot(halves_ref[1 - half, :, columns], matrix, preferred_element_type=jnp.float32)
        other_ref[:, columns] = moved.astype(jnp.bfloat16)
    copies[2].wait()


def paired_first(peer_ref, near_ref, far_ref, started_ref, *refs):
    refs, results, scratch = refs[:3], refs[3:5], refs[5:]
    x_ref = results[0]
    c = lax.axis_index("ch")
    share, chans, _ = peer_ref.shape
    for place in range(share):
        store_row(x_ref, place + 1 - c, (1 - c) * chans, peer_ref[place].astype(jnp.float32))
    slot = c * (x_ref.shape[1] - 1)
    store_row(x_ref, slot, c * chans, near_ref[...].astype(jnp.float32))
    store_row(x_ref, slot, (1 - c) * chans, far_ref[...].astype(jnp.float32))
    own_part(c, refs, results, scratch)


def gathered_first(started_ref, *refs):
    own_part(0, refs[:3], refs[3:5], refs[5:])


def second(paired, count, *refs):
    parts, refs = refs[:count], refs[count:]
    x_ref, sum_ref, other_ref, b_up_ref, b_conv_ref, out_ref, column_ref, u_ref, total_ref, made_ref, sems = refs
    s, c = lax.axis_index("space"), lax.axis_index("ch")
    cout, _, rows, _ = out_ref.shape
    part = cout // 2
    half, x = (1 - c, lax.rem(s, 4) // 2) if paired else (1, None)
    cols = x_ref.shape[3]
    if paired:
        chans = x_ref.shape[2] // 2
        core = lax.rem(s, 2)
        sides = [pl.ds(pl.multiple_of(side * chans, 16), chans) for side in (core, 1 - core)]
        big = part // 2

        def tap_of(tap):
            columns = []
            for near_ref, far_ref, rest_ref in (parts[:3], parts[3:]):
                rows = [near_ref[tap, :big], far_ref[tap, :big], near_ref[tap, big:], far_ref[tap, big:], rest_ref[tap]]
                columns.append(jnp.concatenate(rows, axis=0))
            return jnp.concatenate(columns, axis=1)

        def cell(copy, slot):
            return jnp.concatenate([x_ref[copy, slot, side] for side in sides], axis=0)
    else:

        def tap_of(tap):
            return jnp.concatenate([part_ref[tap] for part_ref in parts], axis=0)

        def cell(copy, slot):
            return x_ref[copy, slot]

    blocks = [(half * part + at, size) for plane in arrival(x, part) for at, size in plane]
    bias = bias_of(b_up_ref, column_ref, blocks)
    upsample(cell, tap_of, bias, u_ref, *ends(s, c))
    source = lax.broadcasted_iota(jnp.int32, (2 * cols, 2 * cols), 0)
    target = lax.broadcasted_iota(jnp.int32, (2 * cols, 2 * cols), 1)
    wanted = jnp.where(source < cols, 2 * source, 2 * (source - cols) + 1)
    interleave = jnp.where(wanted == target, 1.0, 0.0).astype(jnp.bfloat16)
    kernel = other_ref[...]
    bias = column_of(b_conv_ref[...])
    bias = jnp.concatenate([bias, bias], axis=0)
    for start in range(0, rows, 2):
        halves = [
            convolve(kernel, u_ref, start, col_phase) + sum_ref[col_phase, :, start * cols : (start + 2) * cols]
            for col_phase in (0, 1)
        ]
        for number in (0, 1):
            pair = [
                (half[:, number * cols : (number + 1) * cols] + bias).astype(jnp.bfloat16) for half in halves
            ]
            mixed = jnp.dot(jnp.concatenate(pair, axis=1), interleave, preferred_element_type=jnp.float32)
            for side in (0, 1):
                total_ref[side, pl.ds(start + number, 2 * cout, stride=rows), :] = mixed[
                    :, side * cols : (side + 1) * cols
                ]
    copies = []
    for plane in (0, 1):
        for side in (0, 1):
            number = 2 * plane + side
            block = total_ref[side, pl.ds(plane * cout * rows, cout * rows), :]
            made_ref[number] = block.reshape(cout, rows, cols).astype(jnp.bfloat16)
            place = out_ref.at[:, plane, :, pl.ds(side * cols, cols)]
            copies.append(pltpu.make_async_copy(made_ref.at[number], place, sems.at[number]))
            copies[-1].start()
    for copy in copies:
        copy.wait()


def pieces(own_ref, w_up_ref, near_ref, far_ref, peer_ref, w_a_ref, w_b_ref, wide_ref, raw_ref, sems):
    s, c = lax.axis_index("space"), lax.axis_index("ch")
    raw = pltpu.make_async_copy(own_ref, raw_ref, sems.at[3])
    raw.start()
    me = lax.rem(s, 4)
    part, lanes = w_up_ref.shape[1], w_a_ref.shape[2]
    side = pl.ds(pl.multiple_of(lax.rem(me, 2) * lanes, lanes), lanes)
    (first, big), = arrival(me // 2, part)[0][:1]
    (second, small), _, (third, rest) = arrival(me // 2, part)[1]
    cuts = (
        (16, first, big, w_a_ref.at[:, pl.ds(0, big)]),
        (32, second, small, w_a_ref.at[:, pl.ds(big, small)]),
        (32, third, rest, w_b_ref),
    )
    copies = []
    for number, (tap, channel, count, place) in enumerate(cuts):
        source = w_up_ref.at[pl.ds(tap, 16), pl.ds(pl.multiple_of(channel, 16), count), side]
        copies.append(pltpu.make_async_copy(source, place, sems.at[number]))
        copies[-1].start()
    chans, rows, cols = own_ref.shape
    raw.wait()
    wide_ref[...] = raw_ref[...].astype(jnp.float32).reshape(chans * rows, cols)
    inner, outer = (1 - c) * (rows - 1), c * (rows - 1)
    near_ref[...] = wide_ref[pl.ds(inner, chans, stride=rows), :].astype(jnp.bfloat16)
    far_ref[...] = wide_ref[pl.ds(outer, chans, stride=rows), :].astype(jnp.bfloat16)
    share = peer_ref.shape[0]
    for place in range(share):
        row = wide_ref[pl.ds(place + (1 - c) * (rows - share), chans, stride=rows), :]
        peer_ref[place] = row.astype(jnp.bfloat16)
    for copy in copies:
        copy.wait()


def call_pieces(own, w_up):
    chans, rows, cols = own.shape
    part, cin = w_up.shape[1:]
    return pl.pallas_call(
        pieces,
        out_shape=(
            jax.ShapeDtypeStruct((chans, cols), jnp.bfloat16),
            jax.ShapeDtypeStruct((chans, cols), jnp.bfloat16),
            jax.ShapeDtypeStruct((rows // 2 + 1, chans, cols), jnp.bfloat16),
            jax.ShapeDtypeStruct((16, 3 * part // 4, cin // 2), jnp.bfloat16),
            jax.ShapeDtypeStruct((16, part // 2, cin // 2), jnp.bfloat16),
        ),
        in_specs=[ANY, ANY],
        out_specs=(VMEM,) * 5,
        scratch_shapes=[
            pltpu.VMEM((chans * rows, cols), jnp.float32),
            pltpu.VMEM((chans, rows, cols), jnp.bfloat16),
            pltpu.SemaphoreType.DMA((4,)),
        ],
        compiler_params=pltpu.CompilerParams(vmem_limit_bytes=LIMIT),
    )(in_hbm(own), in_hbm(w_up))


def in_hbm(operand):
    return pltpu.with_memory_space_constraint(operand, pltpu.HBM)


def cost(sizes):
    cin, cout, rows, cols = sizes
    flops = 2 * cout * 4 * cin * 2 * cols * (rows + 2) + 2 * 2 * cout * 9 * cout * 2 * cols * rows
    return pl.CostEstimate(flops=flops, bytes_accessed=8 * 2**20, transcendentals=0)


def call_prepare(paired, own, w_half, w_conv, sizes):
    cin, cout, rows, cols = sizes
    wide = own.shape[0] * own.shape[1] if paired else 8
    return pl.pallas_call(
        functools.partial(prepare, paired),
        out_shape=(
            jax.ShapeDtypeStruct((3, rows // 2 + 2, cin, cols), jnp.bfloat16),
            jax.ShapeDtypeStruct((32, cout // 2, cin), jnp.bfloat16),
            jax.ShapeDtypeStruct((2 * cout, 9 * cout), jnp.bfloat16),
            jax.ShapeDtypeStruct((2 * cout, 9 * cout), jnp.bfloat16),
        ),
        in_specs=[ANY] * 3,
        out_specs=(VMEM,) * 4,
        scratch_shapes=[
            pltpu.VMEM((2, 2 * cout, 9 * cout), jnp.bfloat16),
            pltpu.VMEM((27, cout, cout), jnp.bfloat16),
            pltpu.VMEM((wide, cols), jnp.float32),
            pltpu.VMEM(own.shape, jnp.bfloat16),
            pltpu.SemaphoreType.DMA((3,)),
        ],
        cost_estimate=pl.CostEstimate(flops=2 * 18 * 256 * cout * cout, bytes_accessed=8 * 2**20, transcendentals=0),
        compiler_params=pltpu.CompilerParams(vmem_limit_bytes=LIMIT),
    )(in_hbm(own), in_hbm(w_half), in_hbm(w_conv))


def call_first(body, rows_in, prepared, b_up, sizes):
    cin, cout, rows, cols = sizes
    started, w_half, kernel = prepared
    return pl.pallas_call(
        body,
        out_shape=(
            jax.ShapeDtypeStruct(started.shape, jnp.bfloat16),
            jax.ShapeDtypeStruct((2, 2 * cout, rows * cols), jnp.float32),
        ),
        in_specs=[VMEM] * (len(rows_in) + 4),
        out_specs=(VMEM,) * 2,
        scratch_shapes=[
            pltpu.VMEM((cout, cout), jnp.float32),
            pltpu.VMEM((4, rows + 2, cout, cols), jnp.bfloat16),
        ],
        input_output_aliases={len(rows_in): 0},
        cost_estimate=cost(sizes),
        compiler_params=pltpu.CompilerParams(vmem_limit_bytes=LIMIT),
    )(*rows_in, started, w_half, kernel, b_up)


def call_second(paired, parts, results, biases, sizes):
    cin, cout, rows, cols = sizes
    return pl.pallas_call(
        functools.partial(second, paired, len(parts)),
        out_shape=jax.ShapeDtypeStruct((cout, 2, rows, 2 * cols), jnp.bfloat16),
        in_specs=[VMEM] * (len(parts) + 5),
        out_specs=ANY,
        scratch_shapes=[
            pltpu.VMEM((cout, cout), jnp.float32),
            pltpu.VMEM((4, rows + 2, cout, cols), jnp.bfloat16),
            pltpu.VMEM((2, 2 * cout * rows, cols), jnp.float32),
            pltpu.VMEM((4, cout, rows, cols), jnp.bfloat16),
            pltpu.SemaphoreType.DMA((4,)),
        ],
        cost_estimate=cost(sizes),
        compiler_params=pltpu.CompilerParams(vmem_limit_bytes=LIMIT),
    )(*parts, *results, *biases)


def paired(inputs, w_up, b_up, w_conv, b_conv, sizes):
    spaces = lax.axis_size("space")
    s, c = lax.axis_index("space"), lax.axis_index("ch")
    chans, _, held, cols = inputs.shape

    def at(space, ch):
        return space * 2 + ch

    across = [(at(i, j), at(i, 1 - j)) for i in range(spaces) for j in (0, 1)]
    cores = [(at(i, j), at(i ^ 1, j)) for i in range(spaces) for j in (0, 1)]
    pairs = [(at(i, j), at(i ^ 2, j)) for i in range(spaces) for j in (0, 1)]
    chain = [(at(i - 1, 0), at(i, 0)) for i in range(1, spaces)]
    chain += [(at(i + 1, 1), at(i, 1)) for i in range(spaces - 1)]

    outer = [(t, t + 1) for t in range(1, 2 * spaces - 1, 2)]
    outer += [(j, i) for i, j in outer]

    own = inputs.reshape(chans, held, cols)
    near, far, peer, w_a, w_b = call_pieces(own, w_up)
    own, w_conv, peer, w_a, far, near, w_b = lax.optimization_barrier((own, w_conv, peer, w_a, far, near, w_b))
    peer = lax.ppermute(peer, AXES, across)
    w_a = lax.ppermute(w_a, AXES, across)
    far = lax.ppermute(far, AXES, outer)
    near = lax.ppermute(near, AXES, chain)
    w_a, w_b, own, w_conv = lax.optimization_barrier((w_a, w_b, own, w_conv))
    w_ax = lax.ppermute(w_a, AXES, pairs)
    w_b = lax.ppermute(w_b, AXES, across)
    w_ac = lax.ppermute(w_a, AXES, cores)
    x, w_half, kernel, other = call_prepare(True, own, w_up, w_conv, sizes)
    biases = (b_up[None], b_conv[None])
    x, total = call_first(paired_first, (peer, near, far), (x, w_half, kernel), biases[0], sizes)
    results = (x, total, other)
    w_ax, w_ac, *results = lax.optimization_barrier((w_ax, w_ac, *results))
    w_axc = lax.ppermute(w_ax, AXES, cores)
    w_b, *results = lax.optimization_barrier((w_b, *results))
    w_bc = lax.ppermute(w_b, AXES, cores)
    return call_second(True, (w_a, w_ax, w_b, w_ac, w_axc, w_bc), results, biases, sizes)


def gathered(inputs, w_up, b_up, w_conv, b_conv, sizes):
    spaces, chs = lax.axis_size("space"), lax.axis_size("ch")
    c = lax.axis_index("ch")
    w_all = lax.all_gather(w_up[16:48], "ch", axis=1, tiled=True)
    part = w_all.shape[1] // 2
    rows = lax.all_gather(inputs[:, 0], "ch", axis=0, tiled=True).transpose(1, 0, 2)
    forward = [(i, i + 1) for i in range(spaces - 1)]
    backward = [(j, i) for i, j in forward]
    low = lax.ppermute(rows[-1:], "space", forward)
    high = lax.ppermute(rows[:1], "space", backward)
    rows = jnp.concatenate([low, rows, high], axis=0)
    share = inputs.shape[2] // chs
    rows = lax.dynamic_slice_in_dim(rows, c * share, share + 2, 0)
    biases = (b_up[None], b_conv[None])
    *prepared, other = call_prepare(False, rows, w_all[:, :part], w_conv, sizes)
    results = (*call_first(gathered_first, (), prepared, biases[0], sizes), other)
    return call_second(False, (w_all[:16, part:], w_all[16:, part:]), results, biases, sizes)


def local(inputs, w_up, b_up, w_conv, b_conv):
    chs = lax.axis_size("ch")
    sizes = (w_up.shape[2], w_conv.shape[1], 2 * inputs.shape[2] // chs, inputs.shape[3])
    plan = paired if chs == 2 and lax.axis_size("space") % 4 == 0 else gathered
    return plan(inputs, w_up, b_up, w_conv, b_conv, sizes)


def solution(mesh):
    return jax.shard_map(
        local,
        mesh=mesh,
        in_specs=(P("ch", None, "space", None), P(None, "ch", None), P(), P(), P()),
        out_specs=P(None, None, ("space", "ch"), None),
        check_vma=False,
    )
```

```python
import functools

import jax
import jax.numpy as jnp
from jax import lax
from jax.experimental import pallas as pl
from jax.experimental.pallas import tpu as pltpu
from jax.sharding import PartitionSpec as P

AXES = ("space", "ch")
PHASES = (((1, 0), (3, -1)), ((2, 0), (0, 1)))
COLUMNS = ((3, 0, 1), (0, 1, 2))
VMEM = pl.BlockSpec(memory_space=pltpu.VMEM)
ANY = pl.BlockSpec(memory_space=pl.ANY)
LIMIT = 40 * 2**20


def column_of(bias):
    lanes = bias.shape[-1]
    return jnp.transpose(jnp.broadcast_to(bias, (lanes, lanes)))


def shifted(value, step):
    cols = value.shape[1]
    place = lax.broadcasted_iota(jnp.int32, value.shape, 1)
    edge = 0 if step == 1 else cols - 1
    return jnp.where(place == edge, jnp.zeros_like(value), pltpu.roll(value, step % cols, 1))


def upsample(cell, tap_of, bias, u_ref, first, last):
    held, cols = u_ref.shape[1], u_ref.shape[3]
    for row_phase in (0, 1):
        for col_phase in (0, 1):
            taps = []
            for row_tap, row_shift in PHASES[row_phase]:
                for col_tap, col_shift in PHASES[col_phase]:
                    slot = row_shift + 1 - row_phase
                    taps.append((row_tap * 4 + col_tap, slot, col_shift % 3))
            kernel = jnp.concatenate([tap_of(tap) for tap, _, _ in taps], axis=1)
            for places in (range(held // 2),):
                cells = jnp.concatenate(
                    [
                        jnp.concatenate([cell(copy, slot + place) for place in places], axis=1)
                        for _, slot, copy in taps
                    ],
                    axis=0,
                )
                summed = jnp.dot(kernel, cells, preferred_element_type=jnp.float32)
                for number, place in enumerate(places):
                    row = 2 * place + 1 - row_phase
                    value = summed[:, number * cols : (number + 1) * cols] + bias
                    value = jnp.maximum(value, 0.2 * value)
                    if row == 0:
                        value = jnp.where(first, 0.0, value)
                    if row == held - 1:
                        value = jnp.where(last, 0.0, value)
                    value = value.astype(jnp.bfloat16)
                    u_ref[col_phase, row] = value
                    u_ref[2 + col_phase, row] = shifted(value, -1 if col_phase == 0 else 1)


def convolve(kernel, u_ref, start, col_phase):
    cells = jnp.concatenate(
        [
            jnp.concatenate([u_ref[copy, start + row_tap], u_ref[copy, start + row_tap + 1]], 1)
            for row_tap in range(3)
            for copy in COLUMNS[col_phase]
        ],
        axis=0,
    )
    return jnp.dot(kernel, cells, preferred_element_type=jnp.float32)


def split_kernels(w_conv_ref, halves_ref):
    cout = w_conv_ref.shape[1]
    part = cout // 2
    low = lax.broadcasted_iota(jnp.int32, (cout, cout), 1) < part
    for row_tap in range(3):
        for col_tap in range(3):
            taps = [w_conv_ref[a * 9 + row_tap * 3 + col_tap].astype(jnp.float32) for a in range(3)]
            turned = [pltpu.roll(tap, part, 1) for tap in taps]
            columns = pl.ds((row_tap * 3 + col_tap) * cout, cout)
            for plane in (0, 1):
                near, far = 1 - plane, 2 - plane
                rows = pl.ds(plane * cout, cout)
                halves_ref[0, rows, columns] = jnp.where(low, taps[near], turned[far]).astype(jnp.bfloat16)
                halves_ref[1, rows, columns] = jnp.where(low, turned[near], taps[far]).astype(jnp.bfloat16)


def bias_of(bias_ref, column_ref, blocks):
    column_ref[...] = column_of(bias_ref[...])
    return jnp.concatenate([column_ref[pl.ds(pl.multiple_of(at, 16), size)] for at, size in blocks], axis=0)


def ends(s, c):
    first = (s == 0) & (c == 0)
    last = (s == lax.axis_size("space") - 1) & (c == lax.axis_size("ch") - 1)
    return first, last


def store_row(x_ref, slot, offset, value):
    where = pl.ds(pl.multiple_of(offset, 16), value.shape[0])
    x_ref[0, slot, where] = value.astype(jnp.bfloat16)
    x_ref[1, slot, where] = shifted(value, -1).astype(jnp.bfloat16)
    x_ref[2, slot, where] = shifted(value, 1).astype(jnp.bfloat16)


def arrival(x, part):
    if x is None:
        return [[(0, part)], [(0, part)]]
    quarter, half = part // 4, part // 2
    return [
        [(x * half, half), ((1 - x) * half, half)],
        [(x * quarter, quarter), ((1 - x) * quarter, quarter), (half, half)],
    ]


def arrange(x, part):
    source = lax.broadcasted_iota(jnp.int32, (2 * part, 2 * part), 0)
    target = lax.broadcasted_iota(jnp.int32, (2 * part, 2 * part), 1)
    wanted = jnp.zeros_like(target)
    for plane, blocks in enumerate(arrival(x, part)):
        place = plane * part
        for first, size in blocks:
            inside = (target >= place) & (target < place + size)
            wanted = jnp.where(inside, target - place + plane * part + first, wanted)
            place += size
    return jnp.where(source == wanted, 1.0, 0.0).astype(jnp.bfloat16)


def own_part(half, refs, results, scratch):
    w_half_ref, kernel_ref, b_up_ref = refs
    x_ref, sum_ref = results
    column_ref, u_ref = scratch
    s, c = lax.axis_index("space"), lax.axis_index("ch")
    part, cols = w_half_ref.shape[1], u_ref.shape[3]

    def tap_of(tap):
        return jnp.concatenate([w_half_ref[tap], w_half_ref[16 + tap]], axis=0)

    bias = bias_of(b_up_ref, column_ref, [(half * part, part)] * 2)
    upsample(lambda copy, slot: x_ref[copy, slot], tap_of, bias, u_ref, *ends(s, c))
    kernel = kernel_ref[...]
    for start in range(0, u_ref.shape[1] - 2, 2):
        for col_phase in (0, 1):
            sum_ref[col_phase, :, start * cols : (start + 2) * cols] = convolve(kernel, u_ref, start, col_phase)


def prepare(paired, own_ref, w_half_ref, w_conv_ref, x_ref, w_ref, kernel_ref, other_ref, *scratch):
    halves_ref, v_ref, wide_ref, raw_ref, sems = scratch
    s, c = lax.axis_index("space"), lax.axis_index("ch")
    skipped = (w_half_ref.shape[0] - 32) // 2
    copies = [
        pltpu.make_async_copy(own_ref, raw_ref, sems.at[0]),
        pltpu.make_async_copy(w_conv_ref, v_ref, sems.at[1]),
        pltpu.make_async_copy(w_half_ref.at[pl.ds(skipped, 32)], w_ref, sems.at[2]),
    ]
    for copy in copies:
        copy.start()
    copies[0].wait()
    if paired:
        chans, rows, cols = own_ref.shape
        wide_ref[...] = raw_ref[...].astype(jnp.float32).reshape(chans * rows, cols)
        share = x_ref.shape[1] - 1
        for place in range(share):
            value = wide_ref[pl.ds(place + c * (rows - share), chans, stride=rows), :]
            store_row(x_ref, place + 1 - c, c * chans, value)
    else:
        for slot in range(own_ref.shape[0]):
            store_row(x_ref, slot, 0, raw_ref[slot].astype(jnp.float32))
    cout = w_conv_ref.shape[1]
    half, x = (c, lax.rem(s, 4) // 2) if paired else (0, None)
    copies[1].wait()
    split_kernels(v_ref, halves_ref)
    kernel_ref[...] = halves_ref[half]
    matrix = arrange(x, cout // 2)
    for number in range(9):
        columns = pl.ds(number * cout, cout)
        moved = jnp.dot(halves_ref[1 - half, :, columns], matrix, preferred_element_type=jnp.float32)
        other_ref[:, columns] = moved.astype(jnp.bfloat16)
    copies[2].wait()


def paired_first(peer_ref, near_ref, far_ref, started_ref, *refs):
    refs, results, scratch = refs[:3], refs[3:5], refs[5:]
    x_ref = results[0]
    c = lax.axis_index("ch")
    share, chans, _ = peer_ref.shape
    for place in range(share):
        store_row(x_ref, place + 1 - c, (1 - c) * chans, peer_ref[place].astype(jnp.float32))
    slot = c * (x_ref.shape[1] - 1)
    store_row(x_ref, slot, c * chans, near_ref[...].astype(jnp.float32))
    store_row(x_ref, slot, (1 - c) * chans, far_ref[...].astype(jnp.float32))
    own_part(c, refs, results, scratch)


def gathered_first(started_ref, *refs):
    own_part(0, refs[:3], refs[3:5], refs[5:])


def second(paired, count, *refs):
    parts, refs = refs[:count], refs[count:]
    x_ref, sum_ref, other_ref, b_up_ref, b_conv_ref, out_ref, column_ref, u_ref, total_ref, made_ref, sems = refs
    s, c = lax.axis_index("space"), lax.axis_index("ch")
    cout, _, rows, _ = out_ref.shape
    part = cout // 2
    half, x = (1 - c, lax.rem(s, 4) // 2) if paired else (1, None)
    cols = x_ref.shape[3]
    if paired:
        chans = x_ref.shape[2] // 2
        core = lax.rem(s, 2)
        sides = [pl.ds(pl.multiple_of(side * chans, 16), chans) for side in (core, 1 - core)]
        big = part // 2

        def tap_of(tap):
            columns = []
            for near_ref, far_ref, rest_ref in (parts[:3], parts[3:]):
                rows = [near_ref[tap, :big], far_ref[tap, :big], near_ref[tap, big:], far_ref[tap, big:], rest_ref[tap]]
                columns.append(jnp.concatenate(rows, axis=0))
            return jnp.concatenate(columns, axis=1)

        def cell(copy, slot):
            return jnp.concatenate([x_ref[copy, slot, side] for side in sides], axis=0)
    else:

        def tap_of(tap):
            return jnp.concatenate([part_ref[tap] for part_ref in parts], axis=0)

        def cell(copy, slot):
            return x_ref[copy, slot]

    blocks = [(half * part + at, size) for plane in arrival(x, part) for at, size in plane]
    bias = bias_of(b_up_ref, column_ref, blocks)
    upsample(cell, tap_of, bias, u_ref, *ends(s, c))
    source = lax.broadcasted_iota(jnp.int32, (2 * cols, 2 * cols), 0)
    target = lax.broadcasted_iota(jnp.int32, (2 * cols, 2 * cols), 1)
    wanted = jnp.where(source < cols, 2 * source, 2 * (source - cols) + 1)
    interleave = jnp.where(wanted == target, 1.0, 0.0).astype(jnp.bfloat16)
    kernel = other_ref[...]
    bias = column_of(b_conv_ref[...])
    bias = jnp.concatenate([bias, bias], axis=0)
    for start in range(0, rows, 2):
        halves = [
            convolve(kernel, u_ref, start, col_phase) + sum_ref[col_phase, :, start * cols : (start + 2) * cols]
            for col_phase in (0, 1)
        ]
        pairs = []
        for number in (0, 1):
            pair = [
                (half[:, number * cols : (number + 1) * cols] + bias).astype(jnp.bfloat16) for half in halves
            ]
            pairs.append(jnp.concatenate(pair, axis=1))
        both = jnp.dot(jnp.concatenate(pairs, axis=0), interleave, preferred_element_type=jnp.float32)
        for number in (0, 1):
            mixed = both[number * 2 * cout : (number + 1) * 2 * cout]
            for side in (0, 1):
                total_ref[side, pl.ds(start + number, 2 * cout, stride=rows), :] = mixed[
                    :, side * cols : (side + 1) * cols
                ]
    copies = []
    for plane in (0, 1):
        for side in (0, 1):
            number = 2 * plane + side
            block = total_ref[side, pl.ds(plane * cout * rows, cout * rows), :]
            made_ref[number] = block.reshape(cout, rows, cols).astype(jnp.bfloat16)
            place = out_ref.at[:, plane, :, pl.ds(side * cols, cols)]
            copies.append(pltpu.make_async_copy(made_ref.at[number], place, sems.at[number]))
            copies[-1].start()
    for copy in copies:
        copy.wait()


def pieces(own_ref, w_up_ref, near_ref, far_ref, peer_ref, w_a_ref, w_b_ref, wide_ref, raw_ref, sems):
    s, c = lax.axis_index("space"), lax.axis_index("ch")
    raw = pltpu.make_async_copy(own_ref, raw_ref, sems.at[3])
    raw.start()
    me = lax.rem(s, 4)
    part, lanes = w_up_ref.shape[1], w_a_ref.shape[2]
    side = pl.ds(pl.multiple_of(lax.rem(me, 2) * lanes, lanes), lanes)
    (first, big), = arrival(me // 2, part)[0][:1]
    (second, small), _, (third, rest) = arrival(me // 2, part)[1]
    cuts = (
        (16, first, big, w_a_ref.at[:, pl.ds(0, big)]),
        (32, second, small, w_a_ref.at[:, pl.ds(big, small)]),
        (32, third, rest, w_b_ref),
    )
    copies = []
    for number, (tap, channel, count, place) in enumerate(cuts):
        source = w_up_ref.at[pl.ds(tap, 16), pl.ds(pl.multiple_of(channel, 16), count), side]
        copies.append(pltpu.make_async_copy(source, place, sems.at[number]))
        copies[-1].start()
    chans, rows, cols = own_ref.shape
    raw.wait()
    wide_ref[...] = raw_ref[...].astype(jnp.float32).reshape(chans * rows, cols)
    inner, outer = (1 - c) * (rows - 1), c * (rows - 1)
    near_ref[...] = wide_ref[pl.ds(inner, chans, stride=rows), :].astype(jnp.bfloat16)
    far_ref[...] = wide_ref[pl.ds(outer, chans, stride=rows), :].astype(jnp.bfloat16)
    share = peer_ref.shape[0]
    for place in range(share):
        row = wide_ref[pl.ds(place + (1 - c) * (rows - share), chans, stride=rows), :]
        peer_ref[place] = row.astype(jnp.bfloat16)
    for copy in copies:
        copy.wait()


def call_pieces(own, w_up):
    chans, rows, cols = own.shape
    part, cin = w_up.shape[1:]
    return pl.pallas_call(
        pieces,
        out_shape=(
            jax.ShapeDtypeStruct((chans, cols), jnp.bfloat16),
            jax.ShapeDtypeStruct((chans, cols), jnp.bfloat16),
            jax.ShapeDtypeStruct((rows // 2 + 1, chans, cols), jnp.bfloat16),
            jax.ShapeDtypeStruct((16, 3 * part // 4, cin // 2), jnp.bfloat16),
            jax.ShapeDtypeStruct((16, part // 2, cin // 2), jnp.bfloat16),
        ),
        in_specs=[ANY, ANY],
        out_specs=(VMEM,) * 5,
        scratch_shapes=[
            pltpu.VMEM((chans * rows, cols), jnp.float32),
            pltpu.VMEM((chans, rows, cols), jnp.bfloat16),
            pltpu.SemaphoreType.DMA((4,)),
        ],
        compiler_params=pltpu.CompilerParams(vmem_limit_bytes=LIMIT),
    )(in_hbm(own), in_hbm(w_up))


def in_hbm(operand):
    return pltpu.with_memory_space_constraint(operand, pltpu.HBM)


def cost(sizes):
    cin, cout, rows, cols = sizes
    flops = 2 * cout * 4 * cin * 2 * cols * (rows + 2) + 2 * 2 * cout * 9 * cout * 2 * cols * rows
    return pl.CostEstimate(flops=flops, bytes_accessed=8 * 2**20, transcendentals=0)


def call_prepare(paired, own, w_half, w_conv, sizes):
    cin, cout, rows, cols = sizes
    wide = own.shape[0] * own.shape[1] if paired else 8
    return pl.pallas_call(
        functools.partial(prepare, paired),
        out_shape=(
            jax.ShapeDtypeStruct((3, rows // 2 + 2, cin, cols), jnp.bfloat16),
            jax.ShapeDtypeStruct((32, cout // 2, cin), jnp.bfloat16),
            jax.ShapeDtypeStruct((2 * cout, 9 * cout), jnp.bfloat16),
            jax.ShapeDtypeStruct((2 * cout, 9 * cout), jnp.bfloat16),
        ),
        in_specs=[ANY] * 3,
        out_specs=(VMEM,) * 4,
        scratch_shapes=[
            pltpu.VMEM((2, 2 * cout, 9 * cout), jnp.bfloat16),
            pltpu.VMEM((27, cout, cout), jnp.bfloat16),
            pltpu.VMEM((wide, cols), jnp.float32),
            pltpu.VMEM(own.shape, jnp.bfloat16),
            pltpu.SemaphoreType.DMA((3,)),
        ],
        cost_estimate=pl.CostEstimate(flops=2 * 18 * 256 * cout * cout, bytes_accessed=8 * 2**20, transcendentals=0),
        compiler_params=pltpu.CompilerParams(vmem_limit_bytes=LIMIT),
    )(in_hbm(own), in_hbm(w_half), in_hbm(w_conv))


def call_first(body, rows_in, prepared, b_up, sizes):
    cin, cout, rows, cols = sizes
    started, w_half, kernel = prepared
    return pl.pallas_call(
        body,
        out_shape=(
            jax.ShapeDtypeStruct(started.shape, jnp.bfloat16),
            jax.ShapeDtypeStruct((2, 2 * cout, rows * cols), jnp.float32),
        ),
        in_specs=[VMEM] * (len(rows_in) + 4),
        out_specs=(VMEM,) * 2,
        scratch_shapes=[
            pltpu.VMEM((cout, cout), jnp.float32),
            pltpu.VMEM((4, rows + 2, cout, cols), jnp.bfloat16),
        ],
        input_output_aliases={len(rows_in): 0},
        cost_estimate=cost(sizes),
        compiler_params=pltpu.CompilerParams(vmem_limit_bytes=LIMIT),
    )(*rows_in, started, w_half, kernel, b_up)


def call_second(paired, parts, results, biases, sizes):
    cin, cout, rows, cols = sizes
    return pl.pallas_call(
        functools.partial(second, paired, len(parts)),
        out_shape=jax.ShapeDtypeStruct((cout, 2, rows, 2 * cols), jnp.bfloat16),
        in_specs=[VMEM] * (len(parts) + 5),
        out_specs=ANY,
        scratch_shapes=[
            pltpu.VMEM((cout, cout), jnp.float32),
            pltpu.VMEM((4, rows + 2, cout, cols), jnp.bfloat16),
            pltpu.VMEM((2, 2 * cout * rows, cols), jnp.float32),
            pltpu.VMEM((4, cout, rows, cols), jnp.bfloat16),
            pltpu.SemaphoreType.DMA((4,)),
        ],
        cost_estimate=cost(sizes),
        compiler_params=pltpu.CompilerParams(vmem_limit_bytes=LIMIT),
    )(*parts, *results, *biases)


def paired(inputs, w_up, b_up, w_conv, b_conv, sizes):
    spaces = lax.axis_size("space")
    s, c = lax.axis_index("space"), lax.axis_index("ch")
    chans, _, held, cols = inputs.shape

    def at(space, ch):
        return space * 2 + ch

    across = [(at(i, j), at(i, 1 - j)) for i in range(spaces) for j in (0, 1)]
    cores = [(at(i, j), at(i ^ 1, j)) for i in range(spaces) for j in (0, 1)]
    pairs = [(at(i, j), at(i ^ 2, j)) for i in range(spaces) for j in (0, 1)]
    chain = [(at(i - 1, 0), at(i, 0)) for i in range(1, spaces)]
    chain += [(at(i + 1, 1), at(i, 1)) for i in range(spaces - 1)]

    outer = [(t, t + 1) for t in range(1, 2 * spaces - 1, 2)]
    outer += [(j, i) for i, j in outer]

    own = inputs.reshape(chans, held, cols)
    near, far, peer, w_a, w_b = call_pieces(own, w_up)
    own, w_conv, peer, w_a, far, near, w_b = lax.optimization_barrier((own, w_conv, peer, w_a, far, near, w_b))
    peer = lax.ppermute(peer, AXES, across)
    w_a = lax.ppermute(w_a, AXES, across)
    far = lax.ppermute(far, AXES, outer)
    near = lax.ppermute(near, AXES, chain)
    w_a, w_b, own, w_conv = lax.optimization_barrier((w_a, w_b, own, w_conv))
    w_ax = lax.ppermute(w_a, AXES, pairs)
    w_b = lax.ppermute(w_b, AXES, across)
    w_ac = lax.ppermute(w_a, AXES, cores)
    x, w_half, kernel, other = call_prepare(True, own, w_up, w_conv, sizes)
    biases = (b_up[None], b_conv[None])
    x, total = call_first(paired_first, (peer, near, far), (x, w_half, kernel), biases[0], sizes)
    results = (x, total, other)
    w_ax, w_ac, *results = lax.optimization_barrier((w_ax, w_ac, *results))
    w_axc = lax.ppermute(w_ax, AXES, cores)
    w_b, *results = lax.optimization_barrier((w_b, *results))
    w_bc = lax.ppermute(w_b, AXES, cores)
    return call_second(True, (w_a, w_ax, w_b, w_ac, w_axc, w_bc), results, biases, sizes)


def gathered(inputs, w_up, b_up, w_conv, b_conv, sizes):
    spaces, chs = lax.axis_size("space"), lax.axis_size("ch")
    c = lax.axis_index("ch")
    w_all = lax.all_gather(w_up[16:48], "ch", axis=1, tiled=True)
    part = w_all.shape[1] // 2
    rows = lax.all_gather(inputs[:, 0], "ch", axis=0, tiled=True).transpose(1, 0, 2)
    forward = [(i, i + 1) for i in range(spaces - 1)]
    backward = [(j, i) for i, j in forward]
    low = lax.ppermute(rows[-1:], "space", forward)
    high = lax.ppermute(rows[:1], "space", backward)
    rows = jnp.concatenate([low, rows, high], axis=0)
    share = inputs.shape[2] // chs
    rows = lax.dynamic_slice_in_dim(rows, c * share, share + 2, 0)
    biases = (b_up[None], b_conv[None])
    *prepared, other = call_prepare(False, rows, w_all[:, :part], w_conv, sizes)
    results = (*call_first(gathered_first, (), prepared, biases[0], sizes), other)
    return call_second(False, (w_all[:16, part:], w_all[16:, part:]), results, biases, sizes)


def local(inputs, w_up, b_up, w_conv, b_conv):
    chs = lax.axis_size("ch")
    sizes = (w_up.shape[2], w_conv.shape[1], 2 * inputs.shape[2] // chs, inputs.shape[3])
    plan = paired if chs == 2 and lax.axis_size("space") % 4 == 0 else gathered
    return plan(inputs, w_up, b_up, w_conv, b_conv, sizes)


def solution(mesh):
    return jax.shard_map(
        local,
        mesh=mesh,
        in_specs=(P("ch", None, "space", None), P(None, "ch", None), P(), P(), P()),
        out_specs=P(None, None, ("space", "ch"), None),
        check_vma=False,
    )
```
